32 devices in a mesh: cells: 4 (over x, core), tok: 8 (over z, y).
Axes of the slice: x: 2, y: 2, z: 4, core: 2. Of those that a mesh axis runs over, the one named last changes fastest.
Arguments:
- tokens: bfloat16 [32, 200, 4096], P('cells', None, 'tok'), may hold values from -6 to 6
- cotangent: bfloat16 [32, 200, 4096], P('cells', None, 'tok'), may hold values from -6 to 6
- gene_count: int32 [32], P('cells'), may hold values from 2048 to 4096, as said below
- expressed: int32 [32, 4096], P('cells', 'tok'), may hold values 0 or 1
- projection: bfloat16 [266, 64], replicated, may hold values from -6 to 6
- first_gain: float32 [200], replicated, may hold values from 0.5 to 1.5
- first_bias: float32 [200], replicated, may hold values from -1.2 to 1.2
- query_weight: bfloat16 [200, 640], replicated, may hold values from -0.4375 to 0.4375
- key_weight: bfloat16 [200, 640], replicated, may hold values from -0.4375 to 0.4375
- value_weight: bfloat16 [200, 640], replicated, may hold values from -0.4375 to 0.4375
- out_weight: bfloat16 [640, 200], replicated, may hold values from -13.1875 to 13.1875
- out_bias: float32 [200], replicated, may hold values from -1.8 to 1.8
- second_gain: float32 [200], replicated, may hold values from 0.5 to 1.5
- second_bias: float32 [200], replicated, may hold values from -1.2 to 1.2
- up_weight: bfloat16 [200, 800], replicated, may hold values from -0.4375 to 0.4375
- up_bias: float32 [800], replicated, may hold values from -1.8 to 1.8
- down_weight: bfloat16 [200, 800], replicated, may hold values from -0.21875 to 0.21875
- down_bias: float32 [200], replicated, may hold values from -1.8 to 1.8
Outputs:
- output: bfloat16 [32, 200, 4096], P('cells', None, 'tok')
- input_grad: bfloat16 [32, 200, 4096], P('cells', None, 'tok')
- first_gain_grad: float32 [200], replicated
- first_bias_grad: float32 [200], replicated
- query_weight_grad: float32 [200, 640], replicated
- key_weight_grad: float32 [200, 640], replicated
- value_weight_grad: float32 [200, 640], replicated
- out_weight_grad: float32 [640, 200], replicated
- out_bias_grad: float32 [200], replicated
- second_gain_grad: float32 [200], replicated
- second_bias_grad: float32 [200], replicated
- up_weight_grad: float32 [200, 800], replicated
- up_bias_grad: float32 [800], replicated
- down_weight_grad: float32 [200, 800], replicated
- down_bias_grad: float32 [200], replicated
The draws below stay inside these ranges and needn't reach their ends.
Inputs may be any that keep to these rules, and one draw needn't show every extreme that they name: `gene_count`: one cell of every aligned block of 8 cells has all 4096 slots valid.
All inputs are finite; a program needn't handle non-finite values. No bound on the sum of `expressed` on one device may be relied on, other than what follows from the above.
Results may differ from the reference program's by a relative error of at most 0.033.
Values may be sent and summed in bfloat16 or wider, within the bound.
No kernel may reach another device: no remote copies, remote signals or barrier semaphores. Data moves between devices by JAX's collectives and lax.ppermute only.
A program may use at most 192 MiB of HBM per device.

```python
import jax
import jax.numpy as jnp
from jax import lax

HEADS = 10
HEAD_SIZE = 64
D = 200
INNER = 640
FEATURES = 266
FF = 800
CELL_DEV = 8
SLOTS = 4096
CELLS = 32


def draw_gene_count(key, part):
    key = jax.random.fold_in(key, 11)
    first_key, second_key = jax.random.split(key)
    counts = jax.random.randint(first_key, (CELLS,), SLOTS // 2, SLOTS + 1)
    chosen = jax.random.randint(second_key, (CELLS // CELL_DEV,), 0, CELL_DEV)
    cell_number = jnp.arange(CELLS, dtype=jnp.int32)
    full_cell = cell_number % CELL_DEV == chosen[cell_number // CELL_DEV]
    return jnp.where(full_cell, SLOTS, counts).astype(jnp.int32)


def set_ends(values, rng, least, largest):
    shape = values.shape
    index_at = [jax.random.randint(jax.random.fold_in(rng, axis), (), 0, shape[axis]) for axis in range(len(shape))]
    values = values.at[tuple(index_at)].set(least)
    longest = shape.index(max(shape))
    index_at[longest] = (index_at[longest] + 1) % shape[longest]
    return values.at[tuple(index_at)].set(largest)


def block_levels(own_key, extent, shards, low, high):
    def one(axis_at, shards_of):
        steps = jax.random.uniform(jax.random.fold_in(jax.random.fold_in(own_key, 6), axis_at), (shards_of,), jnp.float32, low / len(shards), high / len(shards))
        return jnp.repeat(jnp.exp(steps), extent[axis_at] // shards_of).reshape((-1,) + (1,) * (len(extent) - axis_at - 1))

    factor_of = one(*shards[0])
    for cut in shards[1:]:
        factor_of = factor_of * one(*cut)
    return factor_of


def bell_draw(stream_key, dims, width, reach, cuts=(), kind=jnp.bfloat16):
    values = jax.random.normal(stream_key, dims, jnp.float32) * width
    if len(cuts) > 0:
        values = block_levels(stream_key, dims, cuts, -0.22, 0.18) * values
    return jnp.clip(values, min=-reach, max=reach).astype(kind)


def setup_inputs(seed: int = 0) -> dict:
    key_of = jax.random.split(jax.random.key(seed), 19)
    return {
        "tokens": bell_draw(key_of[0], (CELLS, D, SLOTS), 1.0, 6.0, ((0, 4), (2, 8))),
        "cotangent": bell_draw(key_of[1], (CELLS, D, SLOTS), 1.0, 6.0, ((0, 4), (2, 8))),
        "gene_count": draw_gene_count(jax.random.fold_in(key_of[18], 71), 0),
        "expressed": set_ends((jax.random.randint(key_of[3], (CELLS, SLOTS), 0, 4) < 3).astype(jnp.int32), jax.random.fold_in(key_of[3], 1), 0, 1),
        "projection": bell_draw(key_of[4], (FEATURES, HEAD_SIZE), 1.0, 6.0),
        "first_gain": jnp.clip(1.0 + 0.1 * jax.random.normal(key_of[5], (D,), jnp.float32), 0.5, 1.5),
        "first_bias": bell_draw(key_of[6], (D,), 0.2, 1.2, (), jnp.float32),
        "query_weight": bell_draw(key_of[7], (D, INNER), D ** -0.5, 0.4375),
        "key_weight": bell_draw(key_of[8], (D, INNER), D ** -0.5, 0.4375),
        "value_weight": bell_draw(key_of[9], (D, INNER), D ** -0.5, 0.4375),
        "out_weight": bell_draw(key_of[10], (INNER, D), 2.2, 13.1875),
        "out_bias": bell_draw(key_of[11], (D,), 0.3, 1.8, (), jnp.float32),
        "second_gain": jnp.clip(1.0 + 0.1 * jax.random.normal(key_of[12], (D,), jnp.float32), 0.5, 1.5),
        "second_bias": bell_draw(key_of[13], (D,), 0.2, 1.2, (), jnp.float32),
        "up_weight": bell_draw(key_of[14], (D, FF), D ** -0.5, 0.4375),
        "up_bias": bell_draw(key_of[15], (FF,), 0.3, 1.8, (), jnp.float32),
        "down_weight": bell_draw(key_of[16], (D, FF), FF ** -0.5, 0.21875),
        "down_bias": bell_draw(key_of[17], (D,), 0.3, 1.8, (), jnp.float32),
    }


EPSILON = 1e-05
HIGHEST = lax.Precision.HIGHEST

@jax.custom_vjp
def low(v):
    return lax.optimization_barrier(v.astype(jnp.bfloat16)).astype(jnp.float32)

@jax.custom_vjp
def low_back(v):
    return v

def low_keep(v):
    return (low(v), None)

def low_pass(kept, grad):
    return (grad,)

def back_keep(v):
    return (v, None)

def back_low(kept, grad):
    return (low(grad),)
low.defvjp(low_keep, low_pass)
low_back.defvjp(back_keep, back_low)

def layer_norm(values, gain, bias):
    average = lax.optimization_barrier(jnp.mean(values, axis=-1, keepdims=True))
    centred = values - average
    variance = lax.optimization_barrier(jnp.mean(centred * centred, axis=-1, keepdims=True))
    return centred * lax.rsqrt(variance + EPSILON) * gain + bias

def feature_map(heads_in, projection):
    factor = HEAD_SIZE ** (-0.25)
    raw_proj = low_back(jnp.einsum('rhe,fe->rhf', heads_in, projection, precision=HIGHEST))
    squared = 0.5 * factor * factor * lax.optimization_barrier(jnp.sum(heads_in * heads_in, axis=-1, keepdims=True))
    return jnp.exp(factor * raw_proj - squared) * FEATURES ** (-0.5)

def cell_layer(tokens, alive, projection, params):
    first_gain, first_bias, query_weight, key_weight, value_weight, out_weight, out_bias, second_gain, second_bias, up_weight, up_bias, down_weight, down_bias = params
    rows_here = tokens.shape[0]
    normed = low(layer_norm(tokens, first_gain, first_bias))
    queries = low(low_back(jnp.dot(normed, query_weight, precision=HIGHEST))).reshape(rows_here, HEADS, HEAD_SIZE)
    keys = low(low_back(jnp.dot(normed, key_weight, precision=HIGHEST))).reshape(rows_here, HEADS, HEAD_SIZE)
    values = low(low_back(jnp.dot(normed, value_weight, precision=HIGHEST))).reshape(rows_here, HEADS, HEAD_SIZE)
    phi_query = low(feature_map(queries, projection))
    phi_key = low(feature_map(keys, projection)) * alive[:, None, None]
    extended = jnp.concatenate([values, jnp.ones_like(values[..., :1])], axis=-1)
    kernel = low(low_back(jnp.einsum('rhf,rhe->hfe', phi_key, extended, precision=HIGHEST)))
    combined = low_back(jnp.einsum('rhf,hfe->rhe', phi_query, kernel, precision=HIGHEST))
    attended = low((combined[..., :HEAD_SIZE] / combined[..., HEAD_SIZE:]).reshape(rows_here, HEADS * HEAD_SIZE))
    mixed_rows = tokens + low_back(jnp.dot(attended, out_weight, precision=HIGHEST) + out_bias)
    second = low(layer_norm(mixed_rows, second_gain, second_bias))
    up_proj = low_back(jnp.dot(second, up_weight, precision=HIGHEST) + up_bias)
    activated = low(jax.nn.gelu(up_proj, approximate=False))
    result = mixed_rows + jnp.dot(activated, down_weight.T, precision=HIGHEST) + down_bias
    return jnp.where(alive[:, None] > 0, result, tokens)

def reference(tokens, cotangent, gene_count, expressed, projection, first_gain, first_bias, query_weight, key_weight, value_weight, out_weight, out_bias, second_gain, second_bias, up_weight, up_bias, down_weight, down_bias):
    slot_index = jnp.arange(SLOTS, dtype=jnp.int32)
    alive = ((slot_index[None, :] < gene_count[:, None]) & (expressed > 0)).astype(jnp.float32)
    fixed_proj = projection.astype(jnp.float32)
    params = (first_gain.astype(jnp.float32), first_bias.astype(jnp.float32), query_weight.astype(jnp.float32), key_weight.astype(jnp.float32), value_weight.astype(jnp.float32), out_weight.astype(jnp.float32), out_bias.astype(jnp.float32), second_gain.astype(jnp.float32), second_bias.astype(jnp.float32), up_weight.astype(jnp.float32), up_bias.astype(jnp.float32), down_weight.astype(jnp.float32), down_bias.astype(jnp.float32))
    token_rows = jnp.swapaxes(tokens.astype(jnp.float32), 1, 2)
    cotangent_rows = jnp.swapaxes(cotangent.astype(jnp.float32), 1, 2)

    def forward(inputs, weights):

        def one_cell(cell_item):
            return cell_layer(cell_item[0], cell_item[1], fixed_proj, weights)
        return lax.map(jax.checkpoint(one_cell), (inputs, alive))
    result, pullback = jax.vjp(forward, token_rows, params)
    grad_in, grad_weights = pullback(cotangent_rows)
    return (jnp.swapaxes(result, 1, 2).astype(jnp.bfloat16), jnp.swapaxes(grad_in, 1, 2).astype(jnp.bfloat16), grad_weights[0], grad_weights[1], grad_weights[2], grad_weights[3], grad_weights[4], grad_weights[5], grad_weights[6], grad_weights[7], grad_weights[8], grad_weights[9], grad_weights[10], grad_weights[11], grad_weights[12])
```

```python
import functools
import math

import jax
import jax.numpy as jnp
from jax import lax
from jax.experimental import pallas as pl
from jax.experimental.pallas import tpu as pltpu
from jax.sharding import PartitionSpec as P

HEADS = 10
HEAD_SIZE = 64
FEATURES = 266
D = 200
INNER = HEADS * HEAD_SIZE
FF = 800
EPSILON = 1e-05

MAIN = 256
REST = FEATURES - MAIN
LEFT = 128
EXT = 80
SUM_ROW = INNER
LEFT_ROW = INNER + 16
KROWS = LEFT_ROW + 48

C0 = HEAD_SIZE ** (-0.25)
LOG2E = 1.0 / math.log(2.0)
RAW_SCALE = C0 * LOG2E
SQ_SCALE = 0.5 * C0 * C0 * LOG2E
SHIFT = -0.5 * math.log2(FEATURES)
FF_CHUNK = 160
SMALL = 3 * D + FF + D

BF = jnp.bfloat16
F32 = jnp.float32
VMEM_LIMIT = 56 * 1024 * 1024


def dot(left, right):
    return jnp.dot(left, right, preferred_element_type=F32)


def dot_nt(left, right):
    return lax.dot_general(left, right, (((1,), (1,)), ((), ())), preferred_element_type=F32)


def dot_tn(left, right):
    return lax.dot_general(left, right, (((0,), (0,)), ((), ())), preferred_element_type=F32)


def norm_cols(values, gain, bias):
    average = jnp.mean(values, axis=0, keepdims=True)
    centred = values - average
    inverse = lax.rsqrt(jnp.mean(centred * centred, axis=0, keepdims=True) + EPSILON)
    normed = centred * inverse
    return normed * gain + bias, normed, inverse


def norm_cols_back(grad_out, normed, inverse, gain):
    scaled = grad_out * gain
    return inverse * (
        scaled
        - jnp.mean(scaled, axis=0, keepdims=True)
        - normed * jnp.mean(scaled * normed, axis=0, keepdims=True)
    )


def lane_sums(values):
    total = values[:, :128]
    for start in range(128, values.shape[1], 128):
        total = total + values[:, start : start + 128]
    return total


def head_of_left(shape, axis):
    return lax.broadcasted_iota(jnp.int32, shape, axis) // REST


def features(u_ref, phi_ref, phil_ref, s_ref, pm_ref, pl_ref):
    slots = u_ref.shape[1]

    def one(h, _):
        u = u_ref[pl.ds(pl.multiple_of(h * HEAD_SIZE, HEAD_SIZE), HEAD_SIZE), :]
        wide = u.astype(F32)
        shift = SHIFT - SQ_SCALE * jnp.sum(wide * wide, axis=0, keepdims=True)
        s_ref[pl.ds(h, 1), :] = shift
        raw = dot(pm_ref[...], u)
        phi_ref[pl.ds(pl.multiple_of(h * MAIN, MAIN), MAIN), :] = jnp.exp2(
            raw * RAW_SCALE + shift
        ).astype(BF)
        return 0

    lax.fori_loop(0, HEADS, one, 0, unroll=2)
    owner = head_of_left((LEFT, slots), 0)
    shifts = jnp.zeros((LEFT, slots), F32)
    for h in range(HEADS):
        shifts = jnp.where(owner == h, s_ref[h : h + 1, :], shifts)
    raw = dot(pl_ref[...], u_ref[...])
    phil_ref[...] = jnp.exp2(raw * RAW_SCALE + shifts).astype(BF)


def write_kernel(out_ref, ext_ref, phi_ref, phil_ref, ks_ref):
    def one(h, _):
        total = dot_nt(
            ext_ref[pl.ds(pl.multiple_of(h * EXT, 16), EXT), :],
            phi_ref[pl.ds(pl.multiple_of(h * MAIN, MAIN), MAIN), :],
        )
        out_ref[0, pl.ds(pl.multiple_of(h * HEAD_SIZE, HEAD_SIZE), HEAD_SIZE), :] = total[
            :HEAD_SIZE
        ].astype(BF)
        ks_ref[pl.ds(h, 1), :] = total[HEAD_SIZE : HEAD_SIZE + 1]
        return 0

    ks_ref[...] = jnp.zeros_like(ks_ref)
    lax.fori_loop(0, HEADS, one, 0, unroll=2)
    out_ref[0, SUM_ROW : SUM_ROW + 16, :] = ks_ref[...].astype(BF)
    every = dot_nt(ext_ref[...], phil_ref[...])
    owner = head_of_left((EXT, LEFT), 1)
    left = jnp.zeros((EXT, LEFT), F32)
    for h in range(HEADS):
        left = jnp.where(owner == h, every[h * EXT : (h + 1) * EXT], left)
    left = left.astype(BF)
    out_ref[0, LEFT_ROW:KROWS, 0:LEFT] = left[:48]
    out_ref[0, LEFT_ROW : LEFT_ROW + 32, LEFT:MAIN] = left[48:EXT]
    out_ref[0, LEFT_ROW + 32 : KROWS, LEFT:MAIN] = jnp.zeros((16, LEFT), BF)


def read_kernel(in_ref, kt_ref, kl_ref):
    sums = in_ref[0, SUM_ROW : SUM_ROW + 16, :].astype(F32)
    first = lax.broadcasted_iota(jnp.int32, (16, MAIN), 0) == 0
    left = jnp.concatenate(
        [in_ref[0, LEFT_ROW:KROWS, 0:LEFT], in_ref[0, LEFT_ROW : LEFT_ROW + 32, LEFT:MAIN]], axis=0
    ).astype(F32)
    owner = head_of_left((EXT, LEFT), 1)
    for h in range(HEADS):
        kt_ref[h * EXT : h * EXT + HEAD_SIZE, :] = in_ref[0, h * HEAD_SIZE : (h + 1) * HEAD_SIZE, :]
        kt_ref[h * EXT + HEAD_SIZE : (h + 1) * EXT, :] = jnp.where(
            first, sums[h : h + 1, :], 0.0
        ).astype(BF)
        kl_ref[h * EXT : (h + 1) * EXT, :] = jnp.where(owner == h, left, 0.0).astype(BF)


def feature_grads(
    grad_ref, u_ref, phi_ref, phil_ref, kt_ref, kl_ref, ext_ref, tm_ref, tl_ref, wide_ref
):
    phil_ref[...] = (dot_tn(kl_ref[...], ext_ref[...]) * phil_ref[...].astype(F32)).astype(BF)
    wide_ref[...] = dot(tl_ref[...], phil_ref[...])

    def one(h, _):
        ext_rows = pl.ds(pl.multiple_of(h * EXT, 16), EXT)
        main_rows = pl.ds(pl.multiple_of(h * MAIN, MAIN), MAIN)
        head_rows = pl.ds(pl.multiple_of(h * HEAD_SIZE, HEAD_SIZE), HEAD_SIZE)
        weighted = (
            dot_tn(kt_ref[ext_rows, :], ext_ref[ext_rows, :]) * phi_ref[main_rows, :].astype(F32)
        ).astype(BF)
        through = dot(tm_ref[...], weighted) + wide_ref[ext_rows, :]
        grad_ref[head_rows, :] = (
            C0 * through[:HEAD_SIZE]
            - (C0 * C0) * u_ref[head_rows, :].astype(F32) * through[HEAD_SIZE : HEAD_SIZE + 1]
        ).astype(BF)
        return 0

    lax.fori_loop(0, HEADS, one, 0, unroll=2)


def extended_values(ext_ref, v_ref, alive):
    slots = v_ref.shape[1]
    mark = jnp.where(lax.broadcasted_iota(jnp.int32, (16, slots), 0) == 0, alive, 0.0).astype(BF)
    for h in range(HEADS):
        ext_ref[h * EXT : h * EXT + HEAD_SIZE, :] = (
            v_ref[h * HEAD_SIZE : (h + 1) * HEAD_SIZE, :].astype(F32) * alive
        ).astype(BF)
        ext_ref[h * EXT + HEAD_SIZE : (h + 1) * EXT, :] = mark


def first_body(
    x_ref, alive_ref, g1_ref, b1_ref, wkvt_ref, pm_ref, pl_ref,
    out_ref,
    kv_ref, ext_ref, phi_ref, phil_ref, s_ref, ks_ref,
):
    normed, _, _ = norm_cols(x_ref[0].astype(F32), g1_ref[...], b1_ref[...])
    kv_ref[...] = dot(wkvt_ref[...], normed.astype(BF)).astype(BF)
    extended_values(ext_ref, kv_ref.at[INNER:], alive_ref[0])
    features(kv_ref.at[:INNER], phi_ref, phil_ref, s_ref, pm_ref, pl_ref)
    write_kernel(out_ref, ext_ref, phi_ref, phil_ref, ks_ref)


def second_body(
    x_ref, dy_ref, alive_ref, k_ref, g1_ref, b1_ref, g2_ref, b2_ref, ob_ref, ub_ref, db_ref,
    wqt_ref, wq_ref, wot_ref, wo_ref, upt_ref, up_ref, downt_ref, down_ref,
    pm_ref, pl_ref, tm_ref, tl_ref,
    out_ref, gmix_ref, gnq_ref, kg_ref, dwq_ref, dwo_ref, dup_ref, ddown_ref, small_ref,
    q_ref, gq_ref, ext_ref, phi_ref, phil_ref, s_ref, ks_ref, kt_ref, kl_ref, wide_ref,
    att_ref, rec_ref, act_ref, gup_ref,
):
    slots = x_ref.shape[2]

    @pl.when(pl.program_id(0) == 0)
    def _():
        for ref in (dwq_ref, dwo_ref, dup_ref, ddown_ref, small_ref):
            ref[...] = jnp.zeros_like(ref)

    alive = alive_ref[0]
    row_alive = alive > 0
    tokens = x_ref[0].astype(F32)
    normed, _, _ = norm_cols(tokens, g1_ref[...], b1_ref[...])
    normed_low = normed.astype(BF)
    q_ref[...] = dot(wqt_ref[...], normed_low).astype(BF)
    read_kernel(k_ref, kt_ref, kl_ref)
    features(q_ref, phi_ref, phil_ref, s_ref, pm_ref, pl_ref)
    wide_ref[...] = dot(kl_ref[...], phil_ref[...])

    def attend(h, _):
        ext_rows = pl.ds(pl.multiple_of(h * EXT, 16), EXT)
        main_rows = pl.ds(pl.multiple_of(h * MAIN, MAIN), MAIN)
        head_rows = pl.ds(pl.multiple_of(h * HEAD_SIZE, HEAD_SIZE), HEAD_SIZE)
        combined = dot(kt_ref[ext_rows, :], phi_ref[main_rows, :]) + wide_ref[ext_rows, :]
        inverse = 1.0 / jnp.where(row_alive, combined[HEAD_SIZE : HEAD_SIZE + 1], 1.0)
        rec_ref[pl.ds(h, 1), :] = inverse
        quotient = combined[:HEAD_SIZE] * inverse
        wide_ref[pl.ds(pl.multiple_of(h * EXT, 16), HEAD_SIZE), :] = quotient
        att_ref[head_rows, :] = quotient.astype(BF)
        return 0

    lax.fori_loop(0, HEADS, attend, 0, unroll=2)
    mixed = tokens + dot(wot_ref[...], att_ref[...]) + ob_ref[...]
    second, second_normed, second_inverse = norm_cols(mixed, g2_ref[...], b2_ref[...])
    second_low = second.astype(BF)
    upstream_wide = jnp.where(row_alive, dy_ref[0].astype(F32), 0.0)
    upstream = upstream_wide.astype(BF)

    def feed(c, _):
        rows = pl.ds(pl.multiple_of(c * FF_CHUNK, 16), FF_CHUNK)
        up = dot(upt_ref[rows, :], second_low) + ub_ref[rows, :]
        grad_act = dot(downt_ref[rows, :], upstream)
        half = 0.5 * (1.0 + lax.erf(up * 0.7071067811865476))
        act_ref[rows, :] = (up * half).astype(BF)
        slope = half + up * jnp.exp(-0.5 * up * up) * 0.3989422804014327
        grad_up = (grad_act * slope).astype(BF)
        gup_ref[rows, :] = grad_up
        sums = pl.ds(pl.multiple_of(3 * D + c * FF_CHUNK, 8), FF_CHUNK)
        small_ref[sums, :] += lane_sums(grad_up.astype(F32))
        return 0

    lax.fori_loop(0, FF // FF_CHUNK, feed, 0)
    result = mixed + dot(down_ref[...], act_ref[...]) + db_ref[...]
    out_ref[0] = jnp.where(row_alive, result, tokens).astype(BF)
    ddown_ref[...] += dot_nt(upstream, act_ref[...])
    dup_ref[...] += dot_nt(second_low, gup_ref[...])
    small_ref[3 * D + FF :, :] += lane_sums(upstream_wide)
    grad_second = dot(up_ref[...], gup_ref[...])
    small_ref[0:D, :] += lane_sums(grad_second * second_normed)
    small_ref[D : 2 * D, :] += lane_sums(grad_second)
    grad_mixed = upstream_wide + norm_cols_back(
        grad_second, second_normed, second_inverse, g2_ref[...]
    )
    gmix_ref[0] = grad_mixed
    grad_branch = grad_mixed.astype(BF)
    small_ref[2 * D : 3 * D, :] += lane_sums(grad_branch.astype(F32))
    dwo_ref[...] += dot_nt(att_ref[...], grad_branch)
    pad_row = lax.broadcasted_iota(jnp.int32, (16, slots), 0) == 0

    def attend_back(h, _):
        head_rows = pl.ds(pl.multiple_of(h * HEAD_SIZE, HEAD_SIZE), HEAD_SIZE)
        values = pl.ds(pl.multiple_of(h * EXT, 16), HEAD_SIZE)
        grad_att = dot(wo_ref[head_rows, :], grad_branch)
        inverse = rec_ref[pl.ds(h, 1), :]
        ext_ref[values, :] = (grad_att * inverse).astype(BF)
        grad_sum = -inverse * jnp.sum(grad_att * wide_ref[values, :], axis=0, keepdims=True)
        ext_ref[pl.ds(pl.multiple_of(h * EXT + HEAD_SIZE, 16), 16), :] = jnp.where(
            pad_row, grad_sum, 0.0
        ).astype(BF)
        return 0

    lax.fori_loop(0, HEADS, attend_back, 0, unroll=2)
    write_kernel(kg_ref, ext_ref, phi_ref, phil_ref, ks_ref)
    feature_grads(
        gq_ref, q_ref, phi_ref, phil_ref, kt_ref, kl_ref, ext_ref, tm_ref, tl_ref, wide_ref
    )
    dwq_ref[...] += dot_nt(normed_low, gq_ref[...])
    gnq_ref[0] = dot(wq_ref[...], gq_ref[...])


def third_body(
    x_ref, dy_ref, alive_ref, kg_ref, gmix_ref, gnq_ref, g1_ref, b1_ref, wkvt_ref, wkv_ref,
    pm_ref, pl_ref, tm_ref, tl_ref,
    out_ref, dwkv_ref, small_ref,
    kv_ref, gkv_ref, ext_ref, phi_ref, phil_ref, s_ref, kt_ref, kl_ref, wide_ref,
):
    @pl.when(pl.program_id(0) == 0)
    def _():
        for ref in (dwkv_ref, small_ref):
            ref[...] = jnp.zeros_like(ref)

    alive = alive_ref[0]
    row_alive = alive > 0
    tokens = x_ref[0].astype(F32)
    out, normed, inverse = norm_cols(tokens, g1_ref[...], b1_ref[...])
    out_low = out.astype(BF)
    kv_ref[...] = dot(wkvt_ref[...], out_low).astype(BF)
    extended_values(ext_ref, kv_ref.at[INNER:], alive)
    read_kernel(kg_ref, kt_ref, kl_ref)
    features(kv_ref.at[:INNER], phi_ref, phil_ref, s_ref, pm_ref, pl_ref)
    wide_ref[...] = dot(kl_ref[...], phil_ref[...])

    def value_back(h, _):
        values = pl.ds(pl.multiple_of(h * EXT, 16), HEAD_SIZE)
        main_rows = pl.ds(pl.multiple_of(h * MAIN, MAIN), MAIN)
        grad_rows = pl.ds(pl.multiple_of(INNER + h * HEAD_SIZE, HEAD_SIZE), HEAD_SIZE)
        grad = dot(kt_ref[values, :], phi_ref[main_rows, :]) + wide_ref[values, :]
        gkv_ref[grad_rows, :] = (grad * alive).astype(BF)
        return 0

    lax.fori_loop(0, HEADS, value_back, 0, unroll=2)
    feature_grads(
        gkv_ref.at[:INNER], kv_ref.at[:INNER], phi_ref, phil_ref, kt_ref, kl_ref, ext_ref,
        tm_ref, tl_ref, wide_ref,
    )
    dwkv_ref[...] += dot_nt(out_low, gkv_ref[...])
    grad_normed = gnq_ref[0] + dot(wkv_ref[...], gkv_ref[...])
    small_ref[0:D, :] += lane_sums(grad_normed * normed)
    small_ref[D : 2 * D, :] += lane_sums(grad_normed)
    grad_in = gmix_ref[0] + norm_cols_back(grad_normed, normed, inverse, g1_ref[...])
    out_ref[0] = jnp.where(row_alive, grad_in, dy_ref[0].astype(F32)).astype(BF)


def per_cell(rows, columns):
    return pl.BlockSpec((1, rows, columns), lambda i: (i, 0, 0))


def whole(array):
    return pl.BlockSpec(array.shape, lambda i: (0,) * len(array.shape))


def call(body, cells, ins, in_specs, outs, out_specs, scratch, flops):
    return pl.pallas_call(
        body,
        grid=(cells,),
        in_specs=in_specs,
        out_specs=out_specs,
        out_shape=outs,
        scratch_shapes=[pltpu.VMEM(shape, kind) for shape, kind in scratch],
        compiler_params=pltpu.CompilerParams(
            dimension_semantics=("arbitrary",), vmem_limit_bytes=VMEM_LIMIT
        ),
        cost_estimate=pl.CostEstimate(flops=flops, bytes_accessed=8000000, transcendentals=0),
    )(*ins)


def shards(
    tokens, cotangent, gene_count, expressed, projection, first_gain, first_bias, query_weight,
    key_weight, value_weight, out_weight, out_bias, second_gain, second_bias, up_weight, up_bias,
    down_weight, down_bias,
):
    cells, _, slots = tokens.shape
    position = lax.axis_index("tok")
    slot_index = position * slots + lax.broadcasted_iota(jnp.int32, (cells, slots), 1)
    alive = ((slot_index < gene_count[:, None]) & (expressed > 0)).astype(F32)[:, None, :]

    wkv = jnp.concatenate([key_weight, value_weight], axis=1)
    wkvt, wqt, wot, upt, downt = wkv.T, query_weight.T, out_weight.T, up_weight.T, down_weight.T
    main_proj = projection[:MAIN]
    rest_proj = projection[MAIN:]
    ones = jnp.ones((FEATURES, 1), BF)
    ext_proj = jnp.concatenate(
        [projection, ones, jnp.zeros((FEATURES, EXT - HEAD_SIZE - 1), BF)], axis=1
    ).T
    same = jnp.eye(HEADS, dtype=BF)
    left_proj = (same[:, None, :, None] * rest_proj[None, :, None, :]).reshape(HEADS * REST, INNER)
    left_proj = jnp.pad(left_proj, ((0, LEFT - HEADS * REST), (0, 0)))
    left_ext = (same[:, None, :, None] * ext_proj[:, MAIN:][None, :, None, :]).reshape(
        HEADS * EXT, HEADS * REST
    )
    left_ext = jnp.pad(left_ext, ((0, 0), (0, LEFT - HEADS * REST)))
    main_ext = ext_proj[:, :MAIN]
    g1, b1, g2, b2, ob, db, ub = (
        v[:, None]
        for v in (first_gain, first_bias, second_gain, second_bias, out_bias, down_bias, up_bias)
    )

    token_spec = per_cell(D, slots)
    alive_spec = per_cell(1, slots)
    kernel_spec = per_cell(KROWS, MAIN)
    kernel_shape = jax.ShapeDtypeStruct((cells, KROWS, MAIN), BF)
    rows = cells * slots

    ins = [tokens, alive, g1, b1, wkvt, main_proj, left_proj]
    kernel_part = call(
        first_body, cells, ins,
        [token_spec, alive_spec] + [whole(v) for v in ins[2:]],
        kernel_shape, kernel_spec,
        [
            ((2 * INNER, slots), BF), ((HEADS * EXT, slots), BF), ((HEADS * MAIN, slots), BF),
            ((LEFT, slots), BF), ((16, slots), F32), ((16, MAIN), F32),
        ],
        rows * 1500000,
    )
    kernels = lax.psum(kernel_part, "tok")

    ins = [
        tokens, cotangent, alive, kernels, g1, b1, g2, b2, ob, ub, db,
        wqt, query_weight, wot, out_weight, upt, up_weight, downt, down_weight,
        main_proj, left_proj, main_ext, left_ext,
    ]
    wide_spec = jax.ShapeDtypeStruct((cells, D, slots), F32)
    outs = [
        jax.ShapeDtypeStruct((cells, D, slots), BF), wide_spec, wide_spec, kernel_shape,
        jax.ShapeDtypeStruct((D, INNER), F32), jax.ShapeDtypeStruct((INNER, D), F32),
        jax.ShapeDtypeStruct((D, FF), F32), jax.ShapeDtypeStruct((D, FF), F32),
        jax.ShapeDtypeStruct((SMALL, 128), F32),
    ]
    result, grad_mixed, grad_nq, kernel_grad_part, dwq, dwo, dup, ddown, small2 = call(
        second_body, cells, ins,
        [token_spec, token_spec, alive_spec, kernel_spec] + [whole(v) for v in ins[4:]],
        outs, [token_spec, token_spec, token_spec, kernel_spec] + [whole(v) for v in outs[4:]],
        [
            ((INNER, slots), BF), ((INNER, slots), BF), ((HEADS * EXT, slots), BF),
            ((HEADS * MAIN, slots), BF), ((LEFT, slots), BF), ((16, slots), F32),
            ((16, MAIN), F32), ((HEADS * EXT, MAIN), BF), ((HEADS * EXT, LEFT), BF),
            ((HEADS * EXT, slots), F32), ((INNER, slots), BF), ((16, slots), F32),
            ((FF, slots), BF), ((FF, slots), BF),
        ],
        rows * 4500000,
    )
    kernel_grads = lax.psum(kernel_grad_part, "tok")

    ins = [
        tokens, cotangent, alive, kernel_grads, grad_mixed, grad_nq, g1, b1, wkvt, wkv,
        main_proj, left_proj, main_ext, left_ext,
    ]
    outs = [
        jax.ShapeDtypeStruct((cells, D, slots), BF),
        jax.ShapeDtypeStruct((D, 2 * INNER), F32),
        jax.ShapeDtypeStruct((2 * D, 128), F32),
    ]
    grad_in, dwkv, small3 = call(
        third_body, cells, ins,
        [token_spec, token_spec, alive_spec, kernel_spec, token_spec, token_spec]
        + [whole(v) for v in ins[6:]],
        outs, [token_spec] + [whole(v) for v in outs[1:]],
        [
            ((2 * INNER, slots), BF), ((2 * INNER, slots), BF), ((HEADS * EXT, slots), BF),
            ((HEADS * MAIN, slots), BF), ((LEFT, slots), BF), ((16, slots), F32),
            ((HEADS * EXT, MAIN), BF), ((HEADS * EXT, LEFT), BF), ((HEADS * EXT, slots), F32),
        ],
        rows * 3000000,
    )
    small = jnp.concatenate([jnp.sum(small2, axis=1), jnp.sum(small3, axis=1)])
    small, dwkv, dwq, dwo, dup, ddown = lax.psum(
        (small, dwkv, dwq, dwo, dup, ddown), ("cells", "tok")
    )
    gain2, bias2, outb = small[:D], small[D : 2 * D], small[2 * D : 3 * D]
    upb, downb = small[3 * D : 3 * D + FF], small[3 * D + FF : SMALL]
    gain1, bias1 = small[SMALL : SMALL + D], small[SMALL + D :]
    return (
        result, grad_in, gain1, bias1, dwq, dwkv[:, :INNER], dwkv[:, INNER:], dwo, outb,
        gain2, bias2, dup, upb, ddown, downb,
    )


def solution(mesh):
    rows = P("cells", None, "tok")
    placed = (rows, rows, P("cells"), P("cells", "tok")) + (P(),) * 14
    return jax.shard_map(
        shards,
        mesh=mesh,
        in_specs=placed,
        out_specs=(rows, rows) + (P(),) * 13,
        check_vma=False,
    )
```

```python
import math

import jax
import jax.numpy as jnp
from jax import lax
from jax.experimental import pallas as pl
from jax.experimental.pallas import tpu as pltpu
from jax.sharding import PartitionSpec as P

HEADS = 10
HEAD_SIZE = 64
FEATURES = 266
D = 200
INNER = HEADS * HEAD_SIZE
FF = 800
EPSILON = 1e-05

MAIN = 256
REST = FEATURES - MAIN
LEFT = 128
EXT = 80
SUM_ROW = INNER
LEFT_ROW = INNER + 16
KROWS = LEFT_ROW + 48

C0 = HEAD_SIZE ** (-0.25)
LOG2E = 1.0 / math.log(2.0)
RAW_SCALE = C0 * LOG2E
SQ_SCALE = 0.5 * C0 * C0 * LOG2E
SHIFT = -0.5 * math.log2(FEATURES)
FF_CHUNK = 160
SMALL2 = 4 * D + FF
Q_BLOCKS = INNER // 128
F_BLOCKS = -(-FF // 128)
GRAD2 = (2 * Q_BLOCKS + 2 * F_BLOCKS) * D
GRAD3 = 2 * Q_BLOCKS * D

BF = jnp.bfloat16
F32 = jnp.float32
VMEM_LIMIT = 56 * 1024 * 1024
GROUP = 4
PART = 2


def dot(left, right):
    return jnp.dot(left, right, preferred_element_type=F32)


def dot_nt(left, right):
    return lax.dot_general(left, right, (((1,), (1,)), ((), ())), preferred_element_type=F32)


def dot_tn(left, right):
    return lax.dot_general(left, right, (((0,), (0,)), ((), ())), preferred_element_type=F32)


def iota(shape, axis):
    return lax.broadcasted_iota(jnp.int32, shape, axis)


def norm_cols(values, gain, bias):
    average = jnp.mean(values, axis=0, keepdims=True)
    centred = values - average
    inverse = lax.rsqrt(jnp.mean(centred * centred, axis=0, keepdims=True) + EPSILON)
    normed = centred * inverse
    return normed * gain + bias, normed, inverse


def norm_cols_back(grad_out, normed, inverse, gain):
    scaled = grad_out * gain
    return inverse * (
        scaled
        - jnp.mean(scaled, axis=0, keepdims=True)
        - normed * jnp.mean(scaled * normed, axis=0, keepdims=True)
    )


def lane_sums(values):
    total = values[:, :128]
    for start in range(128, values.shape[1], 128):
        total = total + values[:, start : start + 128]
    return total


def ext_rows(h):
    return slice(h * EXT, (h + 1) * EXT)


def val_rows(h):
    return slice(h * EXT, h * EXT + HEAD_SIZE)


def main_rows(h):
    return slice(h * MAIN, (h + 1) * MAIN)


def head_rows(h):
    return slice(h * HEAD_SIZE, (h + 1) * HEAD_SIZE)


G1, B1, G2, B2, OB, DB, UB = range(7)


def column(cols_ref, which, rows=D):
    return cols_ref[0:rows, which : which + 1]


def prep_body(
    info_ref, vec_ref, projt_ref, wq_ref, wk_ref, wv_ref, wot_ref, up_ref, down_ref,
    cols_ref, wqt_ref, wkv_ref, wkvt_ref, wo_ref, upt_ref, downt_ref,
    pm_ref, pl_ref, tm_ref, tl_ref,
):
    cols_ref[...] = vec_ref[...].T
    wqt_ref[...] = wq_ref[...].T
    wkv_ref[:, :INNER] = wk_ref[...]
    wkv_ref[:, INNER:] = wv_ref[...]
    wkvt_ref[:INNER] = wk_ref[...].T
    wkvt_ref[INNER:] = wv_ref[...].T
    wo_ref[...] = wot_ref[...].T
    upt_ref[...] = up_ref[...].T
    downt_ref[...] = down_ref[...].T
    proj = projt_ref[...].T

    def one_hot(shape, mask):
        return jnp.where(mask, 1.0, 0.0).astype(BF)

    pm_ref[...] = proj[:MAIN]
    s = (16, FEATURES)
    rest = dot(one_hot(s, (iota(s, 0) + MAIN == iota(s, 1)) & (iota(s, 0) < REST)), proj).astype(BF)
    s = (HEAD_SIZE, INNER)
    wide = dot(rest, one_hot(s, iota(s, 0) == iota(s, 1) % HEAD_SIZE)).astype(BF)
    s = (LEFT, 16)
    tall = dot(one_hot(s, iota(s, 0) % REST == iota(s, 1)), wide)
    s = (LEFT, INNER)
    pl_ref[...] = jnp.where(iota(s, 0) // REST == iota(s, 1) // HEAD_SIZE, tall, 0.0).astype(BF)
    s = (EXT, HEAD_SIZE)
    pick = one_hot(s, iota(s, 0) == iota(s, 1))
    s = (EXT, MAIN)
    tm_ref[...] = jnp.where(iota(s, 0) == HEAD_SIZE, 1.0, dot_nt(pick, proj[:MAIN])).astype(BF)
    s = (EXT, 16)
    rest_ext = jnp.where(iota(s, 0) == HEAD_SIZE, 1.0, dot_nt(pick, rest)).astype(BF)
    s = (16, LEFT)
    spread = dot(rest_ext, one_hot(s, iota(s, 0) == iota(s, 1) % REST))
    s = (EXT, LEFT)
    for h in range(HEADS):
        tl_ref[ext_rows(h), :] = jnp.where(iota(s, 1) // REST == h, spread, 0.0).astype(BF)


def shifts_of(u_ref, s_ref):
    for h in range(HEADS):
        wide = u_ref[head_rows(h), :].astype(F32)
        s_ref[h : h + 1, :] = SHIFT - SQ_SCALE * jnp.sum(wide * wide, axis=0, keepdims=True)


def left_features(u_ref, phil_ref, s_ref, pl_ref):
    shape = (LEFT, u_ref.shape[1])
    owner = iota(shape, 0) // REST
    shifts = jnp.zeros(shape, F32)
    for h in range(HEADS):
        shifts = jnp.where(owner == h, s_ref[h : h + 1, :], shifts)
    phil_ref[...] = jnp.exp2(dot(pl_ref[...], u_ref[...]) * RAW_SCALE + shifts).astype(BF)


def main_features(h, u_ref, phi_ref, s_ref, pm_ref):
    raw = dot(pm_ref[...], u_ref[head_rows(h), :])
    phi_ref[main_rows(h), :] = jnp.exp2(raw * RAW_SCALE + s_ref[h : h + 1, :]).astype(BF)


def add_head_kernel(h, acc_ref, ext_ref, phi_ref):
    total = dot_nt(ext_ref[ext_rows(h), :], phi_ref[main_rows(h), :])
    acc_ref[head_rows(h), :] += total[:HEAD_SIZE]
    acc_ref[SUM_ROW + h : SUM_ROW + h + 1, :] += total[HEAD_SIZE : HEAD_SIZE + 1]


def add_left_kernel(acc_ref, ext_ref, phil_ref):
    every = dot_nt(ext_ref[...], phil_ref[...])
    owner = iota((EXT, LEFT), 1) // REST
    left = jnp.zeros((EXT, LEFT), F32)
    for h in range(HEADS):
        left = jnp.where(owner == h, every[ext_rows(h)], left)
    acc_ref[LEFT_ROW:KROWS, 0:LEFT] += left[:48]
    acc_ref[LEFT_ROW : LEFT_ROW + 32, LEFT:MAIN] += left[48:EXT]


def sum_kernels(in_refs, whole_ref):
    total = in_refs[0][...].astype(F32)
    for ref in in_refs[1:]:
        total = total + ref[...].astype(F32)
    whole_ref[...] = total.astype(BF)


def read_kernel(whole_ref, kt_ref, kl_ref):
    sums = whole_ref[SUM_ROW : SUM_ROW + 16, :].astype(F32)
    first = iota((16, MAIN), 0) == 0
    left = jnp.concatenate(
        [whole_ref[LEFT_ROW:KROWS, 0:LEFT], whole_ref[LEFT_ROW : LEFT_ROW + 32, LEFT:MAIN]], axis=0
    ).astype(F32)
    owner = iota((EXT, LEFT), 1) // REST
    for h in range(HEADS):
        kt_ref[val_rows(h), :] = whole_ref[head_rows(h), :]
        kt_ref[h * EXT + HEAD_SIZE : (h + 1) * EXT, :] = jnp.where(
            first, sums[h : h + 1, :], 0.0
        ).astype(BF)
        kl_ref[ext_rows(h), :] = jnp.where(owner == h, left, 0.0).astype(BF)


def left_grads(phil_ref, kl_ref, ext_ref, tl_ref, wide_ref):
    phil_ref[...] = (dot_tn(kl_ref[...], ext_ref[...]) * phil_ref[...].astype(F32)).astype(BF)
    wide_ref[...] = dot(tl_ref[...], phil_ref[...])


def main_grads(h, grad_ref, u_ref, phi_ref, kt_ref, ext_ref, tm_ref, wide_ref):
    weighted = (
        dot_tn(kt_ref[ext_rows(h), :], ext_ref[ext_rows(h), :]) * phi_ref[main_rows(h), :].astype(F32)
    ).astype(BF)
    through = dot(tm_ref[...], weighted) + wide_ref[ext_rows(h), :]
    grad_ref[head_rows(h), :] = (
        C0 * through[:HEAD_SIZE]
        - (C0 * C0) * u_ref[head_rows(h), :].astype(F32) * through[HEAD_SIZE : HEAD_SIZE + 1]
    ).astype(BF)


def keys_values(normed_low, alive, wkvt_ref, k_ref, ext_ref):
    k_ref[...] = dot(wkvt_ref[:INNER, :], normed_low).astype(BF)
    values = dot(wkvt_ref[INNER:, :], normed_low)
    mark = jnp.where(iota((16, values.shape[1]), 0) == 0, alive, 0.0).astype(BF)
    for h in range(HEADS):
        ext_ref[val_rows(h), :] = (values[head_rows(h)] * alive).astype(BF)
        ext_ref[h * EXT + HEAD_SIZE : (h + 1) * EXT, :] = mark


def key_sums(x, alive, cols_ref, wkvt_ref, pm_ref, pl_ref, acc_ref, k_ref, ext_ref, phi_ref, phil_ref, s_ref):
    normed, _, _ = norm_cols(x, column(cols_ref, G1), column(cols_ref, B1))
    keys_values(normed.astype(BF), alive, wkvt_ref, k_ref, ext_ref)
    shifts_of(k_ref, s_ref)
    left_features(k_ref, phil_ref, s_ref, pl_ref)
    for h in range(HEADS):
        main_features(h, k_ref, phi_ref, s_ref, pm_ref)
        add_head_kernel(h, acc_ref, ext_ref, phi_ref)
    add_left_kernel(acc_ref, ext_ref, phil_ref)


def first_body(turn):
    def body(info_ref, x_ref, alive_ref, cols_ref, wkvt_ref, pm_ref, pl_ref, out_ref, acc_ref, *scratch):
        j = pl.program_id(0)

        @pl.when(j == 0)
        def _():
            acc_ref[...] = jnp.zeros_like(acc_ref)

        key_sums(
            x_ref[0].astype(F32), alive_ref[0, turn : turn + 1, :], cols_ref, wkvt_ref, pm_ref, pl_ref,
            acc_ref, *scratch,
        )

        @pl.when(j == pl.num_programs(0) - 1)
        def _():
            out_ref[...] = acc_ref[...].astype(BF)

    return body


def add_blocks(acc_ref, first, values, width):
    for c in range(-(-width // 128)):
        take = min(128, width - c * 128)
        acc_ref[first + c * D : first + (c + 1) * D, 0:take] += values[:, c * 128 : c * 128 + take]


def put_block(out_refs, j, value):
    for k, ref in enumerate(out_refs):

        @pl.when(j == k)
        def _():
            ref[0] = value


def second_body(turn, blocks, start, waits):
    def body(info_ref, x_ref, dy_ref, alive_ref, *rest):
        k_refs, rest = rest[:blocks], rest[blocks:]
        if not start:
            (ga_in, sm_in), rest = rest[:2], rest[2:]
        (
            cols_ref, wqt_ref, wq_ref, wot_ref, wo_ref, upt_ref, up_ref, downt_ref, down_ref,
            pm_ref, pl_ref, tm_ref, tl_ref,
        ), rest = rest[:13], rest[13 + waits :]
        out_refs, rest = rest[:GROUP], rest[GROUP:]
        (
            gmix_ref, gnq_ref, kg_ref, ga_ref, sm_ref,
            whole_ref, acc_ref, q_ref, gq_ref, ext_ref, phi_ref, phil_ref, s_ref, kt_ref, kl_ref, wide_ref,
            att_ref, rec_ref, act_ref, gup_ref,
        ) = rest
        j = pl.program_id(0)

        @pl.when(j == 0)
        def _():
            if start:
                ga_ref[...] = jnp.zeros_like(ga_ref)
                sm_ref[...] = jnp.zeros_like(sm_ref)
            else:
                ga_ref[...] = ga_in[...]
                sm_ref[...] = sm_in[...]
            acc_ref[...] = jnp.zeros_like(acc_ref)
            sum_kernels(k_refs, whole_ref)
            read_kernel(whole_ref, kt_ref, kl_ref)

        alive = alive_ref[0, turn : turn + 1, :]
        row_alive = alive > 0
        tokens = x_ref[0].astype(F32)
        normed, _, _ = norm_cols(tokens, column(cols_ref, G1), column(cols_ref, B1))
        normed_low = normed.astype(BF)
        q_ref[...] = dot(wqt_ref[...], normed_low).astype(BF)
        shifts_of(q_ref, s_ref)
        left_features(q_ref, phil_ref, s_ref, pl_ref)
        wide_ref[...] = dot(kl_ref[...], phil_ref[...])
        for h in range(HEADS):
            main_features(h, q_ref, phi_ref, s_ref, pm_ref)
            combined = dot(kt_ref[ext_rows(h), :], phi_ref[main_rows(h), :]) + wide_ref[ext_rows(h), :]
            inverse = 1.0 / jnp.where(row_alive, combined[HEAD_SIZE : HEAD_SIZE + 1], 1.0)
            rec_ref[h : h + 1, :] = inverse
            quotient = combined[:HEAD_SIZE] * inverse
            wide_ref[val_rows(h), :] = quotient
            att_ref[head_rows(h), :] = quotient.astype(BF)
        mixed = tokens + dot(wot_ref[...], att_ref[...]) + column(cols_ref, OB)
        second, second_normed, second_inverse = norm_cols(
            mixed, column(cols_ref, G2), column(cols_ref, B2)
        )
        second_low = second.astype(BF)
        upstream_wide = jnp.where(row_alive, dy_ref[0].astype(F32), 0.0)
        upstream = upstream_wide.astype(BF)
        for c in range(FF // FF_CHUNK):
            rows = slice(c * FF_CHUNK, (c + 1) * FF_CHUNK)
            up = dot(upt_ref[rows, :], second_low) + cols_ref[rows, UB : UB + 1]
            grad_act = dot(downt_ref[rows, :], upstream)
            half = 0.5 * (1.0 + lax.erf(up * 0.7071067811865476))
            act_ref[rows, :] = (up * half).astype(BF)
            slope = half + up * jnp.exp(-0.5 * up * up) * 0.3989422804014327
            grad_up = (grad_act * slope).astype(BF)
            gup_ref[rows, :] = grad_up
            sm_ref[4 * D + c * FF_CHUNK : 4 * D + (c + 1) * FF_CHUNK, :] += lane_sums(grad_up.astype(F32))
        result = mixed + dot(down_ref[...], act_ref[...]) + column(cols_ref, DB)
        put_block(out_refs, j, jnp.where(row_alive, result, tokens).astype(BF))

        add_blocks(ga_ref, (2 * Q_BLOCKS + F_BLOCKS) * D, dot_nt(upstream, act_ref[...]), FF)
        add_blocks(ga_ref, 2 * Q_BLOCKS * D, dot_nt(second_low, gup_ref[...]), FF)
        sm_ref[3 * D : 4 * D, :] += lane_sums(upstream_wide)
        grad_second = dot(up_ref[...], gup_ref[...])
        sm_ref[0:D, :] += lane_sums(grad_second * second_normed)
        sm_ref[D : 2 * D, :] += lane_sums(grad_second)
        grad_mixed = upstream_wide + norm_cols_back(
            grad_second, second_normed, second_inverse, column(cols_ref, G2)
        )
        gmix_ref[0] = grad_mixed
        grad_branch = grad_mixed.astype(BF)
        sm_ref[2 * D : 3 * D, :] += lane_sums(grad_branch.astype(F32))
        add_blocks(ga_ref, Q_BLOCKS * D, dot_nt(grad_branch, att_ref[...]), INNER)
        pad_row = iota((16, alive.shape[1]), 0) == 0
        grad_att = dot(wo_ref[...], grad_branch)
        for h in range(HEADS):
            grad_head = grad_att[head_rows(h)]
            inverse = rec_ref[h : h + 1, :]
            ext_ref[val_rows(h), :] = (grad_head * inverse).astype(BF)
            grad_sum = -inverse * jnp.sum(grad_head * wide_ref[val_rows(h), :], axis=0, keepdims=True)
            ext_ref[h * EXT + HEAD_SIZE : (h + 1) * EXT, :] = jnp.where(pad_row, grad_sum, 0.0).astype(BF)
        add_left_kernel(acc_ref, ext_ref, phil_ref)
        left_grads(phil_ref, kl_ref, ext_ref, tl_ref, wide_ref)
        for h in range(HEADS):
            add_head_kernel(h, acc_ref, ext_ref, phi_ref)
            main_grads(h, gq_ref, q_ref, phi_ref, kt_ref, ext_ref, tm_ref, wide_ref)
        add_blocks(ga_ref, 0, dot_nt(normed_low, gq_ref[...]), INNER)
        gnq_ref[0] = dot(wq_ref[...], gq_ref[...])

        @pl.when(j == pl.num_programs(0) - 1)
        def _():
            kg_ref[...] = acc_ref[...].astype(BF)

    return body


def third_body(turn, blocks, start, waits):
    def body(info_ref, x_ref, dy_ref, alive_ref, gmix_ref, gnq_ref, *rest):
        k_refs, rest = rest[:blocks], rest[blocks:]
        if not start:
            (ga_in, sm_in), rest = rest[:2], rest[2:]
        (
            cols_ref, wkvt_ref, wkv_ref, pm_ref, pl_ref, tm_ref, tl_ref,
        ), rest = rest[:7], rest[7 + waits :]
        out_refs, rest = rest[:PART], rest[PART:]
        (
            ga_ref, sm_ref,
            whole_ref, k_ref, gkv_ref, ext_ref, phi_ref, phil_ref, s_ref, kt_ref, kl_ref, wide_ref,
        ) = rest
        j = pl.program_id(0)

        @pl.when(j == 0)
        def _():
            if start:
                ga_ref[...] = jnp.zeros_like(ga_ref)
                sm_ref[...] = jnp.zeros_like(sm_ref)
            else:
                ga_ref[...] = ga_in[...]
                sm_ref[...] = sm_in[...]
            sum_kernels(k_refs, whole_ref)
            read_kernel(whole_ref, kt_ref, kl_ref)

        alive = alive_ref[0, turn : turn + 1, :]
        tokens = x_ref[0].astype(F32)
        out, normed, inverse = norm_cols(tokens, column(cols_ref, G1), column(cols_ref, B1))
        out_low = out.astype(BF)
        keys_values(out_low, alive, wkvt_ref, k_ref, ext_ref)
        shifts_of(k_ref, s_ref)
        left_features(k_ref, phil_ref, s_ref, pl_ref)
        wide_ref[...] = dot(kl_ref[...], phil_ref[...])
        for h in range(HEADS):
            main_features(h, k_ref, phi_ref, s_ref, pm_ref)
            grad = dot(kt_ref[val_rows(h), :], phi_ref[main_rows(h), :]) + wide_ref[val_rows(h), :]
            gkv_ref[INNER + h * HEAD_SIZE : INNER + (h + 1) * HEAD_SIZE, :] = (grad * alive).astype(BF)
        left_grads(phil_ref, kl_ref, ext_ref, tl_ref, wide_ref)
        for h in range(HEADS):
            main_grads(h, gkv_ref, k_ref, phi_ref, kt_ref, ext_ref, tm_ref, wide_ref)
        add_blocks(ga_ref, 0, dot_nt(out_low, gkv_ref[...]), 2 * INNER)
        grad_normed = gnq_ref[0] + dot(wkv_ref[...], gkv_ref[...])
        sm_ref[0:D, :] += lane_sums(grad_normed * normed)
        sm_ref[D : 2 * D, :] += lane_sums(grad_normed)
        grad_in = gmix_ref[0] + norm_cols_back(grad_normed, normed, inverse, column(cols_ref, G1))
        put_block(out_refs, j, jnp.where(alive > 0, grad_in, dy_ref[0].astype(F32)).astype(BF))

    return body


def pack_body(sizes):
    def body(info_ref, ga_ref, sm_ref, *rest):
        out_ref = rest[-1]
        base = ga_ref.shape[0]
        out_ref[0:base, :] = ga_ref[...].astype(BF)
        high = sm_ref[...].astype(BF)
        low = (sm_ref[...] - high.astype(F32)).astype(BF)
        ones = jnp.ones((8, 128), BF)
        lines = []
        first = 0
        for size in sizes:
            line = dot_nt(ones, high[first : first + size]) + dot_nt(ones, low[first : first + size])
            for c in range(-(-size // 128)):
                take = min(128, size - c * 128)
                piece = line[0:1, c * 128 : c * 128 + take]
                if take < 128:
                    piece = jnp.concatenate([piece, jnp.zeros((1, 128 - take), F32)], axis=1)
                lines.append(piece)
            first += size
        left = out_ref.shape[0] - base - len(lines)
        lines.append(jnp.zeros((left, 128), F32))
        out_ref[base:, :] = jnp.concatenate(lines, axis=0).astype(BF)

    return body


def place_body(info_ref, *refs):
    for k, ref in enumerate(refs[:-1]):

        @pl.when(pl.program_id(0) == k)
        def _():
            refs[-1][...] = ref[...]


def unpack_body(pieces, sizes):
    def body(info_ref, in_ref, *rest):
        out_refs, whole_ref = rest[:-1], rest[-1]
        whole_ref[...] = in_ref[...].astype(F32)
        row = 0
        for ref, (first, width, transposed) in zip(out_refs, pieces):
            for c in range(-(-width // 128)):
                take = min(128, width - c * 128)
                block = whole_ref[first + c * D : first + (c + 1) * D, 0:take]
                if transposed:
                    ref[c * 128 : c * 128 + take, :] = block.T
                else:
                    ref[:, c * 128 : c * 128 + take] = block
                row = max(row, first + (c + 1) * D)
        for ref, size in zip(out_refs[len(pieces) :], sizes):
            for c in range(-(-size // 128)):
                take = min(128, size - c * 128)
                ref[:, c * 128 : c * 128 + take] = whole_ref[row : row + 1, 0:take]
                row += 1

    return body


def whole(array):
    zeros = (0,) * len(array.shape)
    return pl.BlockSpec(array.shape, lambda i, info: zeros)


def call(body, info, ins, in_specs, outs, out_specs, scratch, grid=1, us=1, aliases=None, waits=()):
    return pl.pallas_call(
        body,
        grid_spec=pltpu.PrefetchScalarGridSpec(
            num_scalar_prefetch=1,
            grid=(grid,),
            in_specs=in_specs + [pl.BlockSpec(memory_space=pl.ANY)] * len(waits),
            out_specs=out_specs,
            scratch_shapes=[pltpu.VMEM(shape, kind) for shape, kind in scratch],
        ),
        out_shape=outs,
        input_output_aliases=aliases or {},
        compiler_params=pltpu.CompilerParams(
            dimension_semantics=("arbitrary",), vmem_limit_bytes=VMEM_LIMIT
        ),
        cost_estimate=pl.CostEstimate(
            flops=int(us * 1.15e9), bytes_accessed=1000000, transcendentals=0
        ),
    )(info, *ins, *waits)


def swap(value, axis, groups=None):
    return lax.all_to_all(value, axis, 0, 0, axis_index_groups=groups, tiled=True)


def share_kernel(part, nt):
    others = nt // GROUP
    got = [part]
    for s in range(1, others):
        got.append(lax.ppermute(part, "tok", [(i, (i + s * GROUP) % nt) for i in range(nt)]))
    return got


def exchange(values, shift, nt):
    moves = [(i, i - i % GROUP + (i + shift) % GROUP) for i in range(nt)]
    return lax.ppermute(values, "tok", moves) if shift else values


class Reduction:
    def __init__(self, info, grads, small, sizes, nc, nt, waits=()):
        need = grads.shape[0] + sum(-(-size // 128) for size in sizes)
        unit = nc * nt * 16
        self.rows = -(-need // unit) * unit
        self.nc, self.nt, self.sizes, self.info = nc, nt, sizes, info
        self.quarter, self.share = self.rows // nc, self.rows // (nc * nt)
        packed = jax.ShapeDtypeStruct((self.rows, 128), BF)
        self.packed = call(
            pack_body(sizes), info, [grads, small], [whole(grads), whole(small)], packed, whole(packed), [],
            waits=waits,
        )

    def total(self, value, count, size):
        return jnp.sum(value.reshape(count, size, 128).astype(F32), axis=0).astype(BF)

    def copies(self, value, count):
        return jnp.broadcast_to(value[None], (count,) + value.shape)

    def over_cells(self):
        self.one = swap(self.packed.reshape(self.nc, self.quarter, 128), "cells")
        return self.one

    def over_tok(self):
        mine = self.total(self.one, self.nc, self.quarter)
        self.two = swap(mine.reshape(self.nt, self.share, 128), "tok")
        return self.two

    def back_tok(self):
        mine = self.total(self.two, self.nt, self.share)
        self.three = swap(self.copies(mine, self.nt), "tok")
        return self.three

    def back_cells(self):
        self.four = swap(self.copies(self.three.reshape(self.quarter, 128), self.nc), "cells")
        return self.four

    def results(self, pieces, outs):
        joined = self.four.reshape(self.rows, 128)
        outs = outs + [jax.ShapeDtypeStruct((1, size), F32) for size in self.sizes]
        outs = call(
            unpack_body(pieces, self.sizes), self.info, [joined], [whole(joined)],
            outs, [whole(v) for v in outs], [((self.rows, 128), F32)],
        )
        return outs[: len(pieces)], [v[0] for v in outs[len(pieces) :]]


def place(info, pieces, cells):
    like = pieces[0]
    shape = (cells,) + like.shape[1:]

    def cell(i, info):
        return i // GROUP * GROUP + lax.rem(info[0] + GROUP - lax.rem(i, GROUP), GROUP), 0, 0

    return call(
        place_body, info, pieces, [whole(v) for v in pieces],
        jax.ShapeDtypeStruct(shape, like.dtype), pl.BlockSpec(like.shape, cell), [], grid=cells, us=3,
    )


def shards(
    tokens, cotangent, gene_count, expressed, projection, first_gain, first_bias, query_weight,
    key_weight, value_weight, out_weight, out_bias, second_gain, second_bias, up_weight, up_bias,
    down_weight, down_bias,
):
    cells, _, slots = tokens.shape
    turns = cells // GROUP
    nt, nc = lax.axis_size("tok"), lax.axis_size("cells")
    position = lax.axis_index("tok")
    groups = [[g * GROUP + i for i in range(GROUP)] for g in range(nt // GROUP)]
    info = jnp.stack([position % GROUP]).astype(jnp.int32)

    def to_cells(array, c):
        return swap(array[c * GROUP : (c + 1) * GROUP], "tok", groups)

    slot_index = position * slots + lax.broadcasted_iota(jnp.int32, (cells, slots), 1)
    alive = ((slot_index < gene_count[:, None]) & (expressed > 0)).astype(F32)
    alive = jnp.swapaxes(alive.reshape(turns, GROUP, slots), 0, 1)
    alive = swap(alive, "tok", groups)
    x = [to_cells(tokens, c) for c in range(turns)]
    dy = [to_cells(cotangent, c) for c in range(turns)]

    vectors = [first_gain, first_bias, second_gain, second_bias, out_bias, down_bias, up_bias]
    vec = jnp.stack([jnp.pad(v, (0, FF - v.shape[0])) for v in vectors + [jnp.zeros((FF,), F32)]])
    outs = [jax.ShapeDtypeStruct((FF, 8), F32)] + [
        jax.ShapeDtypeStruct(shape, BF)
        for shape in (
            (INNER, D), (D, 2 * INNER), (2 * INNER, D), (INNER, D), (FF, D), (FF, D),
            (MAIN, HEAD_SIZE), (LEFT, INNER), (EXT, MAIN), (HEADS * EXT, LEFT),
        )
    ]
    wot = out_weight.T
    ins = [
        vec, projection.T, query_weight, key_weight, value_weight, wot, up_weight, down_weight,
    ]
    cols, wqt, wkv, wkvt, wo, upt, downt, pm, left_proj, tm, tl = call(
        prep_body, info, ins, [whole(v) for v in ins], outs, [whole(v) for v in outs], [], us=4,
    )

    k_out = jax.ShapeDtypeStruct((KROWS, MAIN), BF)
    k_acc = ((KROWS, MAIN), F32)
    key_scratch = [
        ((INNER, slots), BF), ((HEADS * EXT, slots), BF), ((HEADS * MAIN, slots), BF),
        ((LEFT, slots), BF), ((16, slots), F32),
    ]
    in_order = lambda j, info: (j, 0, 0)
    token_spec = pl.BlockSpec((1, D, slots), in_order)
    kernels = []
    for c in range(turns):
        ins = [x[c], alive, cols, wkvt, pm, left_proj]
        part = call(
            first_body(c), info, ins,
            [token_spec, pl.BlockSpec((1, turns, slots), in_order)] + [whole(v) for v in ins[2:]],
            k_out, whole(k_out), [k_acc] + key_scratch, grid=GROUP, us=13,
        )
        kernels.append(share_kernel(part, nt))

    def rotated(rows, first=0):
        return pl.BlockSpec(
            (1, rows, slots), lambda j, info: (lax.rem(info[0] + first + j, GROUP), 0, 0)
        )

    token_out = jax.ShapeDtypeStruct((1, D, slots), BF)
    wide_out = jax.ShapeDtypeStruct((GROUP, D, slots), F32)
    common = [
        ((HEADS * EXT, slots), BF), ((HEADS * MAIN, slots), BF), ((LEFT, slots), BF),
        ((16, slots), F32), ((HEADS * EXT, MAIN), BF), ((HEADS * EXT, LEFT), BF),
        ((HEADS * EXT, slots), F32),
    ]
    weights = [
        cols, wqt, query_weight, wot, wo, upt, up_weight, downt, down_weight,
        pm, left_proj, tm, tl,
    ]
    results, mixed_grads, query_grads, kernel_grads = [], [], [], []
    sums2 = []
    grads2 = [jax.ShapeDtypeStruct((GRAD2, 128), F32), jax.ShapeDtypeStruct((SMALL2, 128), F32)]
    for c in range(turns):
        fixed = kernels[c] + sums2 + weights
        first = 4 + len(kernels[c])
        got = call(
            second_body(c, len(kernels[c]), c == 0, 0), info, [x[c], dy[c], alive] + fixed,
            [rotated(D), rotated(D), rotated(turns)] + [whole(v) for v in fixed],
            [token_out] * GROUP + [wide_out, wide_out, k_out] + grads2,
            [whole(token_out)] * GROUP + [token_spec] * 2 + [whole(v) for v in [k_out] + grads2],
            [((KROWS, MAIN), BF), k_acc, ((INNER, slots), BF), ((INNER, slots), BF)]
            + common + [((INNER, slots), BF), ((16, slots), F32), ((FF, slots), BF), ((FF, slots), BF)],
            grid=GROUP, us=45,
            aliases={} if c == 0 else {first: GROUP + 3, first + 1: GROUP + 4},
        )
        results.append([exchange(got[j], j, nt) for j in range(GROUP)])
        gmix, gnq, kg, *sums2 = got[GROUP:]
        mixed_grads.append(gmix)
        query_grads.append(gnq)
        kernel_grads.append(share_kernel(kg, nt))

    sizes2 = [D, D, D, D, FF]
    reduce2 = Reduction(info, sums2[0], sums2[1], sizes2, nc, nt)

    weights = [cols, wkvt, wkv, pm, left_proj, tm, tl]
    grad_in = []
    sums3 = []
    grads3 = [jax.ShapeDtypeStruct((GRAD3, 128), F32), jax.ShapeDtypeStruct((2 * D, 128), F32)]
    steps = [
        lambda: [reduce2.packed] + results[0][1:],
        lambda: [reduce2.over_cells()],
        lambda: [reduce2.over_tok()] + results[1][1:],
        lambda: [reduce2.back_tok()] + grad_in[1:GROUP],
    ]
    parts = GROUP // PART
    for c in range(turns):
        for p in range(parts):
            number = c * parts + p
            waits = steps[number]() if number < len(steps) else []
            fixed = kernel_grads[c] + sums3 + weights
            first = 6 + len(kernel_grads[c])
            part_spec = pl.BlockSpec((1, D, slots), lambda j, info, p=p: (p * PART + j, 0, 0))
            got = call(
                third_body(c, len(kernel_grads[c]), number == 0, len(waits)), info,
                [x[c], dy[c], alive, mixed_grads[c], query_grads[c]] + fixed,
                [rotated(D, p * PART), rotated(D, p * PART), rotated(turns, p * PART), part_spec, part_spec]
                + [whole(v) for v in fixed],
                [token_out] * PART + grads3, [whole(token_out)] * PART + [whole(v) for v in grads3],
                [((KROWS, MAIN), BF), ((INNER, slots), BF), ((2 * INNER, slots), BF)] + common,
                grid=PART, us=15, waits=waits,
                aliases={} if number == 0 else {first: PART, first + 1: PART + 1},
            )
            grad_in += [exchange(got[j], p * PART + j, nt) for j in range(PART)]
            sums3 = list(got[PART:])
    reduce3 = Reduction(info, sums3[0], sums3[1], [D, D], nc, nt, waits=[reduce2.back_cells()])
    reduce3.over_cells()
    reduce3.over_tok()
    reduce3.back_tok()
    reduce3.back_cells()
    outs = [jax.ShapeDtypeStruct((D, width), F32) for width in (INNER, INNER, FF, FF)]
    pieces = [
        (0, INNER, False), (Q_BLOCKS * D, INNER, False), (2 * Q_BLOCKS * D, FF, False),
        ((2 * Q_BLOCKS + F_BLOCKS) * D, FF, False),
    ]
    (dwq, dwot, dup, ddown), (gain2, bias2, outb, downb, upb) = reduce2.results(pieces, outs)
    outs = [jax.ShapeDtypeStruct((D, INNER), F32)] * 2
    pieces = [(0, INNER, False), (Q_BLOCKS * D, INNER, False)]
    (dwk, dwv), (gain1, bias1) = reduce3.results(pieces, outs)
    return (
        place(info, sum(results, []), cells), place(info, grad_in, cells),
        gain1, bias1, dwq, dwk, dwv, dwot.T, outb, gain2, bias2, dup, upb, ddown, downb,
    )


def solution(mesh):
    rows = P("cells", None, "tok")
    placed = (rows, rows, P("cells"), P("cells", "tok")) + (P(),) * 14
    return jax.shard_map(
        shards,
        mesh=mesh,
        in_specs=placed,
        out_specs=(rows, rows) + (P(),) * 13,
        check_vma=False,
    )
```

```python
import functools
import math

import jax
import jax.numpy as jnp
from jax import lax
from jax.experimental import pallas as pl
from jax.experimental.pallas import tpu as pltpu
from jax.sharding import PartitionSpec as P

HEADS = 10
HEAD_SIZE = 64
FEATURES = 266
D = 200
INNER = HEADS * HEAD_SIZE
DX = 208
FF = 800
EPSILON = 1e-05

MAIN = 256
REST = FEATURES - MAIN
LEFT = 128
EXT = 80
SUM_ROW = INNER
LEFT_ROW = INNER + 16
KROWS = LEFT_ROW + 48

C0 = HEAD_SIZE ** (-0.25)
LOG2E = 1.0 / math.log(2.0)
RAW_SCALE = C0 * LOG2E
SQ_SCALE = 0.5 * C0 * C0 * LOG2E
SHIFT = -0.5 * math.log2(FEATURES)
FF_CHUNK = 160
Q_BLOCKS = INNER // 128
F_BLOCKS = -(-FF // 128)
WQ_AT, WO_AT, UP_AT, DOWN_AT = 0, Q_BLOCKS, 2 * Q_BLOCKS, 2 * Q_BLOCKS + F_BLOCKS
GRAD2 = (2 * Q_BLOCKS + 2 * F_BLOCKS) * DX
GRAD3 = 2 * Q_BLOCKS * DX
SMALL2 = 6
SMALL3 = 2

BF = jnp.bfloat16
F32 = jnp.float32
VMEM_LIMIT = 56 * 1024 * 1024
GROUP = 4
STEP = 2
UNROLL = 5


def dot(left, right):
    return jnp.dot(left, right, preferred_element_type=F32)


def dot_nt(left, right):
    return lax.dot_general(left, right, (((1,), (1,)), ((), ())), preferred_element_type=F32)


def dot_tn(left, right):
    return lax.dot_general(left, right, (((0,), (0,)), ((), ())), preferred_element_type=F32)


def iota(shape, axis):
    return lax.broadcasted_iota(jnp.int32, shape, axis)


def norm_cols(values, gain, bias):
    average = jnp.mean(values, axis=0, keepdims=True)
    centred = values - average
    inverse = lax.rsqrt(jnp.mean(centred * centred, axis=0, keepdims=True) + EPSILON)
    normed = centred * inverse
    return normed * gain + bias, normed, inverse


def norm_cols_back(grad_out, normed, inverse, gain):
    scaled = grad_out * gain
    return inverse * (
        scaled
        - jnp.mean(scaled, axis=0, keepdims=True)
        - normed * jnp.mean(scaled * normed, axis=0, keepdims=True)
    )


def lane_sums(values):
    total = values[:, :128]
    for start in range(128, values.shape[1], 128):
        total = total + values[:, start : start + 128]
    return total


def ext_rows(h):
    return pl.ds(pl.multiple_of(h * EXT, 16), EXT)


def val_rows(h):
    return pl.ds(pl.multiple_of(h * EXT, 16), HEAD_SIZE)


def main_rows(h):
    return pl.ds(pl.multiple_of(h * MAIN, MAIN), MAIN)


def head_rows(h):
    return pl.ds(pl.multiple_of(h * HEAD_SIZE, HEAD_SIZE), HEAD_SIZE)


def one_row(h):
    return pl.ds(h, 1)


def for_heads(step, unroll=HEADS):
    def turn(i, _):
        for k in range(unroll):
            step(i * unroll + k)
        return 0

    if unroll == HEADS:
        turn(0, 0)
    else:
        lax.fori_loop(0, HEADS // unroll, turn, 0)


G1, B1, G2, B2, OB, DB, UB = range(7)


def column(cols_ref, which, rows=D):
    return cols_ref[0:rows, which : which + 1]


def prep_body(
    info_ref, vec_ref, projt_ref, wq_ref, wk_ref, wv_ref, wot_ref, up_ref, down_ref,
    cols_ref, wqt_ref, wkv_ref, wkvt_ref, wo_ref, upt_ref, downt_ref,
    pm_ref, pl_ref, tm_ref, tl_ref,
):
    cols_ref[...] = vec_ref[...].T
    def padded(matrix):
        return jnp.concatenate([matrix.T, jnp.zeros((matrix.shape[1], DX - D), BF)], axis=1)

    wqt_ref[...] = padded(wq_ref[...])
    wkv_ref[:, :INNER] = wk_ref[...]
    wkv_ref[:, INNER:] = wv_ref[...]
    wkvt_ref[:INNER] = padded(wk_ref[...])
    wkvt_ref[INNER:] = padded(wv_ref[...])
    wo_ref[...] = wot_ref[...].T
    upt_ref[...] = padded(up_ref[...])
    downt_ref[...] = down_ref[...].T
    proj = projt_ref[...].T

    def one_hot(shape, mask):
        return jnp.where(mask, 1.0, 0.0).astype(BF)

    pm_ref[...] = proj[:MAIN]
    s = (16, FEATURES)
    rest = dot(one_hot(s, (iota(s, 0) + MAIN == iota(s, 1)) & (iota(s, 0) < REST)), proj).astype(BF)
    s = (HEAD_SIZE, INNER)
    wide = dot(rest, one_hot(s, iota(s, 0) == iota(s, 1) % HEAD_SIZE)).astype(BF)
    s = (LEFT, 16)
    tall = dot(one_hot(s, iota(s, 0) % REST == iota(s, 1)), wide)
    s = (LEFT, INNER)
    pl_ref[...] = jnp.where(iota(s, 0) // REST == iota(s, 1) // HEAD_SIZE, tall, 0.0).astype(BF)
    s = (EXT, HEAD_SIZE)
    pick = one_hot(s, iota(s, 0) == iota(s, 1))
    s = (EXT, MAIN)
    tm_ref[...] = jnp.where(iota(s, 0) == HEAD_SIZE, 1.0, dot_nt(pick, proj[:MAIN])).astype(BF)
    s = (EXT, 16)
    rest_ext = jnp.where(iota(s, 0) == HEAD_SIZE, 1.0, dot_nt(pick, rest)).astype(BF)
    s = (16, LEFT)
    spread = dot(rest_ext, one_hot(s, iota(s, 0) == iota(s, 1) % REST))
    s = (EXT, LEFT)
    for h in range(HEADS):
        tl_ref[ext_rows(h), :] = jnp.where(iota(s, 1) // REST == h, spread, 0.0).astype(BF)


def shifts_of(u_ref, s_ref):
    for h in range(HEADS):
        wide = u_ref[head_rows(h), :].astype(F32)
        s_ref[h : h + 1, :] = SHIFT - SQ_SCALE * jnp.sum(wide * wide, axis=0, keepdims=True)


def left_features(u_ref, phil_ref, s_ref, pl_ref):
    shape = (LEFT, u_ref.shape[1])
    owner = iota(shape, 0) // REST
    shifts = jnp.zeros(shape, F32)
    for h in range(HEADS):
        shifts = jnp.where(owner == h, s_ref[h : h + 1, :], shifts)
    phil_ref[...] = jnp.exp2(dot(pl_ref[...], u_ref[...]) * RAW_SCALE + shifts).astype(BF)


def main_features(h, u_ref, phi_ref, s_ref, pm_ref):
    raw = dot(pm_ref[...], u_ref[head_rows(h), :])
    phi_ref[main_rows(h), :] = jnp.exp2(raw * RAW_SCALE + s_ref[one_row(h), :]).astype(BF)


def add_head_kernel(h, acc_ref, ext_ref, phi_ref):
    total = dot_nt(ext_ref[ext_rows(h), :], phi_ref[main_rows(h), :])
    acc_ref[head_rows(h), :] += total[:HEAD_SIZE]
    acc_ref[one_row(SUM_ROW + h), :] += total[HEAD_SIZE : HEAD_SIZE + 1]


def add_left_kernel(acc_ref, ext_ref, phil_ref):
    every = dot_nt(ext_ref[...], phil_ref[...])
    owner = iota((EXT, LEFT), 1) // REST
    left = jnp.zeros((EXT, LEFT), F32)
    for h in range(HEADS):
        left = jnp.where(owner == h, every[h * EXT : (h + 1) * EXT], left)
    acc_ref[LEFT_ROW:KROWS, 0:LEFT] += left[:48]
    acc_ref[LEFT_ROW : LEFT_ROW + 32, LEFT:MAIN] += left[48:EXT]


def sum_kernels(in_refs, whole_ref):
    total = in_refs[0][...].astype(F32)
    for ref in in_refs[1:]:
        total = total + ref[...].astype(F32)
    whole_ref[...] = total.astype(BF)


def read_kernel(whole_ref, kt_ref, kl_ref):
    sums = whole_ref[SUM_ROW : SUM_ROW + 16, :].astype(F32)
    first = iota((16, MAIN), 0) == 0
    left = jnp.concatenate(
        [whole_ref[LEFT_ROW:KROWS, 0:LEFT], whole_ref[LEFT_ROW : LEFT_ROW + 32, LEFT:MAIN]], axis=0
    ).astype(F32)
    owner = iota((EXT, LEFT), 1) // REST
    for h in range(HEADS):
        kt_ref[val_rows(h), :] = whole_ref[head_rows(h), :]
        kt_ref[h * EXT + HEAD_SIZE : (h + 1) * EXT, :] = jnp.where(
            first, sums[h : h + 1, :], 0.0
        ).astype(BF)
        kl_ref[ext_rows(h), :] = jnp.where(owner == h, left, 0.0).astype(BF)


def left_grads(phil_ref, kl_ref, ext_ref, tl_ref, wide_ref):
    phil_ref[...] = (dot_tn(kl_ref[...], ext_ref[...]) * phil_ref[...].astype(F32)).astype(BF)
    wide_ref[...] = dot(tl_ref[...], phil_ref[...])


def main_grads(h, grad_ref, u_ref, phi_ref, kt_ref, ext_ref, tm_ref, wide_ref):
    weighted = (
        dot_tn(kt_ref[ext_rows(h), :], ext_ref[ext_rows(h), :]) * phi_ref[main_rows(h), :].astype(F32)
    ).astype(BF)
    through = dot(tm_ref[...], weighted) + wide_ref[ext_rows(h), :]
    grad_ref[head_rows(h), :] = (
        C0 * through[:HEAD_SIZE]
        - (C0 * C0) * u_ref[head_rows(h), :].astype(F32) * through[HEAD_SIZE : HEAD_SIZE + 1]
    ).astype(BF)


def with_ones(values):
    rows = iota((DX - D, values.shape[1]), 0)
    return jnp.concatenate([values, jnp.where(rows == 0, 1.0, 0.0)], axis=0).astype(BF)


def side_by_side(ref):
    blocks = [ref[(k,) + (0,) * (len(ref.shape) - 3)] for k in range(STEP)]
    return jnp.concatenate(blocks, axis=1)


def tokens_and_marks(x_ref):
    both = side_by_side(x_ref).astype(F32)
    return both[:D], both[D : D + 1]


def keys_values(normed_low, alive, wkvt_ref, k_ref, ext_ref):
    k_ref[...] = dot(wkvt_ref[:INNER, :], normed_low).astype(BF)
    values = dot(wkvt_ref[INNER:, :], normed_low)
    mark = jnp.where(iota((16, values.shape[1]), 0) == 0, alive, 0.0).astype(BF)
    for h in range(HEADS):
        ext_ref[val_rows(h), :] = (values[h * HEAD_SIZE : (h + 1) * HEAD_SIZE] * alive).astype(BF)
        ext_ref[h * EXT + HEAD_SIZE : (h + 1) * EXT, :] = mark


def key_sums(x, alive, cols_ref, wkvt_ref, pm_ref, pl_ref, acc_ref, k_ref, ext_ref, phi_ref, phil_ref, s_ref):
    normed, _, _ = norm_cols(x, column(cols_ref, G1), column(cols_ref, B1))
    keys_values(with_ones(normed), alive, wkvt_ref, k_ref, ext_ref)
    shifts_of(k_ref, s_ref)
    left_features(k_ref, phil_ref, s_ref, pl_ref)
    for_heads(lambda h: main_features(h, k_ref, phi_ref, s_ref, pm_ref))
    for_heads(lambda h: add_head_kernel(h, acc_ref, ext_ref, phi_ref))
    add_left_kernel(acc_ref, ext_ref, phil_ref)


def first_body(info_ref, x_ref, cols_ref, wkvt_ref, pm_ref, pl_ref, out_ref, acc_ref, *scratch):
    @pl.when(pl.program_id(0) == 0)
    def _():
        acc_ref[...] = jnp.zeros_like(acc_ref)

    tokens, alive = tokens_and_marks(x_ref)
    key_sums(tokens, alive, cols_ref, wkvt_ref, pm_ref, pl_ref, acc_ref, *scratch)

    @pl.when(pl.program_id(0) == pl.num_programs(0) - 1)
    def _():
        out_ref[...] = acc_ref[...].astype(BF)


def add_blocks(acc_ref, at, values):
    rows, width = values.shape
    for c in range(-(-width // 128)):
        take = min(128, width - c * 128)
        first = (at + c) * DX
        acc_ref[first : first + rows, 0:take] += values[:, c * 128 : c * 128 + take]


def add_small(small_ref, which, values):
    small_ref[which * D : (which + 1) * D, :] += lane_sums(values)


def add_first_norm(small_ref, which, acc_ref, weight_refs, cols_ref):
    with_normed = jnp.zeros((D, 128), F32)
    alone = jnp.zeros((D, 128), F32)
    block = 0
    for ref in weight_refs:
        for c in range(ref.shape[1] // 128):
            weight = ref[:, c * 128 : (c + 1) * 128].astype(F32)
            first = block * DX
            with_normed += weight * acc_ref[first : first + D, :]
            alone += weight * acc_ref[first + D : first + D + 1, :]
            block += 1
    gain = (with_normed - column(cols_ref, B1) * alone) / column(cols_ref, G1)
    small_ref[which * D : (which + 1) * D, :] = gain
    small_ref[(which + 1) * D : (which + 2) * D, :] = alone


def pack_sums(out_refs, acc_ref, small_ref, flat_ref, me, rows):
    blocks = acc_ref.shape[0] // DX
    base = blocks * rows
    for k in range(blocks):
        flat_ref[k * rows : (k + 1) * rows, :] = acc_ref[k * DX : k * DX + rows, :]
    flat_ref[base:, :] = jnp.zeros((flat_ref.shape[0] - base, 128), F32)
    high = small_ref[...].astype(BF)
    low = (small_ref[...] - high.astype(F32)).astype(BF)
    ones = jnp.ones((8, 128), BF)
    row = base
    for which in range(small_ref.shape[0] // D):
        part = slice(which * D, (which + 1) * D)
        line = dot_nt(ones, high[part]) + dot_nt(ones, low[part])
        flat_ref[row : row + 1, :] = line[0:1, 0:128]
        flat_ref[row + 1 : row + 2, 0 : D - 128] = line[0:1, 128:D]
        row += 2
    rows = out_refs[0].shape[0]
    for s, ref in enumerate(out_refs):
        owner = jnp.bitwise_xor(me, s)
        ref[...] = flat_ref[pl.ds(pl.multiple_of(owner * rows, 16), rows), :].astype(BF)


def put_side_by_side(out_ref, value):
    slots = value.shape[1] // STEP
    for k in range(STEP):
        out_ref[k] = value[:, k * slots : (k + 1) * slots]


def start_sums(start, ins, refs):
    for k, ref in enumerate(refs):
        ref[...] = jnp.zeros_like(ref) if start else ins[k][...]


def second_body(blocks, start, parts, waits):
    def body(info_ref, x_ref, dy_ref, *rest):
        k_refs, rest = rest[:blocks], rest[blocks:]
        ins = ()
        if not start:
            ins, rest = rest[:2], rest[2:]
        (
            cols_ref, wqt_ref, wq_ref, wot_ref, wo_ref, upt_ref, up_ref, downt_ref, down_ref,
            pm_ref, pl_ref, tm_ref, tl_ref,
        ), rest = rest[:13], rest[13 + waits :]
        (out_ref, gmix_ref, gnq_ref, kg_ref), rest = rest[:4], rest[4:]
        if parts:
            packed_refs, (flat_ref, ga_ref, sm_ref, *rest) = rest[:parts], rest[parts:]
        else:
            (ga_ref, sm_ref), rest = rest[:2], rest[2:]
        (
            whole_ref, acc_ref, q_ref, gq_ref, ext_ref, phi_ref, phil_ref, s_ref, kt_ref, kl_ref, wide_ref,
            att_ref, rec_ref, act_ref, gup_ref, n1_ref, n2_ref,
        ) = rest
        j = pl.program_id(0)

        @pl.when(j == 0)
        def _():
            start_sums(start, ins, (ga_ref, sm_ref))
            acc_ref[...] = jnp.zeros_like(acc_ref)
            sum_kernels(k_refs, whole_ref)
            read_kernel(whole_ref, kt_ref, kl_ref)

        tokens, alive = tokens_and_marks(x_ref)
        row_alive = alive > 0
        normed, _, _ = norm_cols(tokens, column(cols_ref, G1), column(cols_ref, B1))
        n1_ref[...] = with_ones(normed)
        q_ref[...] = dot(wqt_ref[...], n1_ref[...]).astype(BF)
        shifts_of(q_ref, s_ref)
        left_features(q_ref, phil_ref, s_ref, pl_ref)
        wide_ref[...] = dot(kl_ref[...], phil_ref[...])
        for_heads(lambda h: main_features(h, q_ref, phi_ref, s_ref, pm_ref), UNROLL)

        def attend(h):
            combined = dot(kt_ref[ext_rows(h), :], phi_ref[main_rows(h), :]) + wide_ref[ext_rows(h), :]
            inverse = 1.0 / jnp.where(row_alive, combined[HEAD_SIZE : HEAD_SIZE + 1], 1.0)
            rec_ref[one_row(h), :] = inverse
            quotient = combined[:HEAD_SIZE] * inverse
            wide_ref[val_rows(h), :] = quotient
            att_ref[head_rows(h), :] = quotient.astype(BF)

        for_heads(attend, UNROLL)
        mixed = tokens + dot(wot_ref[...], att_ref[...]) + column(cols_ref, OB)
        second, second_normed, second_inverse = norm_cols(
            mixed, column(cols_ref, G2), column(cols_ref, B2)
        )
        n2_ref[...] = with_ones(second)
        upstream_wide = jnp.where(row_alive, side_by_side(dy_ref).astype(F32), 0.0)
        upstream = upstream_wide.astype(BF)
        for c in range(FF // FF_CHUNK):
            rows = slice(c * FF_CHUNK, (c + 1) * FF_CHUNK)
            up = dot(upt_ref[rows, :], n2_ref[...]) + cols_ref[rows, UB : UB + 1]
            grad_act = dot(downt_ref[rows, :], upstream)
            half = 0.5 * (1.0 + lax.erf(up * 0.7071067811865476))
            act_ref[rows, :] = (up * half).astype(BF)
            slope = half + up * jnp.exp(-0.5 * up * up) * 0.3989422804014327
            grad_up = (grad_act * slope).astype(BF)
            gup_ref[rows, :] = grad_up
        result = mixed + dot(down_ref[...], act_ref[...]) + column(cols_ref, DB)
        put_side_by_side(out_ref, jnp.where(row_alive, result, tokens).astype(BF))

        add_blocks(ga_ref, DOWN_AT, dot_nt(upstream, act_ref[...]))
        add_blocks(ga_ref, UP_AT, dot_nt(n2_ref[...], gup_ref[...]))
        add_small(sm_ref, 3, upstream_wide)
        grad_second = dot(up_ref[...], gup_ref[...])
        add_small(sm_ref, 0, grad_second * second_normed)
        add_small(sm_ref, 1, grad_second)
        grad_mixed = upstream_wide + norm_cols_back(
            grad_second, second_normed, second_inverse, column(cols_ref, G2)
        )
        gmix_ref[0] = grad_mixed
        grad_branch = grad_mixed.astype(BF)
        add_small(sm_ref, 2, grad_branch.astype(F32))
        add_blocks(ga_ref, WO_AT, dot_nt(grad_branch, att_ref[...]))
        pad_row = iota((16, alive.shape[1]), 0) == 0
        grad_att = dot(wo_ref[...], grad_branch)
        for h in range(HEADS):
            grad_head = grad_att[h * HEAD_SIZE : (h + 1) * HEAD_SIZE]
            inverse = rec_ref[h : h + 1, :]
            ext_ref[val_rows(h), :] = (grad_head * inverse).astype(BF)
            grad_sum = -inverse * jnp.sum(grad_head * wide_ref[val_rows(h), :], axis=0, keepdims=True)
            ext_ref[h * EXT + HEAD_SIZE : (h + 1) * EXT, :] = jnp.where(pad_row, grad_sum, 0.0).astype(BF)
        add_left_kernel(acc_ref, ext_ref, phil_ref)
        left_grads(phil_ref, kl_ref, ext_ref, tl_ref, wide_ref)
        for_heads(lambda h: add_head_kernel(h, acc_ref, ext_ref, phi_ref), UNROLL)
        for_heads(
            lambda h: main_grads(h, gq_ref, q_ref, phi_ref, kt_ref, ext_ref, tm_ref, wide_ref), UNROLL
        )
        add_blocks(ga_ref, WQ_AT, dot_nt(n1_ref[...], gq_ref[...]))
        gnq_ref[0] = dot(wq_ref[...], gq_ref[...])

        @pl.when(j == pl.num_programs(0) - 1)
        def _():
            kg_ref[...] = acc_ref[...].astype(BF)
            if parts:
                add_first_norm(sm_ref, 4, ga_ref, [wq_ref], cols_ref)
                pack_sums(packed_refs, ga_ref, sm_ref, flat_ref, info_ref[0], DX)

    return body


def third_body(blocks, start, parts, waits):
    def body(info_ref, x_ref, *rest):
        k_refs, rest = rest[:blocks], rest[blocks:]
        ins = ()
        if not start:
            ins, rest = rest[:1], rest[1:]
        (cols_ref, wkvt_ref, wkv_ref, pm_ref, pl_ref, tm_ref, tl_ref), rest = rest[:7], rest[7 + waits :]
        gout_ref, rest = rest[0], rest[1:]
        if parts:
            packed_refs, (flat_ref, ga_ref, sm_ref, *rest) = rest[:parts], rest[parts:]
        else:
            ga_ref, rest = rest[0], rest[1:]
        (
            whole_ref, k_ref, ext_ref, phi_ref, phil_ref, s_ref, kt_ref, kl_ref, wide_ref, n1_ref,
        ) = rest
        gkv_ref = gout_ref.at[0]

        @pl.when(pl.program_id(0) == 0)
        def _():
            start_sums(start, ins, (ga_ref,))
            sum_kernels(k_refs, whole_ref)
            read_kernel(whole_ref, kt_ref, kl_ref)

        tokens, alive = tokens_and_marks(x_ref)
        normed, _, _ = norm_cols(tokens, column(cols_ref, G1), column(cols_ref, B1))
        n1_ref[...] = with_ones(normed)
        keys_values(n1_ref[...], alive, wkvt_ref, k_ref, ext_ref)
        shifts_of(k_ref, s_ref)
        left_features(k_ref, phil_ref, s_ref, pl_ref)
        wide_ref[...] = dot(kl_ref[...], phil_ref[...])
        for_heads(lambda h: main_features(h, k_ref, phi_ref, s_ref, pm_ref))

        def value_grads(h):
            grad = dot(kt_ref[val_rows(h), :], phi_ref[main_rows(h), :]) + wide_ref[val_rows(h), :]
            gkv_ref[head_rows(HEADS + h), :] = (grad * alive).astype(BF)

        for_heads(value_grads)
        left_grads(phil_ref, kl_ref, ext_ref, tl_ref, wide_ref)
        for_heads(lambda h: main_grads(h, gkv_ref, k_ref, phi_ref, kt_ref, ext_ref, tm_ref, wide_ref))
        add_blocks(ga_ref, 0, dot_nt(n1_ref[...], gkv_ref[...]))

        if parts:

            @pl.when(pl.program_id(0) == pl.num_programs(0) - 1)
            def _():
                add_first_norm(sm_ref, 0, ga_ref, [wkv_ref], cols_ref)
                pack_sums(packed_refs, ga_ref, sm_ref, flat_ref, info_ref[0], D)

    return body


def total_body(count, info_ref, *rest):
    if count == 1:
        blocks = [rest[0][k] for k in range(rest[0].shape[0])]
    else:
        blocks = [ref[...] for ref in rest[:count]]
    total = blocks[0].astype(F32)
    for block in blocks[1:]:
        total = total + block.astype(F32)
    out_ref = rest[-1]
    total = total.astype(BF)
    if len(out_ref.shape) == 2:
        out_ref[...] = total
    else:
        for k in range(out_ref.shape[0]):
            out_ref[k] = total


def last_body(info_ref, x_ref, dy_ref, gmix_ref, gnq_ref, gkv_ref, cols_ref, wkv_ref, *rest):
    out_refs = rest[-GROUP:]
    tokens, alive = tokens_and_marks(x_ref)
    _, normed, inverse = norm_cols(tokens, column(cols_ref, G1), column(cols_ref, B1))
    grad_normed = gnq_ref[0] + dot(wkv_ref[...], gkv_ref[0])
    grad_in = gmix_ref[0] + norm_cols_back(grad_normed, normed, inverse, column(cols_ref, G1))
    grad_in = jnp.where(alive > 0, grad_in, side_by_side(dy_ref).astype(F32))
    slots = grad_in.shape[1] // STEP
    odd = lax.rem(info_ref[1], 2) == 1
    first, second = grad_in[:, :slots], grad_in[:, slots:]
    first, second = jnp.where(odd, second, first).astype(BF), jnp.where(odd, first, second).astype(BF)
    for k in range(GROUP // STEP):

        @pl.when(pl.program_id(0) == k)
        def _():
            out_refs[STEP * k][0] = first
            out_refs[STEP * k + 1][0] = second


def place_body(info_ref, *refs):
    for k, ref in enumerate(refs[:-1]):

        @pl.when(pl.program_id(0) == k)
        def _():
            refs[-1][...] = ref[...]


def unpack_body(count, block, pieces, sums, smalls, extras):
    def body(info_ref, *rest):
        in_refs, whole_ref = rest[:count], rest[-1]
        out_refs = list(rest[-1 - len(pieces) - len(sums) - len(smalls) : -1])
        rows = in_refs[0].shape[0]
        for s, ref in enumerate(in_refs):
            owner = jnp.bitwise_xor(info_ref[0], s)
            whole_ref[pl.ds(pl.multiple_of(owner * rows, 16), rows), :] = ref[...].astype(F32)
        for at, width in pieces:
            ref = out_refs.pop(0)
            for c in range(-(-width // 128)):
                take = min(128, width - c * 128)
                first = (at + c) * block
                ref[:, c * 128 : c * 128 + take] = whole_ref[first : first + D, 0:take]
        for at, width in sums:
            ref = out_refs.pop(0)
            for c in range(-(-width // 128)):
                take = min(128, width - c * 128)
                first = (at + c) * block + D
                ref[:, c * 128 : c * 128 + take] = whole_ref[first : first + 1, 0:take]
        for k, (row, width) in enumerate(smalls):
            ref = out_refs.pop(0)
            line = jnp.concatenate(
                [whole_ref[row : row + 1, :], whole_ref[row + 1 : row + 2, 0 : width - 128]], axis=1
            )
            ref[...] = line + rest[count + k][...] if k < extras else line

    return body


def whole(array):
    zeros = (0,) * len(array.shape)
    return pl.BlockSpec(array.shape, lambda i, info: zeros)


def call(body, info, ins, in_specs, outs, out_specs, scratch, grid=1, us=1, aliases=None, waits=()):
    return pl.pallas_call(
        body,
        grid_spec=pltpu.PrefetchScalarGridSpec(
            num_scalar_prefetch=1,
            grid=(grid,),
            in_specs=in_specs + [pl.BlockSpec(memory_space=pl.ANY)] * len(waits),
            out_specs=out_specs,
            scratch_shapes=[pltpu.VMEM(shape, kind) for shape, kind in scratch],
        ),
        out_shape=outs,
        input_output_aliases=aliases or {},
        compiler_params=pltpu.CompilerParams(
            dimension_semantics=("arbitrary",), vmem_limit_bytes=VMEM_LIMIT
        ),
        cost_estimate=pl.CostEstimate(
            flops=int(us * 1.15e9), bytes_accessed=1000000, transcendentals=0
        ),
    )(info, *ins, *waits)


def swap(value, axis, groups=None):
    return lax.all_to_all(value, axis, 0, 0, axis_index_groups=groups, tiled=True)


def share_kernel(part, nt):
    others = nt // GROUP
    got = [part]
    for s in range(1, others):
        got.append(lax.ppermute(part, "tok", [(i, (i + s * GROUP) % nt) for i in range(nt)]))
    return got


class Reduction:
    def __init__(self, packed, info, rows, nc, nt):
        self.packed, self.info, self.rows, self.nc, self.nt = packed, info, rows, nc, nt
        self.quarter, self.share = rows // nc, rows // (nc * nt)

    def cross(self, values):
        return [values[0]] + [
            lax.ppermute(values[s], "cells", [(i, i ^ s) for i in range(self.nc)])
            for s in range(1, self.nc)
        ]

    def total(self, parts, shape, waits):
        out = jax.ShapeDtypeStruct(shape, BF)
        return call(
            functools.partial(total_body, len(parts)), self.info, parts, [whole(v) for v in parts],
            out, whole(out), [], waits=waits,
        )

    def over_cells(self):
        self.one = self.cross(self.packed)

    def over_tok(self, waits):
        mine = self.total(self.one, (self.quarter, 128), waits)
        self.two = swap(mine.reshape(self.nt, self.share, 128), "tok")
        return mine

    def back_tok(self, waits):
        mine = self.total([self.two], (self.nt, self.share, 128), waits)
        self.three = swap(mine, "tok")
        return mine

    def back_cells(self):
        self.four = self.cross([self.three.reshape(self.quarter, 128)] * self.nc)

    def results(self, block, pieces, sums, smalls, waits=(), extras=()):
        outs = [jax.ShapeDtypeStruct((D, width), F32) for _, width in pieces]
        outs += [jax.ShapeDtypeStruct((1, width), F32) for _, width in sums + smalls]
        outs = call(
            unpack_body(self.nc, block, pieces, sums, smalls, len(extras)), self.info,
            self.four + list(extras), [whole(v) for v in self.four + list(extras)], outs, [whole(v) for v in outs], [((self.rows, 128), F32)],
            us=3, waits=waits,
        )
        return outs[: len(pieces)], outs[len(pieces) :]


def padded_rows(need, nc, nt):
    unit = nc * nt * 16
    return -(-need // unit) * unit


def shards(
    tokens, cotangent, gene_count, expressed, projection, first_gain, first_bias, query_weight,
    key_weight, value_weight, out_weight, out_bias, second_gain, second_bias, up_weight, up_bias,
    down_weight, down_bias,
):
    cells, _, slots = tokens.shape
    turns = cells // GROUP
    steps, lanes = GROUP // STEP, STEP * slots
    nt, nc = lax.axis_size("tok"), lax.axis_size("cells")
    position = lax.axis_index("tok")
    groups = [[g * GROUP + i for i in range(GROUP)] for g in range(nt // GROUP)]
    info = jnp.stack([lax.axis_index("cells"), position % GROUP]).astype(jnp.int32)

    slot_index = position * slots + lax.broadcasted_iota(jnp.int32, (cells, slots), 1)
    alive = ((slot_index < gene_count[:, None]) & (expressed > 0)).astype(BF)
    marks = jnp.pad(alive[:, None, :], ((0, 0), (0, DX - D - 1), (0, 0)))

    def turn_of(array, c):
        return array[c * GROUP : (c + 1) * GROUP]

    x = [
        swap(jnp.concatenate([turn_of(tokens, c), turn_of(marks, c)], axis=1), "tok", groups)
        for c in range(turns)
    ]

    vectors = [first_gain, first_bias, second_gain, second_bias, out_bias, down_bias, up_bias]
    vec = jnp.stack([jnp.pad(v, (0, FF - v.shape[0])) for v in vectors + [jnp.zeros((FF,), F32)]])
    outs = [jax.ShapeDtypeStruct((FF, 8), F32)] + [
        jax.ShapeDtypeStruct(shape, BF)
        for shape in (
            (INNER, DX), (D, 2 * INNER), (2 * INNER, DX), (INNER, D), (FF, DX), (FF, D),
            (MAIN, HEAD_SIZE), (LEFT, INNER), (EXT, MAIN), (HEADS * EXT, LEFT),
        )
    ]
    wot = out_weight.T
    ins = [
        vec, projection.T, query_weight, key_weight, value_weight, wot, up_weight, down_weight,
    ]
    cols, wqt, wkv, wkvt, wo, upt, downt, pm, left_proj, tm, tl = call(
        prep_body, info, ins, [whole(v) for v in ins], outs, [whole(v) for v in outs], [], us=4,
    )

    x_spec = pl.BlockSpec((STEP, DX, slots), lambda j, info: (j, 0, 0))

    def step_spec(rows):
        return pl.BlockSpec((1, rows, lanes), lambda j, info: (j, 0, 0))

    k_out = jax.ShapeDtypeStruct((KROWS, MAIN), BF)
    k_acc = ((KROWS, MAIN), F32)
    key_scratch = [
        ((INNER, lanes), BF), ((HEADS * EXT, lanes), BF), ((HEADS * MAIN, lanes), BF),
        ((LEFT, lanes), BF), ((16, lanes), F32),
    ]
    kernels, dy = [], []
    for c in range(turns):
        ins = [x[c], cols, wkvt, pm, left_proj]
        part = call(
            first_body, info, ins, [x_spec] + [whole(v) for v in ins[1:]],
            k_out, whole(k_out), [k_acc] + key_scratch, grid=steps, us=12,
        )
        mine, part = lax.optimization_barrier((turn_of(cotangent, c), part))
        kernels.append(share_kernel(part, nt))
        dy.append(swap(mine, "tok", groups))

    token_out = jax.ShapeDtypeStruct((GROUP, D, slots), BF)
    token_spec = pl.BlockSpec((STEP, D, slots), lambda j, info: (j, 0, 0))
    wide_out = jax.ShapeDtypeStruct((steps, D, lanes), F32)
    common = [
        ((HEADS * EXT, lanes), BF), ((HEADS * MAIN, lanes), BF), ((LEFT, lanes), BF),
        ((16, lanes), F32), ((HEADS * EXT, MAIN), BF), ((HEADS * EXT, LEFT), BF),
        ((HEADS * EXT, lanes), F32),
    ]
    weights = [
        cols, wqt, query_weight, wot, wo, upt, up_weight, downt, down_weight,
        pm, left_proj, tm, tl,
    ]
    rows2 = padded_rows(GRAD2 + 2 * SMALL2, nc, nt)
    sums = [((GRAD2, 128), F32), ((SMALL2 * D, 128), F32)]
    mixed_grads, query_grads, kernel_grads = [], [], []
    results, sums2 = [], []
    for c in range(turns):
        start, last = c == 0, c == turns - 1
        fixed = kernels[c] + sums2 + weights
        if last:
            sum_outs = [jax.ShapeDtypeStruct((rows2 // nc, 128), BF)] * nc
            sum_scratch = [((rows2, 128), F32)] + sums
        else:
            sum_outs = [jax.ShapeDtypeStruct(shape, kind) for shape, kind in sums]
            sum_scratch = []
        out, gmix, gnq, kg, *sums2 = call(
            second_body(len(kernels[c]), start, nc if last else 0, 0), info, [x[c], dy[c]] + fixed,
            [x_spec, token_spec] + [whole(v) for v in fixed],
            [token_out, wide_out, wide_out, k_out] + sum_outs,
            [token_spec, step_spec(D), step_spec(D)] + [whole(v) for v in [k_out] + sum_outs],
            sum_scratch + [((KROWS, MAIN), BF), k_acc, ((INNER, lanes), BF), ((INNER, lanes), BF)]
            + common
            + [
                ((INNER, lanes), BF), ((16, lanes), F32), ((FF, lanes), BF), ((FF, lanes), BF),
                ((DX, lanes), BF), ((DX, lanes), BF),
            ],
            grid=steps, us=40,
        )
        results.append(swap(out, "tok", groups))
        mixed_grads.append(gmix)
        query_grads.append(gnq)
        kernel_grads.append(share_kernel(kg, nt))
    reduce2 = Reduction(sums2, info, rows2, nc, nt)
    reduce2.over_cells()

    rows3 = padded_rows(2 * Q_BLOCKS * D + 2 * SMALL3, nc, nt)
    weights = [cols, wkvt, wkv, pm, left_proj, tm, tl]
    joined_grads, sums3 = [], []
    waits = [sums2[0], results[0]]
    for c in range(turns):
        start, last = c == 0, c == turns - 1
        fixed = kernel_grads[c] + sums3 + weights
        if last:
            sum_outs = [jax.ShapeDtypeStruct((rows3 // nc, 128), BF)] * nc
            sum_scratch = [((rows3, 128), F32), ((GRAD3, 128), F32), ((SMALL3 * D, 128), F32)]
        else:
            sum_outs = [jax.ShapeDtypeStruct((GRAD3, 128), F32)]
            sum_scratch = []
        joined = jax.ShapeDtypeStruct((steps, 2 * INNER, lanes), BF)
        got, *sums3 = call(
            third_body(len(kernel_grads[c]), start, nc if last else 0, len(waits)), info,
            [x[c]] + fixed, [x_spec] + [whole(v) for v in fixed],
            [joined] + sum_outs, [step_spec(2 * INNER)] + [whole(v) for v in sum_outs],
            sum_scratch + [((KROWS, MAIN), BF), ((INNER, lanes), BF)] + common + [((DX, lanes), BF)],
            grid=steps, us=22, waits=waits,
        )
        joined_grads.append(got)
        if start:
            waits = [reduce2.over_tok([got, results[-1]] + kernel_grads[-1][1:])]
    reduce3 = Reduction(sums3, info, rows3, nc, nt)
    reduce3.over_cells()
    waits = [sums3[0], results[-1], reduce2.back_tok([sums3[0]])]
    reduce2.back_cells()
    one_out = jax.ShapeDtypeStruct((1, D, slots), BF)
    grads = []
    for c in range(turns):
        ins = [x[c], dy[c], mixed_grads[c], query_grads[c], joined_grads[c], cols, wkv]

        def pair(rows, blocks=STEP, columns=slots):
            return pl.BlockSpec(
                (blocks, rows, columns), lambda j, info: (jnp.bitwise_xor(info[1] // STEP, j), 0, 0)
            )

        specs = [pair(DX), pair(D)] + [pair(rows, 1, lanes) for rows in (D, D, 2 * INNER)]
        out = call(
            last_body, info, ins, specs + [whole(cols), whole(wkv)], [one_out] * GROUP,
            [whole(one_out)] * GROUP, [], grid=steps, us=6, waits=waits,
        )
        grads += [out[0]] + [
            lax.ppermute(out[s], "tok", [(i, i - i % GROUP + (i % GROUP ^ s)) for i in range(nt)])
            for s in range(1, GROUP)
        ]
        if c == 0:
            waits = [reduce3.over_tok([out[0]]), reduce2.three]
    mine = reduce3.back_tok([out[0]])
    reduce3.back_cells()

    def cell(i, info):
        return i // GROUP * GROUP + jnp.bitwise_xor(info[1], lax.rem(i, GROUP)), 0, 0

    result = jnp.concatenate(results, axis=0)
    grad_in = call(
        place_body, info, grads, [whole(v) for v in grads],
        jax.ShapeDtypeStruct((cells, D, slots), BF), pl.BlockSpec((1, D, slots), cell), [], grid=cells, us=3,
    )
    (dwq, dwot, dup, ddown), (upb, gain2, bias2, outb, downb, gain1q, bias1q) = reduce2.results(
        DX, [(WQ_AT, INNER), (WO_AT, INNER), (UP_AT, FF), (DOWN_AT, FF)], [(UP_AT, FF)],
        [(GRAD2 + 2 * k, D) for k in range(SMALL2)], waits=[mine],
    )
    (dwk, dwv), (gain1, bias1) = reduce3.results(
        D, [(0, INNER), (Q_BLOCKS, INNER)], [], [(2 * Q_BLOCKS * D + 2 * k, D) for k in range(SMALL3)],
        extras=[gain1q, bias1q], waits=[grad_in],
    )
    return (
        result, grad_in, gain1[0], bias1[0], dwq, dwk, dwv, dwot.T, outb[0],
        gain2[0], bias2[0], dup, upb[0], ddown, downb[0],
    )


def solution(mesh):
    rows = P("cells", None, "tok")
    placed = (rows, rows, P("cells"), P("cells", "tok")) + (P(),) * 14
    return jax.shard_map(
        shards,
        mesh=mesh,
        in_specs=placed,
        out_specs=(rows, rows) + (P(),) * 13,
        check_vma=False,
    )
```

```python
import math

import jax
import jax.numpy as jnp
from jax import lax
from jax.experimental import pallas as pl
from jax.experimental.pallas import tpu as pltpu
from jax.sharding import PartitionSpec as P

HEADS = 10
HEAD_SIZE = 64
FEATURES = 266
D = 200
INNER = HEADS * HEAD_SIZE
DX = 208
FF = 800
EPSILON = 1e-05

MAIN = 256
REST = FEATURES - MAIN
LEFT = 128
EXT = 80
SUM_ROW = INNER
LEFT_ROW = INNER + 16
KROWS = LEFT_ROW + 48

C0 = HEAD_SIZE ** (-0.25)
LOG2E = 1.0 / math.log(2.0)
RAW_SCALE = C0 * LOG2E
SQ_SCALE = 0.5 * C0 * C0 * LOG2E
SHIFT = -0.5 * math.log2(FEATURES)
FF_CHUNK = 160
Q_BLOCKS = INNER // 128
F_BLOCKS = -(-FF // 128)
WQ_AT, WO_AT, UP_AT, DOWN_AT = 0, Q_BLOCKS, 2 * Q_BLOCKS, 2 * Q_BLOCKS + F_BLOCKS
GRAD2 = (2 * Q_BLOCKS + 2 * F_BLOCKS) * DX
GRAD3 = 2 * Q_BLOCKS * DX
SMALL2 = 6
SMALL3 = 2

BF = jnp.bfloat16
F32 = jnp.float32
VMEM_LIMIT = 56 * 1024 * 1024
GROUP = 4
STEP = 2
UNROLL = 5


def dot(left, right):
    return jnp.dot(left, right, preferred_element_type=F32)


def dot_nt(left, right):
    return lax.dot_general(left, right, (((1,), (1,)), ((), ())), preferred_element_type=F32)


def dot_tn(left, right):
    return lax.dot_general(left, right, (((0,), (0,)), ((), ())), preferred_element_type=F32)


def iota(shape, axis):
    return lax.broadcasted_iota(jnp.int32, shape, axis)


def norm_cols(values, gain, bias):
    average = jnp.mean(values, axis=0, keepdims=True)
    centred = values - average
    inverse = lax.rsqrt(jnp.mean(centred * centred, axis=0, keepdims=True) + EPSILON)
    normed = centred * inverse
    return normed * gain + bias, normed, inverse


def norm_cols_back(grad_out, normed, inverse, gain):
    scaled = grad_out * gain
    return inverse * (
        scaled
        - jnp.mean(scaled, axis=0, keepdims=True)
        - normed * jnp.mean(scaled * normed, axis=0, keepdims=True)
    )


def lane_sums(values):
    total = values[:, :128]
    for start in range(128, values.shape[1], 128):
        total = total + values[:, start : start + 128]
    return total


def ext_rows(h):
    return pl.ds(pl.multiple_of(h * EXT, 16), EXT)


def val_rows(h):
    return pl.ds(pl.multiple_of(h * EXT, 16), HEAD_SIZE)


def main_rows(h):
    return pl.ds(pl.multiple_of(h * MAIN, MAIN), MAIN)


def head_rows(h):
    return pl.ds(pl.multiple_of(h * HEAD_SIZE, HEAD_SIZE), HEAD_SIZE)


def one_row(h):
    return pl.ds(h, 1)


def for_heads(step, unroll=HEADS):
    def turn(i, _):
        for k in range(unroll):
            step(i * unroll + k)
        return 0

    if unroll == HEADS:
        turn(0, 0)
    else:
        lax.fori_loop(0, HEADS // unroll, turn, 0)


G1, B1, G2, B2, OB, DB, UB = range(7)


def column(cols_ref, which, rows=D):
    return cols_ref[0:rows, which : which + 1]


def prep_body(
    info_ref, vec_ref, projt_ref, wq_ref, wk_ref, wv_ref, wot_ref, up_ref, down_ref,
    cols_ref, wqt_ref, wkv_ref, wkvt_ref, wo_ref, upt_ref, downt_ref,
    pm_ref, pl_ref, tm_ref, tl_ref,
):
    cols_ref[...] = vec_ref[...].T
    def padded(matrix):
        return jnp.concatenate([matrix.T, jnp.zeros((matrix.shape[1], DX - D), BF)], axis=1)

    wqt_ref[...] = padded(wq_ref[...])
    wkv_ref[:, :INNER] = wk_ref[...]
    wkv_ref[:, INNER:] = wv_ref[...]
    wkvt_ref[:INNER] = padded(wk_ref[...])
    wkvt_ref[INNER:] = padded(wv_ref[...])
    wo_ref[...] = wot_ref[...].T
    upt_ref[...] = padded(up_ref[...])
    downt_ref[...] = down_ref[...].T
    proj = projt_ref[...].T

    def one_hot(shape, mask):
        return jnp.where(mask, 1.0, 0.0).astype(BF)

    pm_ref[...] = proj[:MAIN]
    s = (16, FEATURES)
    rest = dot(one_hot(s, (iota(s, 0) + MAIN == iota(s, 1)) & (iota(s, 0) < REST)), proj).astype(BF)
    s = (HEAD_SIZE, INNER)
    wide = dot(rest, one_hot(s, iota(s, 0) == iota(s, 1) % HEAD_SIZE)).astype(BF)
    s = (LEFT, 16)
    tall = dot(one_hot(s, iota(s, 0) % REST == iota(s, 1)), wide)
    s = (LEFT, INNER)
    pl_ref[...] = jnp.where(iota(s, 0) // REST == iota(s, 1) // HEAD_SIZE, tall, 0.0).astype(BF)
    s = (EXT, HEAD_SIZE)
    pick = one_hot(s, iota(s, 0) == iota(s, 1))
    s = (EXT, MAIN)
    tm_ref[...] = jnp.where(iota(s, 0) == HEAD_SIZE, 1.0, dot_nt(pick, proj[:MAIN])).astype(BF)
    s = (EXT, 16)
    rest_ext = jnp.where(iota(s, 0) == HEAD_SIZE, 1.0, dot_nt(pick, rest)).astype(BF)
    s = (16, LEFT)
    spread = dot(rest_ext, one_hot(s, iota(s, 0) == iota(s, 1) % REST))
    s = (EXT, LEFT)
    for h in range(HEADS):
        tl_ref[ext_rows(h), :] = jnp.where(iota(s, 1) // REST == h, spread, 0.0).astype(BF)


def shifts_of(u_ref, s_ref):
    for h in range(HEADS):
        wide = u_ref[head_rows(h), :].astype(F32)
        s_ref[h : h + 1, :] = SHIFT - SQ_SCALE * jnp.sum(wide * wide, axis=0, keepdims=True)


def left_features(u_ref, phil_ref, s_ref, pl_ref):
    shape = (LEFT, u_ref.shape[1])
    owner = iota(shape, 0) // REST
    shifts = jnp.zeros(shape, F32)
    for h in range(HEADS):
        shifts = jnp.where(owner == h, s_ref[h : h + 1, :], shifts)
    phil_ref[...] = jnp.exp2(dot(pl_ref[...], u_ref[...]) * RAW_SCALE + shifts).astype(BF)


def main_features(h, u_ref, phi_ref, s_ref, pm_ref):
    raw = dot(pm_ref[...], u_ref[head_rows(h), :])
    phi_ref[main_rows(h), :] = jnp.exp2(raw * RAW_SCALE + s_ref[one_row(h), :]).astype(BF)


def add_head_kernel(h, acc_ref, ext_ref, phi_ref):
    total = dot_nt(ext_ref[ext_rows(h), :], phi_ref[main_rows(h), :])
    acc_ref[head_rows(h), :] += total[:HEAD_SIZE]
    acc_ref[one_row(SUM_ROW + h), :] += total[HEAD_SIZE : HEAD_SIZE + 1]


def add_left_kernel(acc_ref, ext_ref, phil_ref):
    every = dot_nt(ext_ref[...], phil_ref[...])
    owner = iota((EXT, LEFT), 1) // REST
    left = jnp.zeros((EXT, LEFT), F32)
    for h in range(HEADS):
        left = jnp.where(owner == h, every[h * EXT : (h + 1) * EXT], left)
    acc_ref[LEFT_ROW:KROWS, 0:LEFT] += left[:48]
    acc_ref[LEFT_ROW : LEFT_ROW + 32, LEFT:MAIN] += left[48:EXT]


def sum_kernels(in_refs, whole_ref):
    total = in_refs[0][...].astype(F32)
    for ref in in_refs[1:]:
        total = total + ref[...].astype(F32)
    whole_ref[...] = total.astype(BF)


def read_kernel(whole_ref, kt_ref, kl_ref):
    sums = whole_ref[SUM_ROW : SUM_ROW + 16, :].astype(F32)
    first = iota((16, MAIN), 0) == 0
    left = jnp.concatenate(
        [whole_ref[LEFT_ROW:KROWS, 0:LEFT], whole_ref[LEFT_ROW : LEFT_ROW + 32, LEFT:MAIN]], axis=0
    ).astype(F32)
    owner = iota((EXT, LEFT), 1) // REST
    for h in range(HEADS):
        kt_ref[val_rows(h), :] = whole_ref[head_rows(h), :]
        kt_ref[h * EXT + HEAD_SIZE : (h + 1) * EXT, :] = jnp.where(
            first, sums[h : h + 1, :], 0.0
        ).astype(BF)
        kl_ref[ext_rows(h), :] = jnp.where(owner == h, left, 0.0).astype(BF)


def left_grads(phil_ref, kl_ref, ext_ref, tl_ref, wide_ref):
    phil_ref[...] = (dot_tn(kl_ref[...], ext_ref[...]) * phil_ref[...].astype(F32)).astype(BF)
    wide_ref[...] = dot(tl_ref[...], phil_ref[...])


def weigh(h, phi_ref, kt_ref, ext_ref):
    grad = dot_tn(kt_ref[ext_rows(h), :], ext_ref[ext_rows(h), :])
    phi_ref[main_rows(h), :] = (grad * phi_ref[main_rows(h), :].astype(F32)).astype(BF)


def main_grads(h, grad_ref, u_ref, phi_ref, tm_ref, wide_ref):
    through = dot(tm_ref[...], phi_ref[main_rows(h), :]) + wide_ref[ext_rows(h), :]
    grad_ref[head_rows(h), :] = (
        C0 * through[:HEAD_SIZE]
        - (C0 * C0) * u_ref[head_rows(h), :].astype(F32) * through[HEAD_SIZE : HEAD_SIZE + 1]
    ).astype(BF)


def with_ones(values):
    rows = iota((DX - D, values.shape[1]), 0)
    return jnp.concatenate([values, jnp.where(rows == 0, 1.0, 0.0)], axis=0).astype(BF)


def side_by_side(ref):
    blocks = [ref[(k,) + (0,) * (len(ref.shape) - 3)] for k in range(STEP)]
    return jnp.concatenate(blocks, axis=1)


def tokens_and_marks(x_ref):
    both = side_by_side(x_ref).astype(F32)
    return both[:D], both[D : D + 1]


def keys_values(normed_low, alive, wkvt_ref, k_ref, ext_ref):
    k_ref[...] = dot(wkvt_ref[:INNER, :], normed_low).astype(BF)
    values = dot(wkvt_ref[INNER:, :], normed_low)
    mark = jnp.where(iota((16, values.shape[1]), 0) == 0, alive, 0.0).astype(BF)
    for h in range(HEADS):
        ext_ref[val_rows(h), :] = (values[h * HEAD_SIZE : (h + 1) * HEAD_SIZE] * alive).astype(BF)
        ext_ref[h * EXT + HEAD_SIZE : (h + 1) * EXT, :] = mark


def key_sums(x, alive, cols_ref, wkvt_ref, pm_ref, pl_ref, acc_ref, k_ref, ext_ref, phi_ref, phil_ref, s_ref):
    normed, _, _ = norm_cols(x, column(cols_ref, G1), column(cols_ref, B1))
    keys_values(with_ones(normed), alive, wkvt_ref, k_ref, ext_ref)
    shifts_of(k_ref, s_ref)
    left_features(k_ref, phil_ref, s_ref, pl_ref)
    for_heads(lambda h: main_features(h, k_ref, phi_ref, s_ref, pm_ref))
    for_heads(lambda h: add_head_kernel(h, acc_ref, ext_ref, phi_ref))
    add_left_kernel(acc_ref, ext_ref, phil_ref)


def first_body(info_ref, x_ref, cols_ref, wkvt_ref, pm_ref, pl_ref, out_ref, acc_ref, *scratch):
    @pl.when(pl.program_id(0) == 0)
    def _():
        acc_ref[...] = jnp.zeros_like(acc_ref)

    tokens, alive = tokens_and_marks(x_ref)
    key_sums(tokens, alive, cols_ref, wkvt_ref, pm_ref, pl_ref, acc_ref, *scratch)

    @pl.when(pl.program_id(0) == pl.num_programs(0) - 1)
    def _():
        out_ref[...] = acc_ref[...].astype(BF)


def add_blocks(acc_ref, at, values):
    rows, width = values.shape
    for c in range(-(-width // 128)):
        take = min(128, width - c * 128)
        first = (at + c) * DX
        acc_ref[first : first + rows, 0:take] += values[:, c * 128 : c * 128 + take]


def add_small(small_ref, which, values):
    small_ref[which * D : (which + 1) * D, :] += lane_sums(values)


def add_first_norm(small_ref, which, acc_ref, weight_refs, cols_ref):
    with_normed = jnp.zeros((D, 128), F32)
    alone = jnp.zeros((D, 128), F32)
    block = 0
    for ref in weight_refs:
        for c in range(ref.shape[1] // 128):
            weight = ref[:, c * 128 : (c + 1) * 128].astype(F32)
            first = block * DX
            with_normed += weight * acc_ref[first : first + D, :]
            alone += weight * acc_ref[first + D : first + D + 1, :]
            block += 1
    gain = (with_normed - column(cols_ref, B1) * alone) / column(cols_ref, G1)
    small_ref[which * D : (which + 1) * D, :] = gain
    small_ref[(which + 1) * D : (which + 2) * D, :] = alone


def pack_sums(out_refs, acc_ref, small_ref, flat_ref, me, rows):
    blocks = acc_ref.shape[0] // DX
    base = blocks * rows
    for k in range(blocks):
        flat_ref[k * rows : (k + 1) * rows, :] = acc_ref[k * DX : k * DX + rows, :]
    flat_ref[base:, :] = jnp.zeros((flat_ref.shape[0] - base, 128), F32)
    high = small_ref[...].astype(BF)
    low = (small_ref[...] - high.astype(F32)).astype(BF)
    ones = jnp.ones((8, 128), BF)
    row = base
    for which in range(small_ref.shape[0] // D):
        part = slice(which * D, (which + 1) * D)
        line = dot_nt(ones, high[part]) + dot_nt(ones, low[part])
        flat_ref[row : row + 1, :] = line[0:1, 0:128]
        flat_ref[row + 1 : row + 2, 0 : D - 128] = line[0:1, 128:D]
        row += 2
    rows = out_refs[0].shape[0]
    for s, ref in enumerate(out_refs):
        owner = jnp.bitwise_xor(me, s)
        ref[...] = flat_ref[pl.ds(pl.multiple_of(owner * rows, 16), rows), :].astype(BF)


def put_side_by_side(out_ref, value):
    slots = value.shape[1] // STEP
    for k in range(STEP):
        out_ref[k] = value[:, k * slots : (k + 1) * slots]


def start_sums(start, ins, refs):
    for k, ref in enumerate(refs):
        ref[...] = jnp.zeros_like(ref) if start else ins[k][...]


def second_body(blocks, start, parts, unroll):
    def body(info_ref, x_ref, dy_ref, *rest):
        k_refs, rest = rest[:blocks], rest[blocks:]
        ins = ()
        if not start:
            ins, rest = rest[:2], rest[2:]
        (
            cols_ref, wqt_ref, wq_ref, wot_ref, wo_ref, upt_ref, up_ref, downt_ref, down_ref,
            pm_ref, pl_ref, tm_ref, tl_ref,
        ), rest = rest[:13], rest[13:]
        (out_ref, gmix_ref, gnq_ref, kg_ref), rest = rest[:4], rest[4:]
        if parts:
            packed_refs, (flat_ref, ga_ref, sm_ref, *rest) = rest[:parts], rest[parts:]
        else:
            (ga_ref, sm_ref), rest = rest[:2], rest[2:]
        (
            whole_ref, acc_ref, q_ref, gq_ref, ext_ref, phi_ref, phil_ref, s_ref, kt_ref, kl_ref, wide_ref,
            att_ref, rec_ref, act_ref, gup_ref, n1_ref, n2_ref,
        ) = rest
        j = pl.program_id(0)

        @pl.when(j == 0)
        def _():
            start_sums(start, ins, (ga_ref, sm_ref))
            acc_ref[...] = jnp.zeros_like(acc_ref)
            sum_kernels(k_refs, whole_ref)
            read_kernel(whole_ref, kt_ref, kl_ref)

        tokens, alive = tokens_and_marks(x_ref)
        row_alive = alive > 0
        normed, _, _ = norm_cols(tokens, column(cols_ref, G1), column(cols_ref, B1))
        n1_ref[...] = with_ones(normed)
        q_ref[...] = dot(wqt_ref[...], n1_ref[...]).astype(BF)
        shifts_of(q_ref, s_ref)
        left_features(q_ref, phil_ref, s_ref, pl_ref)
        wide_ref[...] = dot(kl_ref[...], phil_ref[...])
        for_heads(lambda h: main_features(h, q_ref, phi_ref, s_ref, pm_ref))

        def attend(h):
            combined = dot(kt_ref[ext_rows(h), :], phi_ref[main_rows(h), :]) + wide_ref[ext_rows(h), :]
            inverse = 1.0 / jnp.where(row_alive, combined[HEAD_SIZE : HEAD_SIZE + 1], 1.0)
            rec_ref[one_row(h), :] = inverse
            quotient = combined[:HEAD_SIZE] * inverse
            wide_ref[val_rows(h), :] = quotient
            att_ref[head_rows(h), :] = quotient.astype(BF)

        for_heads(attend)
        mixed = tokens + dot(wot_ref[...], att_ref[...]) + column(cols_ref, OB)
        second, second_normed, second_inverse = norm_cols(
            mixed, column(cols_ref, G2), column(cols_ref, B2)
        )
        n2_ref[...] = with_ones(second)
        upstream_wide = jnp.where(row_alive, side_by_side(dy_ref).astype(F32), 0.0)
        upstream = upstream_wide.astype(BF)
        for c in range(FF // FF_CHUNK):
            rows = slice(c * FF_CHUNK, (c + 1) * FF_CHUNK)
            up = dot(upt_ref[rows, :], n2_ref[...]) + cols_ref[rows, UB : UB + 1]
            grad_act = dot(downt_ref[rows, :], upstream)
            half = 0.5 * (1.0 + lax.erf(up * 0.7071067811865476))
            act_ref[rows, :] = (up * half).astype(BF)
            slope = half + up * jnp.exp(-0.5 * up * up) * 0.3989422804014327
            grad_up = (grad_act * slope).astype(BF)
            gup_ref[rows, :] = grad_up
        result = mixed + dot(down_ref[...], act_ref[...]) + column(cols_ref, DB)
        put_side_by_side(out_ref, jnp.where(row_alive, result, tokens).astype(BF))

        add_blocks(ga_ref, DOWN_AT, dot_nt(upstream, act_ref[...]))
        add_blocks(ga_ref, UP_AT, dot_nt(n2_ref[...], gup_ref[...]))
        add_small(sm_ref, 3, upstream_wide)
        grad_second = dot(up_ref[...], gup_ref[...])
        add_small(sm_ref, 0, grad_second * second_normed)
        add_small(sm_ref, 1, grad_second)
        grad_mixed = upstream_wide + norm_cols_back(
            grad_second, second_normed, second_inverse, column(cols_ref, G2)
        )
        gmix_ref[0] = grad_mixed.astype(BF)
        grad_branch = grad_mixed.astype(BF)
        add_small(sm_ref, 2, grad_branch.astype(F32))
        add_blocks(ga_ref, WO_AT, dot_nt(grad_branch, att_ref[...]))
        pad_row = iota((16, alive.shape[1]), 0) == 0
        grad_att = dot(wo_ref[...], grad_branch)
        for h in range(HEADS):
            grad_head = grad_att[h * HEAD_SIZE : (h + 1) * HEAD_SIZE]
            inverse = rec_ref[h : h + 1, :]
            ext_ref[val_rows(h), :] = (grad_head * inverse).astype(BF)
            grad_sum = -inverse * jnp.sum(grad_head * wide_ref[val_rows(h), :], axis=0, keepdims=True)
            ext_ref[h * EXT + HEAD_SIZE : (h + 1) * EXT, :] = jnp.where(pad_row, grad_sum, 0.0).astype(BF)
        add_left_kernel(acc_ref, ext_ref, phil_ref)
        left_grads(phil_ref, kl_ref, ext_ref, tl_ref, wide_ref)
        for_heads(lambda h: add_head_kernel(h, acc_ref, ext_ref, phi_ref), unroll)
        for_heads(lambda h: weigh(h, phi_ref, kt_ref, ext_ref), unroll)
        for_heads(lambda h: main_grads(h, gq_ref, q_ref, phi_ref, tm_ref, wide_ref), unroll)
        add_blocks(ga_ref, WQ_AT, dot_nt(n1_ref[...], gq_ref[...]))
        gnq_ref[0] = dot(wq_ref[...], gq_ref[...]).astype(BF)

        @pl.when(j == pl.num_programs(0) - 1)
        def _():
            kg_ref[...] = acc_ref[...].astype(BF)
            if parts:
                add_first_norm(sm_ref, 4, ga_ref, [wq_ref], cols_ref)
                pack_sums(packed_refs, ga_ref, sm_ref, flat_ref, info_ref[0], DX)

    return body


def third_body(blocks, start, parts):
    def body(info_ref, x_ref, *rest):
        k_refs, rest = rest[:blocks], rest[blocks:]
        ins = ()
        if not start:
            ins, rest = rest[:1], rest[1:]
        (cols_ref, wkvt_ref, wkv_ref, pm_ref, pl_ref, tm_ref, tl_ref), rest = rest[:7], rest[7:]
        gout_ref, rest = rest[0], rest[1:]
        if parts:
            packed_refs, (flat_ref, ga_ref, sm_ref, *rest) = rest[:parts], rest[parts:]
        else:
            ga_ref, rest = rest[0], rest[1:]
        (
            whole_ref, k_ref, ext_ref, phi_ref, phil_ref, s_ref, kt_ref, kl_ref, wide_ref, n1_ref,
        ) = rest
        gkv_ref = gout_ref.at[0]

        @pl.when(pl.program_id(0) == 0)
        def _():
            start_sums(start, ins, (ga_ref,))
            sum_kernels(k_refs, whole_ref)
            read_kernel(whole_ref, kt_ref, kl_ref)

        tokens, alive = tokens_and_marks(x_ref)
        normed, _, _ = norm_cols(tokens, column(cols_ref, G1), column(cols_ref, B1))
        n1_ref[...] = with_ones(normed)
        keys_values(n1_ref[...], alive, wkvt_ref, k_ref, ext_ref)
        shifts_of(k_ref, s_ref)
        left_features(k_ref, phil_ref, s_ref, pl_ref)
        wide_ref[...] = dot(kl_ref[...], phil_ref[...])
        for_heads(lambda h: main_features(h, k_ref, phi_ref, s_ref, pm_ref))

        def value_grads(h):
            grad = dot(kt_ref[val_rows(h), :], phi_ref[main_rows(h), :]) + wide_ref[val_rows(h), :]
            gkv_ref[head_rows(HEADS + h), :] = (grad * alive).astype(BF)

        for_heads(value_grads)
        left_grads(phil_ref, kl_ref, ext_ref, tl_ref, wide_ref)
        for_heads(lambda h: weigh(h, phi_ref, kt_ref, ext_ref))
        for_heads(lambda h: main_grads(h, gkv_ref, k_ref, phi_ref, tm_ref, wide_ref))
        add_blocks(ga_ref, 0, dot_nt(n1_ref[...], gkv_ref[...]))

        if parts:

            @pl.when(pl.program_id(0) == pl.num_programs(0) - 1)
            def _():
                add_first_norm(sm_ref, 0, ga_ref, [wkv_ref], cols_ref)
                pack_sums(packed_refs, ga_ref, sm_ref, flat_ref, info_ref[0], D)

    return body


def last_body(info_ref, x_ref, dy_ref, gmix_ref, gnq_ref, gkv_ref, cols_ref, wkv_ref, *rest):
    out_refs = rest[-GROUP:]
    tokens, alive = tokens_and_marks(x_ref)
    _, normed, inverse = norm_cols(tokens, column(cols_ref, G1), column(cols_ref, B1))
    grad_normed = gnq_ref[0].astype(F32) + dot(wkv_ref[...], gkv_ref[0])
    grad_in = gmix_ref[0].astype(F32) + norm_cols_back(grad_normed, normed, inverse, column(cols_ref, G1))
    grad_in = jnp.where(alive > 0, grad_in, side_by_side(dy_ref).astype(F32))
    slots = grad_in.shape[1] // STEP
    odd = lax.rem(info_ref[1], 2) == 1
    first, second = grad_in[:, :slots], grad_in[:, slots:]
    first, second = jnp.where(odd, second, first).astype(BF), jnp.where(odd, first, second).astype(BF)
    for k in range(GROUP // STEP):

        @pl.when(pl.program_id(0) == k)
        def _():
            out_refs[STEP * k][0] = first
            out_refs[STEP * k + 1][0] = second


def place_body(info_ref, *refs):
    odd = lax.rem(info_ref[1], 2) == 1
    out_ref = refs[-1]
    for k in range((len(refs) - 1) // 2):

        @pl.when(pl.program_id(0) == k)
        def _():
            first, second = refs[2 * k][0], refs[2 * k + 1][0]
            out_ref[0] = jnp.where(odd, second, first)
            out_ref[1] = jnp.where(odd, first, second)


def unpack_body(count, block, pieces, sums, smalls, extras):
    def body(info_ref, *rest):
        in_refs, whole_ref = rest[:count], rest[-1]
        out_refs = list(rest[-1 - len(pieces) - len(sums) - len(smalls) : -1])
        rows = in_refs[0].shape[0]
        for s, ref in enumerate(in_refs):
            owner = jnp.bitwise_xor(info_ref[0], s)
            whole_ref[pl.ds(pl.multiple_of(owner * rows, 16), rows), :] = ref[...].astype(F32)
        for at, width in pieces:
            ref = out_refs.pop(0)
            for c in range(-(-width // 128)):
                take = min(128, width - c * 128)
                first = (at + c) * block
                ref[:, c * 128 : c * 128 + take] = whole_ref[first : first + D, 0:take]
        for at, width in sums:
            ref = out_refs.pop(0)
            ref[...] = jnp.zeros_like(ref)
            for c in range(-(-width // 128)):
                first = (at + c) * block + D
                ref[c : c + 1, :] = whole_ref[first : first + 1, :]
        for k, (row, width) in enumerate(smalls):
            ref = out_refs.pop(0)
            line = jnp.concatenate(
                [whole_ref[row : row + 1, :], whole_ref[row + 1 : row + 2, 0 : width - 128]], axis=1
            )
            ref[...] = line + rest[count + k][...] if k < extras else line

    return body


def whole(array):
    zeros = (0,) * len(array.shape)
    return pl.BlockSpec(array.shape, lambda i, info: zeros)


def call(body, info, ins, in_specs, outs, out_specs, scratch, grid=1, us=1, waits=()):
    if waits:
        first, _ = lax.optimization_barrier((ins[0], list(waits)))
        ins = [first] + list(ins[1:])
    return pl.pallas_call(
        body,
        grid_spec=pltpu.PrefetchScalarGridSpec(
            num_scalar_prefetch=1,
            grid=(grid,),
            in_specs=in_specs,
            out_specs=out_specs,
            scratch_shapes=[pltpu.VMEM(shape, kind) for shape, kind in scratch],
        ),
        out_shape=outs,
        compiler_params=pltpu.CompilerParams(
            dimension_semantics=("arbitrary",), vmem_limit_bytes=VMEM_LIMIT
        ),
        cost_estimate=pl.CostEstimate(
            flops=int(us * 1.15e9), bytes_accessed=int(us * 1e5), transcendentals=0
        ),
    )(info, *ins)


def swap(value, axis, groups=None):
    return lax.all_to_all(value, axis, 0, 0, axis_index_groups=groups, tiled=True)


def share_kernel(part, nt):
    others = nt // GROUP
    got = [part]
    for s in range(1, others):
        got.append(lax.ppermute(part, "tok", [(i, (i + s * GROUP) % nt) for i in range(nt)]))
    return got


class Reduction:
    def __init__(self, packed, info, rows, nc, nt):
        self.packed, self.info, self.rows, self.nc, self.nt = packed, info, rows, nc, nt
        self.quarter, self.share = rows // nc, rows // (nc * nt)

    def cross(self, values):
        return [values[0]] + [
            lax.ppermute(values[s], "cells", [(i, i ^ s) for i in range(self.nc)])
            for s in range(1, self.nc)
        ]

    def total(self, parts, waits):
        parts, _ = lax.optimization_barrier((parts, waits))
        total = parts[0].astype(F32)
        for part in parts[1:]:
            total = total + part.astype(F32)
        return total.astype(BF)

    def over_cells(self):
        self.one = self.cross(self.packed)

    def over_tok(self, waits):
        mine = self.total(self.one, waits)
        self.two = swap(mine.reshape(self.nt, self.share, 128), "tok")
        return mine

    def back_tok(self, waits):
        two, _ = lax.optimization_barrier((self.two, waits))
        mine = self.total([two[k] for k in range(self.nt)], [])
        mine = jnp.broadcast_to(mine[None], (self.nt,) + mine.shape)
        self.three = swap(mine, "tok")
        return mine

    def back_cells(self):
        self.four = self.cross([self.three.reshape(self.quarter, 128)] * self.nc)

    def results(self, block, pieces, sums, smalls, waits=(), extras=()):
        outs = [jax.ShapeDtypeStruct((D, width), F32) for _, width in pieces]
        outs += [jax.ShapeDtypeStruct((8, 128), F32) for _ in sums]
        outs += [jax.ShapeDtypeStruct((1, width), F32) for _, width in smalls]
        outs = call(
            unpack_body(self.nc, block, pieces, sums, smalls, len(extras)), self.info,
            self.four + list(extras), [whole(v) for v in self.four + list(extras)], outs, [whole(v) for v in outs], [((self.rows, 128), F32)],
            us=0.02, waits=waits,
        )
        return outs[: len(pieces)], outs[len(pieces) :]


def padded_rows(need, nc, nt):
    unit = nc * nt * 16
    return -(-need // unit) * unit


def shards(
    tokens, cotangent, gene_count, expressed, projection, first_gain, first_bias, query_weight,
    key_weight, value_weight, out_weight, out_bias, second_gain, second_bias, up_weight, up_bias,
    down_weight, down_bias,
):
    cells, _, slots = tokens.shape
    turns = cells // GROUP
    steps, lanes = GROUP // STEP, STEP * slots
    nt, nc = lax.axis_size("tok"), lax.axis_size("cells")
    position = lax.axis_index("tok")
    groups = [[g * GROUP + i for i in range(GROUP)] for g in range(nt // GROUP)]
    info = jnp.stack([lax.axis_index("cells"), position % GROUP]).astype(jnp.int32)

    slot_index = position * slots + lax.broadcasted_iota(jnp.int32, (cells, slots), 1)
    alive = ((slot_index < gene_count[:, None]) & (expressed > 0)).astype(BF)
    marks = jnp.pad(alive[:, None, :], ((0, 0), (0, DX - D - 1), (0, 0)))

    def turn_of(array, c):
        return array[c * GROUP : (c + 1) * GROUP]

    x = [
        swap(jnp.concatenate([turn_of(tokens, c), turn_of(marks, c)], axis=1), "tok", groups)
        for c in range(turns)
    ]

    vectors = [first_gain, first_bias, second_gain, second_bias, out_bias, down_bias, up_bias]
    vec = jnp.stack([jnp.pad(v, (0, FF - v.shape[0])) for v in vectors + [jnp.zeros((FF,), F32)]])
    outs = [jax.ShapeDtypeStruct((FF, 8), F32)] + [
        jax.ShapeDtypeStruct(shape, BF)
        for shape in (
            (INNER, DX), (D, 2 * INNER), (2 * INNER, DX), (INNER, D), (FF, DX), (FF, D),
            (MAIN, HEAD_SIZE), (LEFT, INNER), (EXT, MAIN), (HEADS * EXT, LEFT),
        )
    ]
    wot = out_weight.T
    ins = [
        vec, projection.T, query_weight, key_weight, value_weight, wot, up_weight, down_weight,
    ]
    cols, wqt, wkv, wkvt, wo, upt, downt, pm, left_proj, tm, tl = call(
        prep_body, info, ins, [whole(v) for v in ins], outs, [whole(v) for v in outs], [], us=4,
    )

    x_spec = pl.BlockSpec((STEP, DX, slots), lambda j, info: (j, 0, 0))

    def step_spec(rows):
        return pl.BlockSpec((1, rows, lanes), lambda j, info: (j, 0, 0))

    k_out = jax.ShapeDtypeStruct((KROWS, MAIN), BF)
    k_acc = ((KROWS, MAIN), F32)
    key_scratch = [
        ((INNER, lanes), BF), ((HEADS * EXT, lanes), BF), ((HEADS * MAIN, lanes), BF),
        ((LEFT, lanes), BF), ((16, lanes), F32),
    ]
    kernels, dy = [], []
    for c in range(turns):
        ins = [x[c], cols, wkvt, pm, left_proj]
        part = call(
            first_body, info, ins, [x_spec] + [whole(v) for v in ins[1:]],
            k_out, whole(k_out), [k_acc] + key_scratch, grid=steps, us=12,
        )
        mine, part = lax.optimization_barrier((turn_of(cotangent, c), part))
        kernels.append(share_kernel(part, nt))
        dy.append(swap(mine, "tok", groups))

    token_out = jax.ShapeDtypeStruct((GROUP, D, slots), BF)
    token_spec = pl.BlockSpec((STEP, D, slots), lambda j, info: (j, 0, 0))
    wide_out = jax.ShapeDtypeStruct((steps, D, lanes), BF)
    common = [
        ((HEADS * EXT, lanes), BF), ((HEADS * MAIN, lanes), BF), ((LEFT, lanes), BF),
        ((16, lanes), F32), ((HEADS * EXT, MAIN), BF), ((HEADS * EXT, LEFT), BF),
        ((HEADS * EXT, lanes), F32),
    ]
    weights = [
        cols, wqt, query_weight, wot, wo, upt, up_weight, downt, down_weight,
        pm, left_proj, tm, tl,
    ]
    rows2 = padded_rows(GRAD2 + 2 * SMALL2, nc, nt)
    sums = [((GRAD2, 128), F32), ((SMALL2 * D, 128), F32)]
    mixed_grads, query_grads, kernel_grads = [], [], []
    results, sums2 = [], []
    for c in range(turns):
        start, last = c == 0, c == turns - 1
        fixed = kernels[c] + sums2 + weights
        if last:
            sum_outs = [jax.ShapeDtypeStruct((rows2 // nc, 128), BF)] * nc
            sum_scratch = [((rows2, 128), F32)] + sums
        else:
            sum_outs = [jax.ShapeDtypeStruct(shape, kind) for shape, kind in sums]
            sum_scratch = []
        out, gmix, gnq, kg, *sums2 = call(
            second_body(len(kernels[c]), start, nc if last else 0, HEADS if start else UNROLL), info, [x[c], dy[c]] + fixed,
            [x_spec, token_spec] + [whole(v) for v in fixed],
            [token_out, wide_out, wide_out, k_out] + sum_outs,
            [token_spec, step_spec(D), step_spec(D)] + [whole(v) for v in [k_out] + sum_outs],
            sum_scratch + [((KROWS, MAIN), BF), k_acc, ((INNER, lanes), BF), ((INNER, lanes), BF)]
            + common
            + [
                ((INNER, lanes), BF), ((16, lanes), F32), ((FF, lanes), BF), ((FF, lanes), BF),
                ((DX, lanes), BF), ((DX, lanes), BF),
            ],
            grid=steps, us=40,
        )
        results.append(swap(out, "tok", groups))
        mixed_grads.append(gmix)
        query_grads.append(gnq)
        kernel_grads.append(share_kernel(kg, nt))
    reduce2 = Reduction(sums2, info, rows2, nc, nt)
    reduce2.over_cells()

    rows3 = padded_rows(2 * Q_BLOCKS * D + 2 * SMALL3, nc, nt)
    weights = [cols, wkvt, wkv, pm, left_proj, tm, tl]
    joined_grads, sums3 = [], []
    waits = [sums2[0], results[0]]
    for c in range(turns):
        start, last = c == 0, c == turns - 1
        fixed = kernel_grads[c] + sums3 + weights
        if last:
            sum_outs = [jax.ShapeDtypeStruct((rows3 // nc, 128), BF)] * nc
            sum_scratch = [((rows3, 128), F32), ((GRAD3, 128), F32), ((SMALL3 * D, 128), F32)]
        else:
            sum_outs = [jax.ShapeDtypeStruct((GRAD3, 128), F32)]
            sum_scratch = []
        joined = jax.ShapeDtypeStruct((steps, 2 * INNER, lanes), BF)
        got, *sums3 = call(
            third_body(len(kernel_grads[c]), start, nc if last else 0), info,
            [x[c]] + fixed, [x_spec] + [whole(v) for v in fixed],
            [joined] + sum_outs, [step_spec(2 * INNER)] + [whole(v) for v in sum_outs],
            sum_scratch + [((KROWS, MAIN), BF), ((INNER, lanes), BF)] + common + [((DX, lanes), BF)],
            grid=steps, us=22, waits=waits,
        )
        joined_grads.append(got)
        if start:
            waits = [reduce2.over_tok([got, results[-1]] + kernel_grads[-1][1:])]
    reduce3 = Reduction(sums3, info, rows3, nc, nt)
    reduce3.over_cells()
    waits = [sums3[0], results[-1], reduce2.back_tok([sums3[0]])]
    one_out = jax.ShapeDtypeStruct((1, D, slots), BF)
    grads = []
    for c in range(turns):
        ins = [x[c], dy[c], mixed_grads[c], query_grads[c], joined_grads[c], cols, wkv]

        def pair(rows, blocks=STEP, columns=slots):
            return pl.BlockSpec(
                (blocks, rows, columns), lambda j, info: (jnp.bitwise_xor(info[1] // STEP, j), 0, 0)
            )

        specs = [pair(DX), pair(D)] + [pair(rows, 1, lanes) for rows in (D, D, 2 * INNER)]
        out = call(
            last_body, info, ins, specs + [whole(cols), whole(wkv)], [one_out] * GROUP,
            [whole(one_out)] * GROUP, [], grid=steps, us=6, waits=waits,
        )
        if c == turns - 1:
            reduce2.back_cells()
            mine = reduce3.back_tok([out[0]] + reduce2.four[1:3] + grads[1:])
            out, _ = lax.optimization_barrier((out, mine))
        grads += [out[0]] + [
            lax.ppermute(out[s], "tok", [(i, i - i % GROUP + (i % GROUP ^ s)) for i in range(nt)])
            for s in range(1, GROUP)
        ]
        if c == 0:
            waits = [reduce3.over_tok([out[0]]), reduce2.three]
    (dwq, dwot, dup, ddown), (upb, gain2, bias2, outb, downb, gain1q, bias1q) = reduce2.results(
        DX, [(WQ_AT, INNER), (WO_AT, INNER), (UP_AT, FF), (DOWN_AT, FF)], [(UP_AT, FF)],
        [(GRAD2 + 2 * k, D) for k in range(SMALL2)], waits=[reduce3.three],
    )
    reduce3.back_cells()

    pairs = GROUP // 2

    def pair_of_cells(i, info):
        return i // pairs * pairs + jnp.bitwise_xor(info[1] // 2, lax.rem(i, pairs)), 0, 0

    result = jnp.concatenate(results, axis=0)
    grad_in = call(
        place_body, info, grads, [whole(v) for v in grads], jax.ShapeDtypeStruct((cells, D, slots), BF),
        pl.BlockSpec((2, D, slots), pair_of_cells), [], grid=cells // 2, us=0.02,
        waits=[gain1q],
    )
    (dwk, dwv), (gain1, bias1) = reduce3.results(
        D, [(0, INNER), (Q_BLOCKS, INNER)], [], [(2 * Q_BLOCKS * D + 2 * k, D) for k in range(SMALL3)],
        extras=[gain1q, bias1q], waits=[grad_in],
    )
    return (
        result, grad_in, gain1[0], bias1[0], dwq, dwk, dwv, dwot.T, outb[0],
        gain2[0], bias2[0], dup, upb.reshape(8 * 128)[:FF], ddown, downb[0],
    )


def solution(mesh):
    rows = P("cells", None, "tok")
    placed = (rows, rows, P("cells"), P("cells", "tok")) + (P(),) * 14
    return jax.shard_map(
        shards,
        mesh=mesh,
        in_specs=placed,
        out_specs=(rows, rows) + (P(),) * 13,
        check_vma=False,
    )
```

```python
import math

import jax
import jax.numpy as jnp
from jax import lax
from jax.experimental import pallas as pl
from jax.experimental.pallas import tpu as pltpu
from jax.sharding import PartitionSpec as P

HEADS = 10
HEAD_SIZE = 64
FEATURES = 266
D = 200
INNER = HEADS * HEAD_SIZE
DX = 208
FF = 800
EPSILON = 1e-05

MAIN = 256
REST = FEATURES - MAIN
LEFT = 128
EXT = 80
SUM_ROW = INNER
LEFT_ROW = INNER + 16
KROWS = LEFT_ROW + 48

C0 = HEAD_SIZE ** (-0.25)
LOG2E = 1.0 / math.log(2.0)
RAW_SCALE = C0 * LOG2E
SQ_SCALE = 0.5 * C0 * C0 * LOG2E
SHIFT = -0.5 * math.log2(FEATURES)
FF_CHUNK = 160
Q_BLOCKS = INNER // 128
F_BLOCKS = -(-FF // 128)
WQ_AT, WO_AT, UP_AT, DOWN_AT = 0, Q_BLOCKS, 2 * Q_BLOCKS, 2 * Q_BLOCKS + F_BLOCKS
GRAD2 = (2 * Q_BLOCKS + 2 * F_BLOCKS) * DX
GRAD3 = 2 * Q_BLOCKS * DX
SMALL2 = 6
SMALL3 = 2

BF = jnp.bfloat16
F32 = jnp.float32
VMEM_LIMIT = 56 * 1024 * 1024
GROUP = 4
STEP = 2
UNROLL = 5


def dot(left, right):
    return jnp.dot(left, right, preferred_element_type=F32)


def dot_nt(left, right):
    return lax.dot_general(left, right, (((1,), (1,)), ((), ())), preferred_element_type=F32)


def dot_tn(left, right):
    return lax.dot_general(left, right, (((0,), (0,)), ((), ())), preferred_element_type=F32)


def iota(shape, axis):
    return lax.broadcasted_iota(jnp.int32, shape, axis)


def norm_cols(values, gain, bias):
    average = jnp.mean(values, axis=0, keepdims=True)
    centred = values - average
    inverse = lax.rsqrt(jnp.mean(centred * centred, axis=0, keepdims=True) + EPSILON)
    normed = centred * inverse
    return normed * gain + bias, normed, inverse


def norm_cols_back(grad_out, normed, inverse, gain):
    scaled = grad_out * gain
    return inverse * (
        scaled
        - jnp.mean(scaled, axis=0, keepdims=True)
        - normed * jnp.mean(scaled * normed, axis=0, keepdims=True)
    )


def lane_sums(values):
    total = values[:, :128]
    for start in range(128, values.shape[1], 128):
        total = total + values[:, start : start + 128]
    return total


def ext_rows(h):
    return pl.ds(pl.multiple_of(h * EXT, 16), EXT)


def val_rows(h):
    return pl.ds(pl.multiple_of(h * EXT, 16), HEAD_SIZE)


def main_rows(h):
    return pl.ds(pl.multiple_of(h * MAIN, MAIN), MAIN)


def head_rows(h):
    return pl.ds(pl.multiple_of(h * HEAD_SIZE, HEAD_SIZE), HEAD_SIZE)


def one_row(h):
    return pl.ds(h, 1)


def for_heads(step, unroll=HEADS):
    def turn(i, _):
        for k in range(unroll):
            step(i * unroll + k)
        return 0

    if unroll == HEADS:
        turn(0, 0)
    else:
        lax.fori_loop(0, HEADS // unroll, turn, 0)


G1, B1, G2, B2, OB, DB, UB = range(7)


def column(cols_ref, which, rows=D):
    return cols_ref[0:rows, which : which + 1]


def prep_body(
    info_ref, vec_ref, projt_ref, wq_ref, wk_ref, wv_ref, wot_ref, up_ref, down_ref,
    cols_ref, wqt_ref, wkv_ref, wkvt_ref, wo_ref, upt_ref, downt_ref,
    pm_ref, pl_ref, tm_ref, tl_ref,
):
    cols_ref[...] = vec_ref[...].T
    def padded(matrix):
        return jnp.concatenate([matrix.T, jnp.zeros((matrix.shape[1], DX - D), BF)], axis=1)

    wqt_ref[...] = padded(wq_ref[...])
    wkv_ref[:, :INNER] = wk_ref[...]
    wkv_ref[:, INNER:] = wv_ref[...]
    wkvt_ref[:INNER] = padded(wk_ref[...])
    wkvt_ref[INNER:] = padded(wv_ref[...])
    wo_ref[...] = wot_ref[...].T
    upt_ref[...] = padded(up_ref[...])
    downt_ref[...] = down_ref[...].T
    proj = projt_ref[...].T

    def one_hot(shape, mask):
        return jnp.where(mask, 1.0, 0.0).astype(BF)

    pm_ref[...] = proj[:MAIN]
    s = (16, FEATURES)
    rest = dot(one_hot(s, (iota(s, 0) + MAIN == iota(s, 1)) & (iota(s, 0) < REST)), proj).astype(BF)
    s = (HEAD_SIZE, INNER)
    wide = dot(rest, one_hot(s, iota(s, 0) == iota(s, 1) % HEAD_SIZE)).astype(BF)
    s = (LEFT, 16)
    tall = dot(one_hot(s, iota(s, 0) % REST == iota(s, 1)), wide)
    s = (LEFT, INNER)
    pl_ref[...] = jnp.where(iota(s, 0) // REST == iota(s, 1) // HEAD_SIZE, tall, 0.0).astype(BF)
    s = (EXT, HEAD_SIZE)
    pick = one_hot(s, iota(s, 0) == iota(s, 1))
    s = (EXT, MAIN)
    tm_ref[...] = jnp.where(iota(s, 0) == HEAD_SIZE, 1.0, dot_nt(pick, proj[:MAIN])).astype(BF)
    s = (EXT, 16)
    rest_ext = jnp.where(iota(s, 0) == HEAD_SIZE, 1.0, dot_nt(pick, rest)).astype(BF)
    s = (16, LEFT)
    spread = dot(rest_ext, one_hot(s, iota(s, 0) == iota(s, 1) % REST))
    s = (EXT, LEFT)
    for h in range(HEADS):
        tl_ref[ext_rows(h), :] = jnp.where(iota(s, 1) // REST == h, spread, 0.0).astype(BF)


def shifts_of(u_ref, s_ref):
    for h in range(HEADS):
        wide = u_ref[head_rows(h), :].astype(F32)
        s_ref[h : h + 1, :] = SHIFT - SQ_SCALE * jnp.sum(wide * wide, axis=0, keepdims=True)


def left_features(u_ref, phil_ref, s_ref, pl_ref):
    shape = (LEFT, u_ref.shape[1])
    owner = iota(shape, 0) // REST
    shifts = jnp.zeros(shape, F32)
    for h in range(HEADS):
        shifts = jnp.where(owner == h, s_ref[h : h + 1, :], shifts)
    phil_ref[...] = jnp.exp2(dot(pl_ref[...], u_ref[...]) * RAW_SCALE + shifts).astype(BF)


def main_features(h, u_ref, phi_ref, s_ref, pm_ref):
    raw = dot(pm_ref[...], u_ref[head_rows(h), :])
    phi_ref[main_rows(h), :] = jnp.exp2(raw * RAW_SCALE + s_ref[one_row(h), :]).astype(BF)


def add_head_kernel(h, acc_ref, ext_ref, phi_ref):
    total = dot_nt(ext_ref[ext_rows(h), :], phi_ref[main_rows(h), :])
    acc_ref[head_rows(h), :] += total[:HEAD_SIZE]
    acc_ref[one_row(SUM_ROW + h), :] += total[HEAD_SIZE : HEAD_SIZE + 1]


def add_left_kernel(acc_ref, ext_ref, phil_ref):
    every = dot_nt(ext_ref[...], phil_ref[...])
    owner = iota((EXT, LEFT), 1) // REST
    left = jnp.zeros((EXT, LEFT), F32)
    for h in range(HEADS):
        left = jnp.where(owner == h, every[h * EXT : (h + 1) * EXT], left)
    acc_ref[LEFT_ROW:KROWS, 0:LEFT] += left[:48]
    acc_ref[LEFT_ROW : LEFT_ROW + 32, LEFT:MAIN] += left[48:EXT]


def sum_kernels(in_refs, whole_ref):
    total = in_refs[0][...].astype(F32)
    for ref in in_refs[1:]:
        total = total + ref[...].astype(F32)
    whole_ref[...] = total.astype(BF)


def read_kernel(whole_ref, kt_ref, kl_ref):
    sums = whole_ref[SUM_ROW : SUM_ROW + 16, :].astype(F32)
    first = iota((16, MAIN), 0) == 0
    left = jnp.concatenate(
        [whole_ref[LEFT_ROW:KROWS, 0:LEFT], whole_ref[LEFT_ROW : LEFT_ROW + 32, LEFT:MAIN]], axis=0
    ).astype(F32)
    owner = iota((EXT, LEFT), 1) // REST
    for h in range(HEADS):
        kt_ref[val_rows(h), :] = whole_ref[head_rows(h), :]
        kt_ref[h * EXT + HEAD_SIZE : (h + 1) * EXT, :] = jnp.where(
            first, sums[h : h + 1, :], 0.0
        ).astype(BF)
        kl_ref[ext_rows(h), :] = jnp.where(owner == h, left, 0.0).astype(BF)


def left_grads(phil_ref, kl_ref, ext_ref, tl_ref, wide_ref):
    phil_ref[...] = (dot_tn(kl_ref[...], ext_ref[...]) * phil_ref[...].astype(F32)).astype(BF)
    wide_ref[...] = dot(tl_ref[...], phil_ref[...])


def weigh(h, phi_ref, kt_ref, ext_ref):
    grad = dot_tn(kt_ref[ext_rows(h), :], ext_ref[ext_rows(h), :])
    phi_ref[main_rows(h), :] = (grad * phi_ref[main_rows(h), :].astype(F32)).astype(BF)


def main_grads(h, grad_ref, u_ref, phi_ref, tm_ref, wide_ref):
    through = dot(tm_ref[...], phi_ref[main_rows(h), :]) + wide_ref[ext_rows(h), :]
    grad_ref[head_rows(h), :] = (
        C0 * through[:HEAD_SIZE]
        - (C0 * C0) * u_ref[head_rows(h), :].astype(F32) * through[HEAD_SIZE : HEAD_SIZE + 1]
    ).astype(BF)


def with_ones(values):
    rows = iota((DX - D, values.shape[1]), 0)
    return jnp.concatenate([values, jnp.where(rows == 0, 1.0, 0.0)], axis=0).astype(BF)


def side_by_side(ref):
    blocks = [ref[(k,) + (0,) * (len(ref.shape) - 3)] for k in range(STEP)]
    return jnp.concatenate(blocks, axis=1)


def tokens_and_marks(x_ref):
    both = side_by_side(x_ref).astype(F32)
    return both[:D], both[D : D + 1]


def keys_values(normed_low, alive, wkvt_ref, k_ref, ext_ref):
    k_ref[...] = dot(wkvt_ref[:INNER, :], normed_low).astype(BF)
    values = dot(wkvt_ref[INNER:, :], normed_low)
    mark = jnp.where(iota((16, values.shape[1]), 0) == 0, alive, 0.0).astype(BF)
    for h in range(HEADS):
        ext_ref[val_rows(h), :] = (values[h * HEAD_SIZE : (h + 1) * HEAD_SIZE] * alive).astype(BF)
        ext_ref[h * EXT + HEAD_SIZE : (h + 1) * EXT, :] = mark


def key_sums(x, alive, cols_ref, wkvt_ref, pm_ref, pl_ref, acc_ref, k_ref, ext_ref, phi_ref, phil_ref, s_ref):
    normed, _, _ = norm_cols(x, column(cols_ref, G1), column(cols_ref, B1))
    keys_values(with_ones(normed), alive, wkvt_ref, k_ref, ext_ref)
    shifts_of(k_ref, s_ref)
    left_features(k_ref, phil_ref, s_ref, pl_ref)
    for_heads(lambda h: main_features(h, k_ref, phi_ref, s_ref, pm_ref))
    for_heads(lambda h: add_head_kernel(h, acc_ref, ext_ref, phi_ref))
    add_left_kernel(acc_ref, ext_ref, phil_ref)


def first_body(info_ref, x_ref, cols_ref, wkvt_ref, pm_ref, pl_ref, out_ref, acc_ref, *scratch):
    @pl.when(pl.program_id(0) == 0)
    def _():
        acc_ref[...] = jnp.zeros_like(acc_ref)

    tokens, alive = tokens_and_marks(x_ref)
    key_sums(tokens, alive, cols_ref, wkvt_ref, pm_ref, pl_ref, acc_ref, *scratch)

    @pl.when(pl.program_id(0) == pl.num_programs(0) - 1)
    def _():
        out_ref[...] = acc_ref[...].astype(BF)


def add_blocks(acc_ref, at, values):
    rows, width = values.shape
    for c in range(-(-width // 128)):
        take = min(128, width - c * 128)
        first = (at + c) * DX
        acc_ref[first : first + rows, 0:take] += values[:, c * 128 : c * 128 + take]


def add_small(small_ref, which, values):
    small_ref[which * D : (which + 1) * D, :] += lane_sums(values)


def add_first_norm(small_ref, which, acc_ref, weight_refs, cols_ref):
    with_normed = jnp.zeros((D, 128), F32)
    alone = jnp.zeros((D, 128), F32)
    block = 0
    for ref in weight_refs:
        for c in range(ref.shape[1] // 128):
            weight = ref[:, c * 128 : (c + 1) * 128].astype(F32)
            first = block * DX
            with_normed += weight * acc_ref[first : first + D, :]
            alone += weight * acc_ref[first + D : first + D + 1, :]
            block += 1
    gain = (with_normed - column(cols_ref, B1) * alone) / column(cols_ref, G1)
    small_ref[which * D : (which + 1) * D, :] = gain
    small_ref[(which + 1) * D : (which + 2) * D, :] = alone


def pack_sums(out_refs, acc_ref, small_ref, flat_ref, me, rows):
    blocks = acc_ref.shape[0] // DX
    base = blocks * rows
    for k in range(blocks):
        flat_ref[k * rows : (k + 1) * rows, :] = acc_ref[k * DX : k * DX + rows, :]
    flat_ref[base:, :] = jnp.zeros((flat_ref.shape[0] - base, 128), F32)
    high = small_ref[...].astype(BF)
    low = (small_ref[...] - high.astype(F32)).astype(BF)
    ones = jnp.ones((8, 128), BF)
    row = base
    for which in range(small_ref.shape[0] // D):
        part = slice(which * D, (which + 1) * D)
        line = dot_nt(ones, high[part]) + dot_nt(ones, low[part])
        flat_ref[row : row + 1, :] = line[0:1, 0:128]
        flat_ref[row + 1 : row + 2, 0 : D - 128] = line[0:1, 128:D]
        row += 2
    rows = out_refs[0].shape[0]
    for s, ref in enumerate(out_refs):
        owner = jnp.bitwise_xor(me, s)
        ref[...] = flat_ref[pl.ds(pl.multiple_of(owner * rows, 16), rows), :].astype(BF)


def put_side_by_side(out_ref, value):
    slots = value.shape[1] // STEP
    for k in range(STEP):
        out_ref[k] = value[:, k * slots : (k + 1) * slots]


def start_sums(start, ins, refs):
    for k, ref in enumerate(refs):
        ref[...] = jnp.zeros_like(ref) if start else ins[k][...]


def second_body(blocks, start, parts, unroll):
    def body(info_ref, x_ref, dy_ref, *rest):
        k_refs, rest = rest[:blocks], rest[blocks:]
        ins = ()
        if not start:
            ins, rest = rest[:2], rest[2:]
        (
            cols_ref, wqt_ref, wq_ref, wot_ref, wo_ref, upt_ref, up_ref, downt_ref, down_ref,
            pm_ref, pl_ref, tm_ref, tl_ref,
        ), rest = rest[:13], rest[13:]
        (out_ref, gmix_ref, gnq_ref, kg_ref), rest = rest[:4], rest[4:]
        if parts:
            packed_refs, (flat_ref, ga_ref, sm_ref, *rest) = rest[:parts], rest[parts:]
        else:
            (ga_ref, sm_ref), rest = rest[:2], rest[2:]
        (
            whole_ref, acc_ref, q_ref, gq_ref, ext_ref, phi_ref, phil_ref, s_ref, kt_ref, kl_ref, wide_ref,
            att_ref, rec_ref, act_ref, gup_ref, n1_ref, n2_ref,
        ) = rest
        j = pl.program_id(0)

        @pl.when(j == 0)
        def _():
            start_sums(start, ins, (ga_ref, sm_ref))
            acc_ref[...] = jnp.zeros_like(acc_ref)
            sum_kernels(k_refs, whole_ref)
            read_kernel(whole_ref, kt_ref, kl_ref)

        tokens, alive = tokens_and_marks(x_ref)
        row_alive = alive > 0
        normed, _, _ = norm_cols(tokens, column(cols_ref, G1), column(cols_ref, B1))
        n1_ref[...] = with_ones(normed)
        q_ref[...] = dot(wqt_ref[...], n1_ref[...]).astype(BF)
        shifts_of(q_ref, s_ref)
        left_features(q_ref, phil_ref, s_ref, pl_ref)
        wide_ref[...] = dot(kl_ref[...], phil_ref[...])
        for_heads(lambda h: main_features(h, q_ref, phi_ref, s_ref, pm_ref))

        def attend(h):
            combined = dot(kt_ref[ext_rows(h), :], phi_ref[main_rows(h), :]) + wide_ref[ext_rows(h), :]
            inverse = 1.0 / jnp.where(row_alive, combined[HEAD_SIZE : HEAD_SIZE + 1], 1.0)
            rec_ref[one_row(h), :] = inverse
            quotient = combined[:HEAD_SIZE] * inverse
            wide_ref[val_rows(h), :] = quotient
            att_ref[head_rows(h), :] = quotient.astype(BF)

        for_heads(attend)
        mixed = tokens + dot(wot_ref[...], att_ref[...]) + column(cols_ref, OB)
        second, second_normed, second_inverse = norm_cols(
            mixed, column(cols_ref, G2), column(cols_ref, B2)
        )
        n2_ref[...] = with_ones(second)
        upstream_wide = jnp.where(row_alive, side_by_side(dy_ref).astype(F32), 0.0)
        upstream = upstream_wide.astype(BF)
        for c in range(FF // FF_CHUNK):
            rows = slice(c * FF_CHUNK, (c + 1) * FF_CHUNK)
            up = dot(upt_ref[rows, :], n2_ref[...]) + cols_ref[rows, UB : UB + 1]
            grad_act = dot(downt_ref[rows, :], upstream)
            half = 0.5 * (1.0 + lax.erf(up * 0.7071067811865476))
            act_ref[rows, :] = (up * half).astype(BF)
            slope = half + up * jnp.exp(-0.5 * up * up) * 0.3989422804014327
            grad_up = (grad_act * slope).astype(BF)
            gup_ref[rows, :] = grad_up
        result = mixed + dot(down_ref[...], act_ref[...]) + column(cols_ref, DB)
        put_side_by_side(out_ref, jnp.where(row_alive, result, tokens).astype(BF))

        add_small(sm_ref, 3, upstream_wide)
        grad_second = dot(up_ref[...], gup_ref[...])
        add_blocks(ga_ref, DOWN_AT, dot_nt(upstream, act_ref[...]))
        add_small(sm_ref, 0, grad_second * second_normed)
        add_small(sm_ref, 1, grad_second)
        grad_mixed = upstream_wide + norm_cols_back(
            grad_second, second_normed, second_inverse, column(cols_ref, G2)
        )
        gmix_ref[0] = grad_mixed.astype(BF)
        grad_branch = grad_mixed.astype(BF)
        add_small(sm_ref, 2, grad_branch.astype(F32))
        pad_row = iota((16, alive.shape[1]), 0) == 0
        grad_att = dot(wo_ref[...], grad_branch)
        add_blocks(ga_ref, UP_AT, dot_nt(n2_ref[...], gup_ref[...]))
        add_blocks(ga_ref, WO_AT, dot_nt(grad_branch, att_ref[...]))
        for h in range(HEADS):
            grad_head = grad_att[h * HEAD_SIZE : (h + 1) * HEAD_SIZE]
            inverse = rec_ref[h : h + 1, :]
            ext_ref[val_rows(h), :] = (grad_head * inverse).astype(BF)
            grad_sum = -inverse * jnp.sum(grad_head * wide_ref[val_rows(h), :], axis=0, keepdims=True)
            ext_ref[h * EXT + HEAD_SIZE : (h + 1) * EXT, :] = jnp.where(pad_row, grad_sum, 0.0).astype(BF)
        add_left_kernel(acc_ref, ext_ref, phil_ref)
        left_grads(phil_ref, kl_ref, ext_ref, tl_ref, wide_ref)
        for_heads(lambda h: add_head_kernel(h, acc_ref, ext_ref, phi_ref))
        for_heads(lambda h: weigh(h, phi_ref, kt_ref, ext_ref), unroll)
        for_heads(lambda h: main_grads(h, gq_ref, q_ref, phi_ref, tm_ref, wide_ref), unroll)
        add_blocks(ga_ref, WQ_AT, dot_nt(n1_ref[...], gq_ref[...]))
        gnq_ref[0] = dot(wq_ref[...], gq_ref[...]).astype(BF)

        @pl.when(j == pl.num_programs(0) - 1)
        def _():
            kg_ref[...] = acc_ref[...].astype(BF)
            if parts:
                add_first_norm(sm_ref, 4, ga_ref, [wq_ref], cols_ref)
                pack_sums(packed_refs, ga_ref, sm_ref, flat_ref, info_ref[0], DX)

    return body


def third_body(blocks, start, parts):
    def body(info_ref, x_ref, gnq_ref, *rest):
        k_refs, rest = rest[:blocks], rest[blocks:]
        ins = ()
        if not start:
            ins, rest = rest[:1], rest[1:]
        (cols_ref, wkvt_ref, wkv_ref, pm_ref, pl_ref, tm_ref, tl_ref), rest = rest[:7], rest[7:]
        gn_ref, rest = rest[0], rest[1:]
        if parts:
            packed_refs, (flat_ref, ga_ref, sm_ref, *rest) = rest[:parts], rest[parts:]
        else:
            ga_ref, rest = rest[0], rest[1:]
        (
            whole_ref, k_ref, gkv_ref, ext_ref, phi_ref, phil_ref, s_ref, kt_ref, kl_ref, wide_ref, n1_ref,
        ) = rest

        @pl.when(pl.program_id(0) == 0)
        def _():
            start_sums(start, ins, (ga_ref,))
            sum_kernels(k_refs, whole_ref)
            read_kernel(whole_ref, kt_ref, kl_ref)

        tokens, alive = tokens_and_marks(x_ref)
        normed, _, _ = norm_cols(tokens, column(cols_ref, G1), column(cols_ref, B1))
        n1_ref[...] = with_ones(normed)
        keys_values(n1_ref[...], alive, wkvt_ref, k_ref, ext_ref)
        shifts_of(k_ref, s_ref)
        left_features(k_ref, phil_ref, s_ref, pl_ref)
        wide_ref[...] = dot(kl_ref[...], phil_ref[...])
        for_heads(lambda h: main_features(h, k_ref, phi_ref, s_ref, pm_ref))

        def value_grads(h):
            grad = dot(kt_ref[val_rows(h), :], phi_ref[main_rows(h), :]) + wide_ref[val_rows(h), :]
            gkv_ref[head_rows(HEADS + h), :] = (grad * alive).astype(BF)

        for_heads(value_grads)
        left_grads(phil_ref, kl_ref, ext_ref, tl_ref, wide_ref)
        for_heads(lambda h: weigh(h, phi_ref, kt_ref, ext_ref))
        for_heads(lambda h: main_grads(h, gkv_ref, k_ref, phi_ref, tm_ref, wide_ref))
        add_blocks(ga_ref, 0, dot_nt(n1_ref[...], gkv_ref[...]))
        gn_ref[0] = (gnq_ref[0].astype(F32) + dot(wkv_ref[...], gkv_ref[...])).astype(BF)

        if parts:

            @pl.when(pl.program_id(0) == pl.num_programs(0) - 1)
            def _():
                add_first_norm(sm_ref, 0, ga_ref, [wkv_ref], cols_ref)
                pack_sums(packed_refs, ga_ref, sm_ref, flat_ref, info_ref[0], D)

    return body


def last_body(info_ref, x_ref, dy_ref, gmix_ref, gn_ref, cols_ref, *rest):
    out_refs = rest[-GROUP:]
    tokens, alive = tokens_and_marks(x_ref)
    _, normed, inverse = norm_cols(tokens, column(cols_ref, G1), column(cols_ref, B1))
    grad_in = gmix_ref[0].astype(F32) + norm_cols_back(gn_ref[0].astype(F32), normed, inverse, column(cols_ref, G1))
    grad_in = jnp.where(alive > 0, grad_in, side_by_side(dy_ref).astype(F32))
    slots = grad_in.shape[1] // STEP
    odd = lax.rem(info_ref[1], 2) == 1
    first, second = grad_in[:, :slots], grad_in[:, slots:]
    first, second = jnp.where(odd, second, first).astype(BF), jnp.where(odd, first, second).astype(BF)
    for k in range(GROUP // STEP):

        @pl.when(pl.program_id(0) == k)
        def _():
            out_refs[STEP * k][0] = first
            out_refs[STEP * k + 1][0] = second


def place_body(info_ref, *refs):
    out_ref = refs[-1]
    for k, ref in enumerate(refs[:-1]):
        cell = k // GROUP * GROUP + jnp.bitwise_xor(info_ref[1], k % GROUP)
        out_ref[pl.ds(cell, 1)] = ref[...]


def unpack_body(count, block, pieces, sums, smalls, extras):
    def body(info_ref, *rest):
        in_refs, whole_ref = rest[:count], rest[-1]
        out_refs = list(rest[-1 - len(pieces) - len(sums) - len(smalls) : -1])
        rows = in_refs[0].shape[0]
        for s, ref in enumerate(in_refs):
            owner = jnp.bitwise_xor(info_ref[0], s)
            whole_ref[pl.ds(pl.multiple_of(owner * rows, 16), rows), :] = ref[...].astype(F32)
        for at, width in pieces:
            ref = out_refs.pop(0)
            for c in range(-(-width // 128)):
                take = min(128, width - c * 128)
                first = (at + c) * block
                ref[:, c * 128 : c * 128 + take] = whole_ref[first : first + D, 0:take]
        for at, width in sums:
            ref = out_refs.pop(0)
            ref[...] = jnp.zeros_like(ref)
            for c in range(-(-width // 128)):
                first = (at + c) * block + D
                ref[c : c + 1, :] = whole_ref[first : first + 1, :]
        for k, (row, width) in enumerate(smalls):
            ref = out_refs.pop(0)
            line = jnp.concatenate(
                [whole_ref[row : row + 1, :], whole_ref[row + 1 : row + 2, 0 : width - 128]], axis=1
            )
            ref[...] = line + rest[count + k][...] if k < extras else line

    return body


def whole(array):
    zeros = (0,) * len(array.shape)
    return pl.BlockSpec(array.shape, lambda i, info: zeros)


def call(body, info, ins, in_specs, outs, out_specs, scratch, grid=1, us=1, waits=()):
    if waits:
        first, _ = lax.optimization_barrier((ins[0], list(waits)))
        ins = [first] + list(ins[1:])
    return pl.pallas_call(
        body,
        grid_spec=pltpu.PrefetchScalarGridSpec(
            num_scalar_prefetch=1,
            grid=(grid,),
            in_specs=in_specs,
            out_specs=out_specs,
            scratch_shapes=[pltpu.VMEM(shape, kind) for shape, kind in scratch],
        ),
        out_shape=outs,
        compiler_params=pltpu.CompilerParams(
            dimension_semantics=("arbitrary",), vmem_limit_bytes=VMEM_LIMIT
        ),
        cost_estimate=pl.CostEstimate(
            flops=int(us * 1.15e9), bytes_accessed=int(us * 1e5), transcendentals=0
        ),
    )(info, *ins)


def swap(value, axis, groups=None):
    return lax.all_to_all(value, axis, 0, 0, axis_index_groups=groups, tiled=True)


def share_kernel(part, nt):
    others = nt // GROUP
    got = [part]
    for s in range(1, others):
        got.append(lax.ppermute(part, "tok", [(i, (i + s * GROUP) % nt) for i in range(nt)]))
    return got


class Reduction:
    def __init__(self, packed, info, rows, nc, nt):
        self.packed, self.info, self.rows, self.nc, self.nt = packed, info, rows, nc, nt
        self.quarter, self.share = rows // nc, rows // (nc * nt)

    def cross(self, values):
        return [values[0]] + [
            lax.ppermute(values[s], "cells", [(i, i ^ s) for i in range(self.nc)])
            for s in range(1, self.nc)
        ]

    def total(self, parts, waits):
        parts, _ = lax.optimization_barrier((parts, waits))
        total = parts[0].astype(F32)
        for part in parts[1:]:
            total = total + part.astype(F32)
        return total.astype(BF)

    def over_cells(self):
        self.one = self.cross(self.packed)

    def over_tok(self, waits):
        mine = self.total(self.one, waits)
        self.two = swap(mine.reshape(self.nt, self.share, 128), "tok")
        return mine

    def back_tok(self, waits):
        two, _ = lax.optimization_barrier((self.two, waits))
        mine = self.total([two[k] for k in range(self.nt)], [])
        mine = jnp.broadcast_to(mine[None], (self.nt,) + mine.shape)
        self.three = swap(mine, "tok")
        return mine

    def back_cells(self):
        self.four = self.cross([self.three.reshape(self.quarter, 128)] * self.nc)

    def results(self, block, pieces, sums, smalls, waits=(), extras=()):
        outs = [jax.ShapeDtypeStruct((D, width), F32) for _, width in pieces]
        outs += [jax.ShapeDtypeStruct((8, 128), F32) for _ in sums]
        outs += [jax.ShapeDtypeStruct((1, width), F32) for _, width in smalls]
        outs = call(
            unpack_body(self.nc, block, pieces, sums, smalls, len(extras)), self.info,
            self.four + list(extras), [whole(v) for v in self.four + list(extras)], outs, [whole(v) for v in outs], [((self.rows, 128), F32)],
            us=0.02, waits=waits,
        )
        return outs[: len(pieces)], outs[len(pieces) :]


def padded_rows(need, nc, nt):
    unit = nc * nt * 16
    return -(-need // unit) * unit


def shards(
    tokens, cotangent, gene_count, expressed, projection, first_gain, first_bias, query_weight,
    key_weight, value_weight, out_weight, out_bias, second_gain, second_bias, up_weight, up_bias,
    down_weight, down_bias,
):
    cells, _, slots = tokens.shape
    turns = cells // GROUP
    steps, lanes = GROUP // STEP, STEP * slots
    nt, nc = lax.axis_size("tok"), lax.axis_size("cells")
    position = lax.axis_index("tok")
    groups = [[g * GROUP + i for i in range(GROUP)] for g in range(nt // GROUP)]
    info = jnp.stack([lax.axis_index("cells"), position % GROUP]).astype(jnp.int32)

    slot_index = position * slots + lax.broadcasted_iota(jnp.int32, (cells, slots), 1)
    alive = ((slot_index < gene_count[:, None]) & (expressed > 0)).astype(BF)
    marks = jnp.pad(alive[:, None, :], ((0, 0), (0, DX - D - 1), (0, 0)))

    def turn_of(array, c):
        return array[c * GROUP : (c + 1) * GROUP]

    def to_cells(c):
        return swap(jnp.concatenate([turn_of(tokens, c), turn_of(marks, c)], axis=1), "tok", groups)

    x = [to_cells(0)]

    vectors = [first_gain, first_bias, second_gain, second_bias, out_bias, down_bias, up_bias]
    vec = jnp.stack([jnp.pad(v, (0, FF - v.shape[0])) for v in vectors + [jnp.zeros((FF,), F32)]])
    outs = [jax.ShapeDtypeStruct((FF, 8), F32)] + [
        jax.ShapeDtypeStruct(shape, BF)
        for shape in (
            (INNER, DX), (D, 2 * INNER), (2 * INNER, DX), (INNER, D), (FF, DX), (FF, D),
            (MAIN, HEAD_SIZE), (LEFT, INNER), (EXT, MAIN), (HEADS * EXT, LEFT),
        )
    ]
    wot = out_weight.T
    ins = [
        vec, projection.T, query_weight, key_weight, value_weight, wot, up_weight, down_weight,
    ]
    cols, wqt, wkv, wkvt, wo, upt, downt, pm, left_proj, tm, tl = call(
        prep_body, info, ins, [whole(v) for v in ins], outs, [whole(v) for v in outs], [], us=4,
    )

    tokens, marks, cols = lax.optimization_barrier((tokens, marks, cols))
    x += [to_cells(c) for c in range(1, turns)]
    x_spec = pl.BlockSpec((STEP, DX, slots), lambda j, info: (j, 0, 0))

    def step_spec(rows):
        return pl.BlockSpec((1, rows, lanes), lambda j, info: (j, 0, 0))

    k_out = jax.ShapeDtypeStruct((KROWS, MAIN), BF)
    k_acc = ((KROWS, MAIN), F32)
    key_scratch = [
        ((INNER, lanes), BF), ((HEADS * EXT, lanes), BF), ((HEADS * MAIN, lanes), BF),
        ((LEFT, lanes), BF), ((16, lanes), F32),
    ]
    kernels, dy = [], []
    for c in range(turns):
        ins = [x[c], cols, wkvt, pm, left_proj]
        part = call(
            first_body, info, ins, [x_spec] + [whole(v) for v in ins[1:]],
            k_out, whole(k_out), [k_acc] + key_scratch, grid=steps, us=12,
        )
        mine, part = lax.optimization_barrier((turn_of(cotangent, c), part))
        kernels.append(share_kernel(part, nt))
        dy.append(swap(mine, "tok", groups))

    token_out = jax.ShapeDtypeStruct((GROUP, D, slots), BF)
    token_spec = pl.BlockSpec((STEP, D, slots), lambda j, info: (j, 0, 0))
    wide_out = jax.ShapeDtypeStruct((steps, D, lanes), BF)
    common = [
        ((HEADS * EXT, lanes), BF), ((HEADS * MAIN, lanes), BF), ((LEFT, lanes), BF),
        ((16, lanes), F32), ((HEADS * EXT, MAIN), BF), ((HEADS * EXT, LEFT), BF),
        ((HEADS * EXT, lanes), F32),
    ]
    weights = [
        cols, wqt, query_weight, wot, wo, upt, up_weight, downt, down_weight,
        pm, left_proj, tm, tl,
    ]
    rows2 = padded_rows(GRAD2 + 2 * SMALL2, nc, nt)
    sums = [((GRAD2, 128), F32), ((SMALL2 * D, 128), F32)]
    mixed_grads, query_grads, kernel_grads = [], [], []
    results, sums2 = [], []
    for c in range(turns):
        start, last = c == 0, c == turns - 1
        fixed = kernels[c] + sums2 + weights
        if last:
            sum_outs = [jax.ShapeDtypeStruct((rows2 // nc, 128), BF)] * nc
            sum_scratch = [((rows2, 128), F32)] + sums
        else:
            sum_outs = [jax.ShapeDtypeStruct(shape, kind) for shape, kind in sums]
            sum_scratch = []
        out, gmix, gnq, kg, *sums2 = call(
            second_body(len(kernels[c]), start, nc if last else 0, HEADS if start else UNROLL), info, [x[c], dy[c]] + fixed,
            [x_spec, token_spec] + [whole(v) for v in fixed],
            [token_out, wide_out, wide_out, k_out] + sum_outs,
            [token_spec, step_spec(D), step_spec(D)] + [whole(v) for v in [k_out] + sum_outs],
            sum_scratch + [((KROWS, MAIN), BF), k_acc, ((INNER, lanes), BF), ((INNER, lanes), BF)]
            + common
            + [
                ((INNER, lanes), BF), ((16, lanes), F32), ((FF, lanes), BF), ((FF, lanes), BF),
                ((DX, lanes), BF), ((DX, lanes), BF),
            ],
            grid=steps, us=40,
        )
        results.append(swap(out, "tok", groups))
        mixed_grads.append(gmix)
        query_grads.append(gnq)
        kernel_grads.append(share_kernel(kg, nt))
    reduce2 = Reduction(sums2, info, rows2, nc, nt)
    reduce2.over_cells()

    rows3 = padded_rows(2 * Q_BLOCKS * D + 2 * SMALL3, nc, nt)
    weights = [cols, wkvt, wkv, pm, left_proj, tm, tl]
    normed_grads, sums3 = [], []
    waits = [sums2[0], results[0]]
    for c in range(turns):
        start, last = c == 0, c == turns - 1
        fixed = kernel_grads[c] + sums3 + weights
        if last:
            sum_outs = [jax.ShapeDtypeStruct((rows3 // nc, 128), BF)] * nc
            sum_scratch = [((rows3, 128), F32), ((GRAD3, 128), F32), ((SMALL3 * D, 128), F32)]
        else:
            sum_outs = [jax.ShapeDtypeStruct((GRAD3, 128), F32)]
            sum_scratch = []
        got, *sums3 = call(
            third_body(len(kernel_grads[c]), start, nc if last else 0), info,
            [x[c], query_grads[c]] + fixed, [x_spec, step_spec(D)] + [whole(v) for v in fixed],
            [wide_out] + sum_outs, [step_spec(D)] + [whole(v) for v in sum_outs],
            sum_scratch
            + [((KROWS, MAIN), BF), ((INNER, lanes), BF), ((2 * INNER, lanes), BF)] + common
            + [((DX, lanes), BF)],
            grid=steps, us=22, waits=waits,
        )
        normed_grads.append(got)
        if start:
            waits = [reduce2.over_tok([got, results[-1]] + kernel_grads[-1][1:])]
    reduce3 = Reduction(sums3, info, rows3, nc, nt)
    reduce3.over_cells()
    waits = [sums3[0], results[-1], reduce2.back_tok([sums3[0]])]
    one_out = jax.ShapeDtypeStruct((1, D, slots), BF)
    grads = []
    for c in range(turns):
        ins = [x[c], dy[c], mixed_grads[c], normed_grads[c], cols]

        def pair(rows, blocks=STEP, columns=slots):
            return pl.BlockSpec(
                (blocks, rows, columns), lambda j, info: (jnp.bitwise_xor(info[1] // STEP, j), 0, 0)
            )

        specs = [pair(DX), pair(D), pair(D, 1, lanes), pair(D, 1, lanes), whole(cols)]
        out = call(
            last_body, info, ins, specs, [one_out] * GROUP,
            [whole(one_out)] * GROUP, [], grid=steps, us=6, waits=waits,
        )
        if c == turns - 1:
            reduce2.back_cells()
            mine = reduce3.back_tok([out[0]] + reduce2.four[1:3] + grads[1:])
            out, _ = lax.optimization_barrier((out, mine))
        grads += [out[0]] + [
            lax.ppermute(out[s], "tok", [(i, i - i % GROUP + (i % GROUP ^ s)) for i in range(nt)])
            for s in range(1, GROUP)
        ]
        if c == 0:
            waits = [reduce3.over_tok([out[0]]), reduce2.three]
    (dwq, dwot, dup, ddown), (upb, gain2, bias2, outb, downb, gain1q, bias1q) = reduce2.results(
        DX, [(WQ_AT, INNER), (WO_AT, INNER), (UP_AT, FF), (DOWN_AT, FF)], [(UP_AT, FF)],
        [(GRAD2 + 2 * k, D) for k in range(SMALL2)], waits=[mine],
    )
    reduce3.three, _ = lax.optimization_barrier((reduce3.three, gain1q))
    reduce3.back_cells()

    result = jnp.concatenate(results, axis=0)
    grad_in = call(
        place_body, info, grads, [whole(v) for v in grads], jax.ShapeDtypeStruct((cells, D, slots), BF),
        pl.BlockSpec((cells, D, slots), lambda i, info: (0, 0, 0)), [], us=0.02,
        waits=[reduce3.three],
    )
    (dwk, dwv), (gain1, bias1) = reduce3.results(
        D, [(0, INNER), (Q_BLOCKS, INNER)], [], [(2 * Q_BLOCKS * D + 2 * k, D) for k in range(SMALL3)],
        extras=[gain1q, bias1q], waits=[grad_in],
    )
    return (
        result, grad_in, gain1[0], bias1[0], dwq, dwk, dwv, dwot.T, outb[0],
        gain2[0], bias2[0], dup, upb.reshape(8 * 128)[:FF], ddown, downb[0],
    )


def solution(mesh):
    rows = P("cells", None, "tok")
    placed = (rows, rows, P("cells"), P("cells", "tok")) + (P(),) * 14
    return jax.shard_map(
        shards,
        mesh=mesh,
        in_specs=placed,
        out_specs=(rows, rows) + (P(),) * 13,
        check_vma=False,
    )
```

```python
import math

import jax
import jax.numpy as jnp
from jax import lax
from jax.experimental import pallas as pl
from jax.experimental.pallas import tpu as pltpu
from jax.sharding import PartitionSpec as P

HEADS = 10
HEAD_SIZE = 64
FEATURES = 266
D = 200
INNER = HEADS * HEAD_SIZE
DX = 208
FF = 800
EPSILON = 1e-05

MAIN = 256
REST = FEATURES - MAIN
LEFT = 128
EXT = 80
SUM_ROW = INNER
LEFT_ROW = INNER + 16
KROWS = LEFT_ROW + 48

C0 = HEAD_SIZE ** (-0.25)
LOG2E = 1.0 / math.log(2.0)
RAW_SCALE = C0 * LOG2E
SQ_SCALE = 0.5 * C0 * C0 * LOG2E
SHIFT = -0.5 * math.log2(FEATURES)
FF_CHUNK = 160
Q_BLOCKS = INNER // 128
F_BLOCKS = -(-FF // 128)
WQ_AT, WO_AT, UP_AT, DOWN_AT = 0, Q_BLOCKS, 2 * Q_BLOCKS, 2 * Q_BLOCKS + F_BLOCKS
GRAD2 = (2 * Q_BLOCKS + 2 * F_BLOCKS) * DX
GRAD3 = 2 * Q_BLOCKS * DX
SMALL2 = 6
SMALL3 = 2

BF = jnp.bfloat16
F32 = jnp.float32
VMEM_LIMIT = 56 * 1024 * 1024
SMALL_LIMIT = 24 * 1024 * 1024
GROUP = 4
STEP = 2
UNROLL = 5


def dot(left, right):
    return jnp.dot(left, right, preferred_element_type=F32)


def dot_nt(left, right):
    return lax.dot_general(left, right, (((1,), (1,)), ((), ())), preferred_element_type=F32)


def dot_tn(left, right):
    return lax.dot_general(left, right, (((0,), (0,)), ((), ())), preferred_element_type=F32)


def iota(shape, axis):
    return lax.broadcasted_iota(jnp.int32, shape, axis)


def norm_cols(values, gain, bias):
    average = jnp.mean(values, axis=0, keepdims=True)
    centred = values - average
    inverse = lax.rsqrt(jnp.mean(centred * centred, axis=0, keepdims=True) + EPSILON)
    normed = centred * inverse
    return normed * gain + bias, normed, inverse


def norm_cols_back(grad_out, normed, inverse, gain):
    scaled = grad_out * gain
    return inverse * (
        scaled
        - jnp.mean(scaled, axis=0, keepdims=True)
        - normed * jnp.mean(scaled * normed, axis=0, keepdims=True)
    )


def lane_sums(values):
    total = values[:, :128]
    for start in range(128, values.shape[1], 128):
        total = total + values[:, start : start + 128]
    return total


def ext_rows(h):
    return pl.ds(pl.multiple_of(h * EXT, 16), EXT)


def val_rows(h):
    return pl.ds(pl.multiple_of(h * EXT, 16), HEAD_SIZE)


def main_rows(h):
    return pl.ds(pl.multiple_of(h * MAIN, MAIN), MAIN)


def head_rows(h):
    return pl.ds(pl.multiple_of(h * HEAD_SIZE, HEAD_SIZE), HEAD_SIZE)


def one_row(h):
    return pl.ds(h, 1)


def for_heads(step, unroll=HEADS):
    def turn(i, _):
        for k in range(unroll):
            step(i * unroll + k)
        return 0

    if unroll == HEADS:
        turn(0, 0)
    else:
        lax.fori_loop(0, HEADS // unroll, turn, 0)


G1, B1, G2, B2, OB, DB, UB = range(7)


def column(cols_ref, which, rows=D):
    return cols_ref[0:rows, which : which + 1]


def prep_body(
    info_ref, vec_ref, projt_ref, wq_ref, wk_ref, wv_ref, wot_ref, up_ref, down_ref,
    cols_ref, wqt_ref, wkv_ref, wkvt_ref, wo_ref, upt_ref, downt_ref,
    pm_ref, pl_ref, tm_ref, tl_ref,
):
    cols_ref[...] = vec_ref[...].T
    def padded(matrix):
        return jnp.concatenate([matrix.T, jnp.zeros((matrix.shape[1], DX - D), BF)], axis=1)

    wqt_ref[...] = padded(wq_ref[...])
    wkv_ref[:, :INNER] = wk_ref[...]
    wkv_ref[:, INNER:] = wv_ref[...]
    wkvt_ref[:INNER] = padded(wk_ref[...])
    wkvt_ref[INNER:] = padded(wv_ref[...])
    wo_ref[...] = wot_ref[...].T
    upt_ref[...] = padded(up_ref[...])
    downt_ref[...] = down_ref[...].T
    proj = projt_ref[...].T

    def one_hot(shape, mask):
        return jnp.where(mask, 1.0, 0.0).astype(BF)

    pm_ref[...] = proj[:MAIN]
    s = (16, FEATURES)
    rest = dot(one_hot(s, (iota(s, 0) + MAIN == iota(s, 1)) & (iota(s, 0) < REST)), proj).astype(BF)
    s = (HEAD_SIZE, INNER)
    wide = dot(rest, one_hot(s, iota(s, 0) == iota(s, 1) % HEAD_SIZE)).astype(BF)
    s = (LEFT, 16)
    tall = dot(one_hot(s, iota(s, 0) % REST == iota(s, 1)), wide)
    s = (LEFT, INNER)
    pl_ref[...] = jnp.where(iota(s, 0) // REST == iota(s, 1) // HEAD_SIZE, tall, 0.0).astype(BF)
    s = (EXT, HEAD_SIZE)
    pick = one_hot(s, iota(s, 0) == iota(s, 1))
    s = (EXT, MAIN)
    tm_ref[...] = jnp.where(iota(s, 0) == HEAD_SIZE, 1.0, dot_nt(pick, proj[:MAIN])).astype(BF)
    s = (EXT, 16)
    rest_ext = jnp.where(iota(s, 0) == HEAD_SIZE, 1.0, dot_nt(pick, rest)).astype(BF)
    s = (16, LEFT)
    spread = dot(rest_ext, one_hot(s, iota(s, 0) == iota(s, 1) % REST))
    s = (EXT, LEFT)
    for h in range(HEADS):
        tl_ref[ext_rows(h), :] = jnp.where(iota(s, 1) // REST == h, spread, 0.0).astype(BF)


def shifts_of(u_ref, s_ref):
    for h in range(HEADS):
        wide = u_ref[head_rows(h), :].astype(F32)
        s_ref[h : h + 1, :] = SHIFT - SQ_SCALE * jnp.sum(wide * wide, axis=0, keepdims=True)


def left_features(u_ref, phil_ref, s_ref, pl_ref):
    shape = (LEFT, u_ref.shape[1])
    owner = iota(shape, 0) // REST
    shifts = jnp.zeros(shape, F32)
    for h in range(HEADS):
        shifts = jnp.where(owner == h, s_ref[h : h + 1, :], shifts)
    phil_ref[...] = jnp.exp2(dot(pl_ref[...], u_ref[...]) * RAW_SCALE + shifts).astype(BF)


def main_features(h, u_ref, phi_ref, s_ref, pm_ref):
    raw = dot(pm_ref[...], u_ref[head_rows(h), :])
    phi_ref[main_rows(h), :] = jnp.exp2(raw * RAW_SCALE + s_ref[one_row(h), :]).astype(BF)


def add_head_kernel(h, acc_ref, ext_ref, phi_ref):
    total = dot_nt(ext_ref[ext_rows(h), :], phi_ref[main_rows(h), :])
    acc_ref[head_rows(h), :] += total[:HEAD_SIZE]
    acc_ref[one_row(SUM_ROW + h), :] += total[HEAD_SIZE : HEAD_SIZE + 1]


def add_left_kernel(acc_ref, ext_ref, phil_ref):
    every = dot_nt(ext_ref[...], phil_ref[...])
    owner = iota((EXT, LEFT), 1) // REST
    left = jnp.zeros((EXT, LEFT), F32)
    for h in range(HEADS):
        left = jnp.where(owner == h, every[h * EXT : (h + 1) * EXT], left)
    acc_ref[LEFT_ROW:KROWS, 0:LEFT] += left[:48]
    acc_ref[LEFT_ROW : LEFT_ROW + 32, LEFT:MAIN] += left[48:EXT]


def sum_kernels(in_refs, whole_ref):
    total = in_refs[0][...].astype(F32)
    for ref in in_refs[1:]:
        total = total + ref[...].astype(F32)
    whole_ref[...] = total.astype(BF)


def read_kernel(whole_ref, kt_ref, kl_ref):
    sums = whole_ref[SUM_ROW : SUM_ROW + 16, :].astype(F32)
    first = iota((16, MAIN), 0) == 0
    left = jnp.concatenate(
        [whole_ref[LEFT_ROW:KROWS, 0:LEFT], whole_ref[LEFT_ROW : LEFT_ROW + 32, LEFT:MAIN]], axis=0
    ).astype(F32)
    owner = iota((EXT, LEFT), 1) // REST
    for h in range(HEADS):
        kt_ref[val_rows(h), :] = whole_ref[head_rows(h), :]
        kt_ref[h * EXT + HEAD_SIZE : (h + 1) * EXT, :] = jnp.where(
            first, sums[h : h + 1, :], 0.0
        ).astype(BF)
        kl_ref[ext_rows(h), :] = jnp.where(owner == h, left, 0.0).astype(BF)


def left_grads(phil_ref, kl_ref, ext_ref, tl_ref, wide_ref):
    phil_ref[...] = (dot_tn(kl_ref[...], ext_ref[...]) * phil_ref[...].astype(F32)).astype(BF)
    wide_ref[...] = dot(tl_ref[...], phil_ref[...])


def weigh(h, phi_ref, kt_ref, ext_ref):
    grad = dot_tn(kt_ref[ext_rows(h), :], ext_ref[ext_rows(h), :])
    phi_ref[main_rows(h), :] = (grad * phi_ref[main_rows(h), :].astype(F32)).astype(BF)


def main_grads(h, grad_ref, u_ref, phi_ref, tm_ref, wide_ref):
    through = dot(tm_ref[...], phi_ref[main_rows(h), :]) + wide_ref[ext_rows(h), :]
    grad_ref[head_rows(h), :] = (
        C0 * through[:HEAD_SIZE]
        - (C0 * C0) * u_ref[head_rows(h), :].astype(F32) * through[HEAD_SIZE : HEAD_SIZE + 1]
    ).astype(BF)


def with_ones(values):
    rows = iota((DX - D, values.shape[1]), 0)
    return jnp.concatenate([values, jnp.where(rows == 0, 1.0, 0.0)], axis=0).astype(BF)


def side_by_side(ref):
    blocks = [ref[(k,) + (0,) * (len(ref.shape) - 3)] for k in range(STEP)]
    return jnp.concatenate(blocks, axis=1)


def tokens_and_marks(x_ref):
    both = side_by_side(x_ref).astype(F32)
    return both[:D], both[D : D + 1]


def keys_values(normed_low, alive, wkvt_ref, k_ref, ext_ref):
    k_ref[...] = dot(wkvt_ref[:INNER, :], normed_low).astype(BF)
    values = dot(wkvt_ref[INNER:, :], normed_low)
    mark = jnp.where(iota((16, values.shape[1]), 0) == 0, alive, 0.0).astype(BF)
    for h in range(HEADS):
        ext_ref[val_rows(h), :] = (values[h * HEAD_SIZE : (h + 1) * HEAD_SIZE] * alive).astype(BF)
        ext_ref[h * EXT + HEAD_SIZE : (h + 1) * EXT, :] = mark


def key_sums(x, alive, cols_ref, wkvt_ref, pm_ref, pl_ref, acc_ref, k_ref, ext_ref, phi_ref, phil_ref, s_ref):
    normed, _, _ = norm_cols(x, column(cols_ref, G1), column(cols_ref, B1))
    keys_values(with_ones(normed), alive, wkvt_ref, k_ref, ext_ref)
    shifts_of(k_ref, s_ref)
    left_features(k_ref, phil_ref, s_ref, pl_ref)
    for_heads(lambda h: main_features(h, k_ref, phi_ref, s_ref, pm_ref))
    for_heads(lambda h: add_head_kernel(h, acc_ref, ext_ref, phi_ref))
    add_left_kernel(acc_ref, ext_ref, phil_ref)


def first_body(info_ref, x_ref, cols_ref, wkvt_ref, pm_ref, pl_ref, out_ref, acc_ref, *scratch):
    @pl.when(pl.program_id(0) == 0)
    def _():
        acc_ref[...] = jnp.zeros_like(acc_ref)

    tokens, alive = tokens_and_marks(x_ref)
    key_sums(tokens, alive, cols_ref, wkvt_ref, pm_ref, pl_ref, acc_ref, *scratch)

    @pl.when(pl.program_id(0) == pl.num_programs(0) - 1)
    def _():
        out_ref[...] = acc_ref[...].astype(BF)


def add_blocks(acc_ref, at, values):
    rows, width = values.shape
    for c in range(-(-width // 128)):
        take = min(128, width - c * 128)
        first = (at + c) * DX
        acc_ref[first : first + rows, 0:take] += values[:, c * 128 : c * 128 + take]


def add_small(small_ref, which, values):
    small_ref[which * D : (which + 1) * D, :] += lane_sums(values)


def add_first_norm(small_ref, which, acc_ref, weight_refs, cols_ref):
    with_normed = jnp.zeros((D, 128), F32)
    alone = jnp.zeros((D, 128), F32)
    block = 0
    for ref in weight_refs:
        for c in range(ref.shape[1] // 128):
            weight = ref[:, c * 128 : (c + 1) * 128].astype(F32)
            first = block * DX
            with_normed += weight * acc_ref[first : first + D, :]
            alone += weight * acc_ref[first + D : first + D + 1, :]
            block += 1
    gain = (with_normed - column(cols_ref, B1) * alone) / column(cols_ref, G1)
    small_ref[which * D : (which + 1) * D, :] = gain
    small_ref[(which + 1) * D : (which + 2) * D, :] = alone


def pack_sums(out_refs, acc_ref, small_ref, flat_ref, me, rows):
    blocks = acc_ref.shape[0] // DX
    base = blocks * rows
    for k in range(blocks):
        flat_ref[k * rows : (k + 1) * rows, :] = acc_ref[k * DX : k * DX + rows, :]
    flat_ref[base:, :] = jnp.zeros((flat_ref.shape[0] - base, 128), F32)
    high = small_ref[...].astype(BF)
    low = (small_ref[...] - high.astype(F32)).astype(BF)
    ones = jnp.ones((8, 128), BF)
    row = base
    for which in range(small_ref.shape[0] // D):
        part = slice(which * D, (which + 1) * D)
        line = dot_nt(ones, high[part]) + dot_nt(ones, low[part])
        flat_ref[row : row + 1, :] = line[0:1, 0:128]
        flat_ref[row + 1 : row + 2, 0 : D - 128] = line[0:1, 128:D]
        row += 2
    rows = out_refs[0].shape[0]
    for s, ref in enumerate(out_refs):
        owner = jnp.bitwise_xor(me, s)
        ref[...] = flat_ref[pl.ds(pl.multiple_of(owner * rows, 16), rows), :].astype(BF)


def put_side_by_side(out_ref, value):
    slots = value.shape[1] // STEP
    for k in range(STEP):
        out_ref[k] = value[:, k * slots : (k + 1) * slots]


def start_sums(start, ins, refs):
    for k, ref in enumerate(refs):
        ref[...] = jnp.zeros_like(ref) if start else ins[k][...]


def second_body(blocks, start, parts, unroll):
    def body(info_ref, x_ref, dy_ref, *rest):
        k_refs, rest = rest[:blocks], rest[blocks:]
        ins = ()
        if not start:
            ins, rest = rest[:2], rest[2:]
        (
            cols_ref, wqt_ref, wq_ref, wot_ref, wo_ref, upt_ref, up_ref, downt_ref, down_ref,
            pm_ref, pl_ref, tm_ref, tl_ref,
        ), rest = rest[:13], rest[13:]
        (out_ref, gmix_ref, gnq_ref, kg_ref), rest = rest[:4], rest[4:]
        if parts:
            packed_refs, (flat_ref, ga_ref, sm_ref, *rest) = rest[:parts], rest[parts:]
        else:
            (ga_ref, sm_ref), rest = rest[:2], rest[2:]
        (
            whole_ref, acc_ref, q_ref, gq_ref, ext_ref, phi_ref, phil_ref, s_ref, kt_ref, kl_ref, wide_ref,
            att_ref, rec_ref, act_ref, gup_ref, n1_ref, n2_ref,
        ) = rest
        j = pl.program_id(0)

        @pl.when(j == 0)
        def _():
            start_sums(start, ins, (ga_ref, sm_ref))
            acc_ref[...] = jnp.zeros_like(acc_ref)
            sum_kernels(k_refs, whole_ref)
            read_kernel(whole_ref, kt_ref, kl_ref)

        tokens, alive = tokens_and_marks(x_ref)
        row_alive = alive > 0
        normed, _, _ = norm_cols(tokens, column(cols_ref, G1), column(cols_ref, B1))
        n1_ref[...] = with_ones(normed)
        q_ref[...] = dot(wqt_ref[...], n1_ref[...]).astype(BF)
        shifts_of(q_ref, s_ref)
        left_features(q_ref, phil_ref, s_ref, pl_ref)
        wide_ref[...] = dot(kl_ref[...], phil_ref[...])
        for_heads(lambda h: main_features(h, q_ref, phi_ref, s_ref, pm_ref))

        def attend(h):
            combined = dot(kt_ref[ext_rows(h), :], phi_ref[main_rows(h), :]) + wide_ref[ext_rows(h), :]
            inverse = 1.0 / jnp.where(row_alive, combined[HEAD_SIZE : HEAD_SIZE + 1], 1.0)
            rec_ref[one_row(h), :] = inverse
            quotient = combined[:HEAD_SIZE] * inverse
            wide_ref[val_rows(h), :] = quotient
            att_ref[head_rows(h), :] = quotient.astype(BF)

        for_heads(attend)
        mixed = tokens + dot(wot_ref[...], att_ref[...]) + column(cols_ref, OB)
        second, second_normed, second_inverse = norm_cols(
            mixed, column(cols_ref, G2), column(cols_ref, B2)
        )
        n2_ref[...] = with_ones(second)
        upstream_wide = jnp.where(row_alive, side_by_side(dy_ref).astype(F32), 0.0)
        upstream = upstream_wide.astype(BF)
        for c in range(FF // FF_CHUNK):
            rows = slice(c * FF_CHUNK, (c + 1) * FF_CHUNK)
            up = dot(upt_ref[rows, :], n2_ref[...]) + cols_ref[rows, UB : UB + 1]
            grad_act = dot(downt_ref[rows, :], upstream)
            half = 0.5 * (1.0 + lax.erf(up * 0.7071067811865476))
            act_ref[rows, :] = (up * half).astype(BF)
            slope = half + up * jnp.exp(-0.5 * up * up) * 0.3989422804014327
            grad_up = (grad_act * slope).astype(BF)
            gup_ref[rows, :] = grad_up
        result = mixed + dot(down_ref[...], act_ref[...]) + column(cols_ref, DB)
        put_side_by_side(out_ref, jnp.where(row_alive, result, tokens).astype(BF))

        add_small(sm_ref, 3, upstream_wide)
        grad_second = dot(up_ref[...], gup_ref[...])
        add_blocks(ga_ref, DOWN_AT, dot_nt(upstream, act_ref[...]))
        add_small(sm_ref, 0, grad_second * second_normed)
        add_small(sm_ref, 1, grad_second)
        grad_mixed = upstream_wide + norm_cols_back(
            grad_second, second_normed, second_inverse, column(cols_ref, G2)
        )
        gmix_ref[0] = grad_mixed.astype(BF)
        grad_branch = grad_mixed.astype(BF)
        add_small(sm_ref, 2, grad_branch.astype(F32))
        pad_row = iota((16, alive.shape[1]), 0) == 0
        grad_att = dot(wo_ref[...], grad_branch)
        add_blocks(ga_ref, UP_AT, dot_nt(n2_ref[...], gup_ref[...]))
        add_blocks(ga_ref, WO_AT, dot_nt(grad_branch, att_ref[...]))
        for h in range(HEADS):
            grad_head = grad_att[h * HEAD_SIZE : (h + 1) * HEAD_SIZE]
            inverse = rec_ref[h : h + 1, :]
            ext_ref[val_rows(h), :] = (grad_head * inverse).astype(BF)
            grad_sum = -inverse * jnp.sum(grad_head * wide_ref[val_rows(h), :], axis=0, keepdims=True)
            ext_ref[h * EXT + HEAD_SIZE : (h + 1) * EXT, :] = jnp.where(pad_row, grad_sum, 0.0).astype(BF)
        add_left_kernel(acc_ref, ext_ref, phil_ref)
        left_grads(phil_ref, kl_ref, ext_ref, tl_ref, wide_ref)
        for_heads(lambda h: add_head_kernel(h, acc_ref, ext_ref, phi_ref))
        for_heads(lambda h: weigh(h, phi_ref, kt_ref, ext_ref))
        for_heads(lambda h: main_grads(h, gq_ref, q_ref, phi_ref, tm_ref, wide_ref), unroll)
        add_blocks(ga_ref, WQ_AT, dot_nt(n1_ref[...], gq_ref[...]))
        gnq_ref[0] = dot(wq_ref[...], gq_ref[...]).astype(BF)

        @pl.when(j == pl.num_programs(0) - 1)
        def _():
            kg_ref[...] = acc_ref[...].astype(BF)
            if parts:
                add_first_norm(sm_ref, 4, ga_ref, [wq_ref], cols_ref)
                pack_sums(packed_refs, ga_ref, sm_ref, flat_ref, info_ref[0], DX)

    return body


def third_body(blocks, start, parts):
    def body(info_ref, x_ref, gnq_ref, *rest):
        k_refs, rest = rest[:blocks], rest[blocks:]
        ins = ()
        if not start:
            ins, rest = rest[:1], rest[1:]
        (cols_ref, wkvt_ref, wkv_ref, pm_ref, pl_ref, tm_ref, tl_ref), rest = rest[:7], rest[7:]
        gn_ref, rest = rest[0], rest[1:]
        if parts:
            packed_refs, (flat_ref, ga_ref, sm_ref, *rest) = rest[:parts], rest[parts:]
        else:
            ga_ref, rest = rest[0], rest[1:]
        (
            whole_ref, k_ref, gkv_ref, ext_ref, phi_ref, phil_ref, s_ref, kt_ref, kl_ref, wide_ref, n1_ref,
        ) = rest

        @pl.when(pl.program_id(0) == 0)
        def _():
            start_sums(start, ins, (ga_ref,))
            sum_kernels(k_refs, whole_ref)
            read_kernel(whole_ref, kt_ref, kl_ref)

        tokens, alive = tokens_and_marks(x_ref)
        normed, _, _ = norm_cols(tokens, column(cols_ref, G1), column(cols_ref, B1))
        n1_ref[...] = with_ones(normed)
        keys_values(n1_ref[...], alive, wkvt_ref, k_ref, ext_ref)
        shifts_of(k_ref, s_ref)
        left_features(k_ref, phil_ref, s_ref, pl_ref)
        wide_ref[...] = dot(kl_ref[...], phil_ref[...])
        for_heads(lambda h: main_features(h, k_ref, phi_ref, s_ref, pm_ref))

        def value_grads(h):
            grad = dot(kt_ref[val_rows(h), :], phi_ref[main_rows(h), :]) + wide_ref[val_rows(h), :]
            gkv_ref[head_rows(HEADS + h), :] = (grad * alive).astype(BF)

        for_heads(value_grads)
        left_grads(phil_ref, kl_ref, ext_ref, tl_ref, wide_ref)
        for_heads(lambda h: weigh(h, phi_ref, kt_ref, ext_ref))
        for_heads(lambda h: main_grads(h, gkv_ref, k_ref, phi_ref, tm_ref, wide_ref))
        add_blocks(ga_ref, 0, dot_nt(n1_ref[...], gkv_ref[...]))
        gn_ref[0] = (gnq_ref[0].astype(F32) + dot(wkv_ref[...], gkv_ref[...])).astype(BF)

        if parts:

            @pl.when(pl.program_id(0) == pl.num_programs(0) - 1)
            def _():
                add_first_norm(sm_ref, 0, ga_ref, [wkv_ref], cols_ref)
                pack_sums(packed_refs, ga_ref, sm_ref, flat_ref, info_ref[0], D)

    return body


def last_body(info_ref, x_ref, dy_ref, gmix_ref, gn_ref, cols_ref, *rest):
    out_refs = rest[-GROUP:]
    tokens, alive = tokens_and_marks(x_ref)
    _, normed, inverse = norm_cols(tokens, column(cols_ref, G1), column(cols_ref, B1))
    grad_in = gmix_ref[0].astype(F32) + norm_cols_back(gn_ref[0].astype(F32), normed, inverse, column(cols_ref, G1))
    grad_in = jnp.where(alive > 0, grad_in, side_by_side(dy_ref).astype(F32))
    slots = grad_in.shape[1] // STEP
    odd = lax.rem(info_ref[1], 2) == 1
    first, second = grad_in[:, :slots], grad_in[:, slots:]
    first, second = jnp.where(odd, second, first).astype(BF), jnp.where(odd, first, second).astype(BF)
    for k in range(GROUP // STEP):

        @pl.when(pl.program_id(0) == k)
        def _():
            out_refs[STEP * k][0] = first
            out_refs[STEP * k + 1][0] = second


def place_body(info_ref, *refs):
    out_ref = refs[-1]
    for k, ref in enumerate(refs[:-1]):
        cell = k // GROUP * GROUP + jnp.bitwise_xor(info_ref[1], k % GROUP)
        out_ref[pl.ds(cell, 1)] = ref[...]


def unpack_body(count, block, pieces, sums, smalls, extras):
    def body(info_ref, *rest):
        in_refs, whole_ref = rest[:count], rest[-1]
        out_refs = list(rest[-1 - len(pieces) - len(sums) - len(smalls) : -1])
        rows = in_refs[0].shape[0]
        for s, ref in enumerate(in_refs):
            owner = jnp.bitwise_xor(info_ref[0], s)
            whole_ref[pl.ds(pl.multiple_of(owner * rows, 16), rows), :] = ref[...].astype(F32)
        for at, width in pieces:
            ref = out_refs.pop(0)
            for c in range(-(-width // 128)):
                take = min(128, width - c * 128)
                first = (at + c) * block
                ref[:, c * 128 : c * 128 + take] = whole_ref[first : first + D, 0:take]
        for at, width in sums:
            ref = out_refs.pop(0)
            ref[...] = jnp.zeros_like(ref)
            for c in range(-(-width // 128)):
                first = (at + c) * block + D
                ref[c : c + 1, :] = whole_ref[first : first + 1, :]
        for k, (row, width) in enumerate(smalls):
            ref = out_refs.pop(0)
            line = jnp.concatenate(
                [whole_ref[row : row + 1, :], whole_ref[row + 1 : row + 2, 0 : width - 128]], axis=1
            )
            ref[...] = line + rest[count + k][...] if k < extras else line

    return body


def whole(array):
    zeros = (0,) * len(array.shape)
    return pl.BlockSpec(array.shape, lambda i, info: zeros)


def call(body, info, ins, in_specs, outs, out_specs, scratch, grid=1, us=1, waits=(), limit=VMEM_LIMIT):
    if waits:
        first, _ = lax.optimization_barrier((ins[0], list(waits)))
        ins = [first] + list(ins[1:])
    return pl.pallas_call(
        body,
        grid_spec=pltpu.PrefetchScalarGridSpec(
            num_scalar_prefetch=1,
            grid=(grid,),
            in_specs=in_specs,
            out_specs=out_specs,
            scratch_shapes=[pltpu.VMEM(shape, kind) for shape, kind in scratch],
        ),
        out_shape=outs,
        compiler_params=pltpu.CompilerParams(
            dimension_semantics=("arbitrary",), vmem_limit_bytes=limit
        ),
        cost_estimate=pl.CostEstimate(
            flops=int(us * 1.15e9), bytes_accessed=int(us * 1e5), transcendentals=0
        ),
    )(info, *ins)


def swap(value, axis, groups=None):
    return lax.all_to_all(value, axis, 0, 0, axis_index_groups=groups, tiled=True)


def share_kernel(part, nt):
    others = nt // GROUP
    got = [part]
    for s in range(1, others):
        got.append(lax.ppermute(part, "tok", [(i, (i + s * GROUP) % nt) for i in range(nt)]))
    return got


class Reduction:
    def __init__(self, packed, info, rows, nc, nt):
        self.packed, self.info, self.rows, self.nc, self.nt = packed, info, rows, nc, nt
        self.quarter, self.share = rows // nc, rows // (nc * nt)

    def cross(self, values):
        return [values[0]] + [
            lax.ppermute(values[s], "cells", [(i, i ^ s) for i in range(self.nc)])
            for s in range(1, self.nc)
        ]

    def total(self, parts, waits):
        parts, _ = lax.optimization_barrier((parts, waits))
        total = parts[0].astype(F32)
        for part in parts[1:]:
            total = total + part.astype(F32)
        return total.astype(BF)

    def over_cells(self):
        self.one = self.cross(self.packed)

    def over_tok(self, waits):
        mine = self.total(self.one, waits)
        self.two = swap(mine.reshape(self.nt, self.share, 128), "tok")
        return mine

    def back_tok(self, waits):
        two, _ = lax.optimization_barrier((self.two, waits))
        mine = self.total([two[k] for k in range(self.nt)], [])
        mine = jnp.broadcast_to(mine[None], (self.nt,) + mine.shape)
        self.three = swap(mine, "tok")
        return mine

    def back_cells(self):
        self.four = self.cross([self.three.reshape(self.quarter, 128)] * self.nc)

    def results(self, block, pieces, sums, smalls, waits=(), extras=()):
        outs = [jax.ShapeDtypeStruct((D, width), F32) for _, width in pieces]
        outs += [jax.ShapeDtypeStruct((8, 128), F32) for _ in sums]
        outs += [jax.ShapeDtypeStruct((1, width), F32) for _, width in smalls]
        outs = call(
            unpack_body(self.nc, block, pieces, sums, smalls, len(extras)), self.info,
            self.four + list(extras), [whole(v) for v in self.four + list(extras)], outs, [whole(v) for v in outs], [((self.rows, 128), F32)],
            us=0.02, waits=waits, limit=SMALL_LIMIT,
        )
        return outs[: len(pieces)], outs[len(pieces) :]


def padded_rows(need, nc, nt):
    unit = nc * nt * 16
    return -(-need // unit) * unit


def shards(
    tokens, cotangent, gene_count, expressed, projection, first_gain, first_bias, query_weight,
    key_weight, value_weight, out_weight, out_bias, second_gain, second_bias, up_weight, up_bias,
    down_weight, down_bias,
):
    cells, _, slots = tokens.shape
    turns = cells // GROUP
    steps, lanes = GROUP // STEP, STEP * slots
    nt, nc = lax.axis_size("tok"), lax.axis_size("cells")
    position = lax.axis_index("tok")
    groups = [[g * GROUP + i for i in range(GROUP)] for g in range(nt // GROUP)]
    info = jnp.stack([lax.axis_index("cells"), position % GROUP]).astype(jnp.int32)

    slot_index = position * slots + lax.broadcasted_iota(jnp.int32, (cells, slots), 1)
    alive = ((slot_index < gene_count[:, None]) & (expressed > 0)).astype(BF)
    marks = jnp.pad(alive[:, None, :], ((0, 0), (0, DX - D - 1), (0, 0)))

    def turn_of(array, c):
        return array[c * GROUP : (c + 1) * GROUP]

    def to_cells(c):
        return swap(jnp.concatenate([turn_of(tokens, c), turn_of(marks, c)], axis=1), "tok", groups)

    x = [to_cells(0)]

    vectors = [first_gain, first_bias, second_gain, second_bias, out_bias, down_bias, up_bias]
    vec = jnp.stack([jnp.pad(v, (0, FF - v.shape[0])) for v in vectors + [jnp.zeros((FF,), F32)]])
    outs = [jax.ShapeDtypeStruct((FF, 8), F32)] + [
        jax.ShapeDtypeStruct(shape, BF)
        for shape in (
            (INNER, DX), (D, 2 * INNER), (2 * INNER, DX), (INNER, D), (FF, DX), (FF, D),
            (MAIN, HEAD_SIZE), (LEFT, INNER), (EXT, MAIN), (HEADS * EXT, LEFT),
        )
    ]
    wot = out_weight.T
    ins = [
        vec, projection.T, query_weight, key_weight, value_weight, wot, up_weight, down_weight,
    ]
    cols, wqt, wkv, wkvt, wo, upt, downt, pm, left_proj, tm, tl = call(
        prep_body, info, ins, [whole(v) for v in ins], outs, [whole(v) for v in outs], [], us=4,
    )

    tokens, marks, cols = lax.optimization_barrier((tokens, marks, cols))
    x += [to_cells(c) for c in range(1, turns)]
    x_spec = pl.BlockSpec((STEP, DX, slots), lambda j, info: (j, 0, 0))

    def step_spec(rows):
        return pl.BlockSpec((1, rows, lanes), lambda j, info: (j, 0, 0))

    k_out = jax.ShapeDtypeStruct((KROWS, MAIN), BF)
    k_acc = ((KROWS, MAIN), F32)
    key_scratch = [
        ((INNER, lanes), BF), ((HEADS * EXT, lanes), BF), ((HEADS * MAIN, lanes), BF),
        ((LEFT, lanes), BF), ((16, lanes), F32),
    ]
    kernels, dy = [], []
    for c in range(turns):
        ins = [x[c], cols, wkvt, pm, left_proj]
        part = call(
            first_body, info, ins, [x_spec] + [whole(v) for v in ins[1:]],
            k_out, whole(k_out), [k_acc] + key_scratch, grid=steps, us=12,
        )
        mine, part = lax.optimization_barrier((turn_of(cotangent, c), part))
        kernels.append(share_kernel(part, nt))
        dy.append(swap(mine, "tok", groups))

    token_out = jax.ShapeDtypeStruct((GROUP, D, slots), BF)
    token_spec = pl.BlockSpec((STEP, D, slots), lambda j, info: (j, 0, 0))
    wide_out = jax.ShapeDtypeStruct((steps, D, lanes), BF)
    common = [
        ((HEADS * EXT, lanes), BF), ((HEADS * MAIN, lanes), BF), ((LEFT, lanes), BF),
        ((16, lanes), F32), ((HEADS * EXT, MAIN), BF), ((HEADS * EXT, LEFT), BF),
        ((HEADS * EXT, lanes), F32),
    ]
    weights = [
        cols, wqt, query_weight, wot, wo, upt, up_weight, downt, down_weight,
        pm, left_proj, tm, tl,
    ]
    rows2 = padded_rows(GRAD2 + 2 * SMALL2, nc, nt)
    sums = [((GRAD2, 128), F32), ((SMALL2 * D, 128), F32)]
    mixed_grads, query_grads, kernel_grads = [], [], []
    results, sums2 = [], []
    for c in range(turns):
        start, last = c == 0, c == turns - 1
        fixed = kernels[c] + sums2 + weights
        if last:
            sum_outs = [jax.ShapeDtypeStruct((rows2 // nc, 128), BF)] * nc
            sum_scratch = [((rows2, 128), F32)] + sums
        else:
            sum_outs = [jax.ShapeDtypeStruct(shape, kind) for shape, kind in sums]
            sum_scratch = []
        out, gmix, gnq, kg, *sums2 = call(
            second_body(len(kernels[c]), start, nc if last else 0, HEADS if start else UNROLL), info, [x[c], dy[c]] + fixed,
            [x_spec, token_spec] + [whole(v) for v in fixed],
            [token_out, wide_out, wide_out, k_out] + sum_outs,
            [token_spec, step_spec(D), step_spec(D)] + [whole(v) for v in [k_out] + sum_outs],
            sum_scratch + [((KROWS, MAIN), BF), k_acc, ((INNER, lanes), BF), ((INNER, lanes), BF)]
            + common
            + [
                ((INNER, lanes), BF), ((16, lanes), F32), ((FF, lanes), BF), ((FF, lanes), BF),
                ((DX, lanes), BF), ((DX, lanes), BF),
            ],
            grid=steps, us=40,
        )
        results.append(swap(out, "tok", groups))
        mixed_grads.append(gmix)
        query_grads.append(gnq)
        kernel_grads.append(share_kernel(kg, nt))
    reduce2 = Reduction(sums2, info, rows2, nc, nt)
    reduce2.over_cells()

    rows3 = padded_rows(2 * Q_BLOCKS * D + 2 * SMALL3, nc, nt)
    weights = [cols, wkvt, wkv, pm, left_proj, tm, tl]
    normed_grads, sums3 = [], []
    waits = [sums2[0], results[0]]
    for c in range(turns):
        start, last = c == 0, c == turns - 1
        fixed = kernel_grads[c] + sums3 + weights
        if last:
            sum_outs = [jax.ShapeDtypeStruct((rows3 // nc, 128), BF)] * nc
            sum_scratch = [((rows3, 128), F32), ((GRAD3, 128), F32), ((SMALL3 * D, 128), F32)]
        else:
            sum_outs = [jax.ShapeDtypeStruct((GRAD3, 128), F32)]
            sum_scratch = []
        got, *sums3 = call(
            third_body(len(kernel_grads[c]), start, nc if last else 0), info,
            [x[c], query_grads[c]] + fixed, [x_spec, step_spec(D)] + [whole(v) for v in fixed],
            [wide_out] + sum_outs, [step_spec(D)] + [whole(v) for v in sum_outs],
            sum_scratch
            + [((KROWS, MAIN), BF), ((INNER, lanes), BF), ((2 * INNER, lanes), BF)] + common
            + [((DX, lanes), BF)],
            grid=steps, us=22, waits=waits,
        )
        normed_grads.append(got)
        if start:
            waits = [reduce2.over_tok([got, results[-1]] + kernel_grads[-1][1:])]
    reduce3 = Reduction(sums3, info, rows3, nc, nt)
    reduce3.over_cells()
    waits = [sums3[0], results[-1], reduce2.back_tok([sums3[0]])]
    one_out = jax.ShapeDtypeStruct((1, D, slots), BF)
    grads = []
    for c in range(turns):
        ins = [x[c], dy[c], mixed_grads[c], normed_grads[c], cols]

        def pair(rows, blocks=STEP, columns=slots):
            return pl.BlockSpec(
                (blocks, rows, columns), lambda j, info: (jnp.bitwise_xor(info[1] // STEP, j), 0, 0)
            )

        specs = [pair(DX), pair(D), pair(D, 1, lanes), pair(D, 1, lanes), whole(cols)]
        out = call(
            last_body, info, ins, specs, [one_out] * GROUP,
            [whole(one_out)] * GROUP, [], grid=steps, us=6, waits=waits,
        )
        if c == turns - 1:
            reduce2.back_cells()
            mine = reduce3.back_tok([out[0]] + reduce2.four[1:3] + grads[1:])
            out, _ = lax.optimization_barrier((out, mine))
        grads += [out[0]] + [
            lax.ppermute(out[s], "tok", [(i, i - i % GROUP + (i % GROUP ^ s)) for i in range(nt)])
            for s in range(1, GROUP)
        ]
        if c == 0:
            waits = [reduce3.over_tok([out[0]]), reduce2.three]
    (dwq, dwot, dup, ddown), (upb, gain2, bias2, outb, downb, gain1q, bias1q) = reduce2.results(
        DX, [(WQ_AT, INNER), (WO_AT, INNER), (UP_AT, FF), (DOWN_AT, FF)], [(UP_AT, FF)],
        [(GRAD2 + 2 * k, D) for k in range(SMALL2)], waits=[mine],
    )
    reduce3.three, _ = lax.optimization_barrier((reduce3.three, gain1q))
    reduce3.back_cells()

    result = jnp.concatenate(results, axis=0)
    grad_in = call(
        place_body, info, grads, [whole(v) for v in grads], jax.ShapeDtypeStruct((cells, D, slots), BF),
        pl.BlockSpec((cells, D, slots), lambda i, info: (0, 0, 0)), [], us=0.02,
        waits=[reduce3.three], limit=SMALL_LIMIT,
    )
    (dwk, dwv), (gain1, bias1) = reduce3.results(
        D, [(0, INNER), (Q_BLOCKS, INNER)], [], [(2 * Q_BLOCKS * D + 2 * k, D) for k in range(SMALL3)],
        extras=[gain1q, bias1q], waits=[grad_in],
    )
    return (
        result, grad_in, gain1[0], bias1[0], dwq, dwk, dwv, dwot.T, outb[0],
        gain2[0], bias2[0], dup, upb.reshape(8 * 128)[:FF], ddown, downb[0],
    )


def solution(mesh):
    rows = P("cells", None, "tok")
    placed = (rows, rows, P("cells"), P("cells", "tok")) + (P(),) * 14
    return jax.shard_map(
        shards,
        mesh=mesh,
        in_specs=placed,
        out_specs=(rows, rows) + (P(),) * 13,
        check_vma=False,
    )
```

```python
import math

import jax
import jax.numpy as jnp
from jax import lax
from jax.experimental import pallas as pl
from jax.experimental.pallas import tpu as pltpu
from jax.sharding import PartitionSpec as P

HEADS = 10
HEAD_SIZE = 64
FEATURES = 266
D = 200
INNER = HEADS * HEAD_SIZE
DX = 208
FF = 800
EPSILON = 1e-05

MAIN = 256
REST = FEATURES - MAIN
LEFT = 128
EXT = 80
SUM_ROW = INNER
LEFT_ROW = INNER + 16
KROWS = LEFT_ROW + 48

C0 = HEAD_SIZE ** (-0.25)
LOG2E = 1.0 / math.log(2.0)
RAW_SCALE = C0 * LOG2E
SQ_SCALE = 0.5 * C0 * C0 * LOG2E
SHIFT = -0.5 * math.log2(FEATURES)
FF_CHUNK = 160
Q_BLOCKS = INNER // 128
F_BLOCKS = -(-FF // 128)
WQ_AT, WO_AT, UP_AT, DOWN_AT = 0, Q_BLOCKS, 2 * Q_BLOCKS, 2 * Q_BLOCKS + F_BLOCKS
GRAD2 = (2 * Q_BLOCKS + 2 * F_BLOCKS) * DX
GRAD3 = 2 * Q_BLOCKS * DX
SMALL2 = 6
SMALL3 = 2

BF = jnp.bfloat16
F32 = jnp.float32
VMEM_LIMIT = 56 * 1024 * 1024
SMALL_LIMIT = 24 * 1024 * 1024
GROUP = 4
STEP = 2
UNROLL = 5


def dot(left, right):
    return jnp.dot(left, right, preferred_element_type=F32)


def dot_nt(left, right):
    return lax.dot_general(left, right, (((1,), (1,)), ((), ())), preferred_element_type=F32)


def dot_tn(left, right):
    return lax.dot_general(left, right, (((0,), (0,)), ((), ())), preferred_element_type=F32)


def iota(shape, axis):
    return lax.broadcasted_iota(jnp.int32, shape, axis)


def norm_cols(values, gain, bias):
    average = jnp.mean(values, axis=0, keepdims=True)
    centred = values - average
    inverse = lax.rsqrt(jnp.mean(centred * centred, axis=0, keepdims=True) + EPSILON)
    normed = centred * inverse
    return normed * gain + bias, normed, inverse


def norm_cols_back(grad_out, normed, inverse, gain):
    scaled = grad_out * gain
    return inverse * (
        scaled
        - jnp.mean(scaled, axis=0, keepdims=True)
        - normed * jnp.mean(scaled * normed, axis=0, keepdims=True)
    )


def lane_sums(values):
    total = values[:, :128]
    for start in range(128, values.shape[1], 128):
        total = total + values[:, start : start + 128]
    return total


def ext_rows(h):
    return pl.ds(pl.multiple_of(h * EXT, 16), EXT)


def val_rows(h):
    return pl.ds(pl.multiple_of(h * EXT, 16), HEAD_SIZE)


def main_rows(h):
    return pl.ds(pl.multiple_of(h * MAIN, MAIN), MAIN)


def head_rows(h):
    return pl.ds(pl.multiple_of(h * HEAD_SIZE, HEAD_SIZE), HEAD_SIZE)


def one_row(h):
    return pl.ds(h, 1)


def for_heads(step, unroll=HEADS):
    def turn(i, _):
        for k in range(unroll):
            step(i * unroll + k)
        return 0

    if unroll == HEADS:
        turn(0, 0)
    else:
        lax.fori_loop(0, HEADS // unroll, turn, 0)


G1, B1, G2, B2, OB, DB, UB = range(7)


def column(cols_ref, which, rows=D):
    return cols_ref[0:rows, which : which + 1]


def prep_body(
    info_ref, vec_ref, projt_ref, wq_ref, wk_ref, wv_ref, wot_ref, up_ref, down_ref,
    cols_ref, wqt_ref, wkv_ref, wkvt_ref, wo_ref, upt_ref, downt_ref,
    pm_ref, pl_ref, tm_ref, tl_ref,
):
    cols_ref[...] = vec_ref[...].T
    def padded(matrix):
        return jnp.concatenate([matrix.T, jnp.zeros((matrix.shape[1], DX - D), BF)], axis=1)

    wqt_ref[...] = padded(wq_ref[...])
    wkv_ref[:, :INNER] = wk_ref[...]
    wkv_ref[:, INNER:] = wv_ref[...]
    wkvt_ref[:INNER] = padded(wk_ref[...])
    wkvt_ref[INNER:] = padded(wv_ref[...])
    wo_ref[...] = wot_ref[...].T
    upt_ref[...] = padded(up_ref[...])
    downt_ref[...] = down_ref[...].T
    proj = projt_ref[...].T

    def one_hot(shape, mask):
        return jnp.where(mask, 1.0, 0.0).astype(BF)

    pm_ref[...] = proj[:MAIN]
    s = (16, FEATURES)
    rest = dot(one_hot(s, (iota(s, 0) + MAIN == iota(s, 1)) & (iota(s, 0) < REST)), proj).astype(BF)
    s = (HEAD_SIZE, INNER)
    wide = dot(rest, one_hot(s, iota(s, 0) == iota(s, 1) % HEAD_SIZE)).astype(BF)
    s = (LEFT, 16)
    tall = dot(one_hot(s, iota(s, 0) % REST == iota(s, 1)), wide)
    s = (LEFT, INNER)
    pl_ref[...] = jnp.where(iota(s, 0) // REST == iota(s, 1) // HEAD_SIZE, tall, 0.0).astype(BF)
    s = (EXT, HEAD_SIZE)
    pick = one_hot(s, iota(s, 0) == iota(s, 1))
    s = (EXT, MAIN)
    tm_ref[...] = jnp.where(iota(s, 0) == HEAD_SIZE, 1.0, dot_nt(pick, proj[:MAIN])).astype(BF)
    s = (EXT, 16)
    rest_ext = jnp.where(iota(s, 0) == HEAD_SIZE, 1.0, dot_nt(pick, rest)).astype(BF)
    s = (16, LEFT)
    spread = dot(rest_ext, one_hot(s, iota(s, 0) == iota(s, 1) % REST))
    s = (EXT, LEFT)
    for h in range(HEADS):
        tl_ref[ext_rows(h), :] = jnp.where(iota(s, 1) // REST == h, spread, 0.0).astype(BF)


def shifts_of(u_ref, s_ref):
    for h in range(HEADS):
        wide = u_ref[head_rows(h), :].astype(F32)
        s_ref[h : h + 1, :] = SHIFT - SQ_SCALE * jnp.sum(wide * wide, axis=0, keepdims=True)


def left_features(u_ref, phil_ref, s_ref, pl_ref):
    shape = (LEFT, u_ref.shape[1])
    owner = iota(shape, 0) // REST
    shifts = jnp.zeros(shape, F32)
    for h in range(HEADS):
        shifts = jnp.where(owner == h, s_ref[h : h + 1, :], shifts)
    phil_ref[...] = jnp.exp2(dot(pl_ref[...], u_ref[...]) * RAW_SCALE + shifts).astype(BF)


def main_features(h, u_ref, phi_ref, s_ref, pm_ref):
    raw = dot(pm_ref[...], u_ref[head_rows(h), :])
    phi_ref[main_rows(h), :] = jnp.exp2(raw * RAW_SCALE + s_ref[one_row(h), :]).astype(BF)


def add_head_kernel(h, acc_ref, ext_ref, phi_ref):
    total = dot_nt(ext_ref[ext_rows(h), :], phi_ref[main_rows(h), :])
    acc_ref[head_rows(h), :] += total[:HEAD_SIZE]
    acc_ref[one_row(SUM_ROW + h), :] += total[HEAD_SIZE : HEAD_SIZE + 1]


def add_left_kernel(acc_ref, ext_ref, phil_ref):
    every = dot_nt(ext_ref[...], phil_ref[...])
    owner = iota((EXT, LEFT), 1) // REST
    left = jnp.zeros((EXT, LEFT), F32)
    for h in range(HEADS):
        left = jnp.where(owner == h, every[h * EXT : (h + 1) * EXT], left)
    acc_ref[LEFT_ROW:KROWS, 0:LEFT] += left[:48]
    acc_ref[LEFT_ROW : LEFT_ROW + 32, LEFT:MAIN] += left[48:EXT]


def sum_kernels(in_refs, whole_ref):
    total = in_refs[0][...].astype(F32)
    for ref in in_refs[1:]:
        total = total + ref[...].astype(F32)
    whole_ref[...] = total.astype(BF)


def read_kernel(whole_ref, kt_ref, kl_ref):
    sums = whole_ref[SUM_ROW : SUM_ROW + 16, :].astype(F32)
    first = iota((16, MAIN), 0) == 0
    left = jnp.concatenate(
        [whole_ref[LEFT_ROW:KROWS, 0:LEFT], whole_ref[LEFT_ROW : LEFT_ROW + 32, LEFT:MAIN]], axis=0
    ).astype(F32)
    owner = iota((EXT, LEFT), 1) // REST
    for h in range(HEADS):
        kt_ref[val_rows(h), :] = whole_ref[head_rows(h), :]
        kt_ref[h * EXT + HEAD_SIZE : (h + 1) * EXT, :] = jnp.where(
            first, sums[h : h + 1, :], 0.0
        ).astype(BF)
        kl_ref[ext_rows(h), :] = jnp.where(owner == h, left, 0.0).astype(BF)


def left_grads(phil_ref, kl_ref, ext_ref, tl_ref, wide_ref):
    phil_ref[...] = (dot_tn(kl_ref[...], ext_ref[...]) * phil_ref[...].astype(F32)).astype(BF)
    wide_ref[...] = dot(tl_ref[...], phil_ref[...])


def weigh(h, phi_ref, kt_ref, ext_ref):
    grad = dot_tn(kt_ref[ext_rows(h), :], ext_ref[ext_rows(h), :])
    phi_ref[main_rows(h), :] = (grad * phi_ref[main_rows(h), :].astype(F32)).astype(BF)


def main_grads(h, grad_ref, u_ref, phi_ref, tm_ref, wide_ref):
    through = dot(tm_ref[...], phi_ref[main_rows(h), :]) + wide_ref[ext_rows(h), :]
    grad_ref[head_rows(h), :] = (
        C0 * through[:HEAD_SIZE]
        - (C0 * C0) * u_ref[head_rows(h), :].astype(F32) * through[HEAD_SIZE : HEAD_SIZE + 1]
    ).astype(BF)


def with_ones(values):
    rows = iota((DX - D, values.shape[1]), 0)
    return jnp.concatenate([values, jnp.where(rows == 0, 1.0, 0.0)], axis=0).astype(BF)


def side_by_side(ref):
    blocks = [ref[(k,) + (0,) * (len(ref.shape) - 3)] for k in range(STEP)]
    return jnp.concatenate(blocks, axis=1)


def tokens_and_marks(x_ref):
    both = side_by_side(x_ref).astype(F32)
    return both[:D], both[D : D + 1]


def keys_values(normed_low, alive, wkvt_ref, k_ref, ext_ref):
    k_ref[...] = dot(wkvt_ref[:INNER, :], normed_low).astype(BF)
    values = dot(wkvt_ref[INNER:, :], normed_low)
    mark = jnp.where(iota((16, values.shape[1]), 0) == 0, alive, 0.0).astype(BF)
    for h in range(HEADS):
        ext_ref[val_rows(h), :] = (values[h * HEAD_SIZE : (h + 1) * HEAD_SIZE] * alive).astype(BF)
        ext_ref[h * EXT + HEAD_SIZE : (h + 1) * EXT, :] = mark


def key_sums(x, alive, cols_ref, wkvt_ref, pm_ref, pl_ref, acc_ref, k_ref, ext_ref, phi_ref, phil_ref, s_ref):
    normed, _, _ = norm_cols(x, column(cols_ref, G1), column(cols_ref, B1))
    keys_values(with_ones(normed), alive, wkvt_ref, k_ref, ext_ref)
    shifts_of(k_ref, s_ref)
    left_features(k_ref, phil_ref, s_ref, pl_ref)
    for_heads(lambda h: main_features(h, k_ref, phi_ref, s_ref, pm_ref))
    for_heads(lambda h: add_head_kernel(h, acc_ref, ext_ref, phi_ref))
    add_left_kernel(acc_ref, ext_ref, phil_ref)


def first_body(info_ref, x_ref, cols_ref, wkvt_ref, pm_ref, pl_ref, out_ref, acc_ref, *scratch):
    @pl.when(pl.program_id(0) == 0)
    def _():
        acc_ref[...] = jnp.zeros_like(acc_ref)

    tokens, alive = tokens_and_marks(x_ref)
    key_sums(tokens, alive, cols_ref, wkvt_ref, pm_ref, pl_ref, acc_ref, *scratch)

    @pl.when(pl.program_id(0) == pl.num_programs(0) - 1)
    def _():
        out_ref[...] = acc_ref[...].astype(BF)


def add_blocks(acc_ref, at, values):
    rows, width = values.shape
    for c in range(-(-width // 128)):
        take = min(128, width - c * 128)
        first = (at + c) * DX
        acc_ref[first : first + rows, 0:take] += values[:, c * 128 : c * 128 + take]


def add_small(small_ref, which, values):
    small_ref[which * D : (which + 1) * D, :] += lane_sums(values)


def add_first_norm(small_ref, which, acc_ref, weight_refs, cols_ref):
    with_normed = jnp.zeros((D, 128), F32)
    alone = jnp.zeros((D, 128), F32)
    block = 0
    for ref in weight_refs:
        for c in range(ref.shape[1] // 128):
            weight = ref[:, c * 128 : (c + 1) * 128].astype(F32)
            first = block * DX
            with_normed += weight * acc_ref[first : first + D, :]
            alone += weight * acc_ref[first + D : first + D + 1, :]
            block += 1
    gain = (with_normed - column(cols_ref, B1) * alone) / column(cols_ref, G1)
    small_ref[which * D : (which + 1) * D, :] = gain
    small_ref[(which + 1) * D : (which + 2) * D, :] = alone


def pack_sums(out_refs, acc_ref, small_ref, flat_ref, me, rows):
    blocks = acc_ref.shape[0] // DX
    base = blocks * rows
    for k in range(blocks):
        flat_ref[k * rows : (k + 1) * rows, :] = acc_ref[k * DX : k * DX + rows, :]
    flat_ref[base:, :] = jnp.zeros((flat_ref.shape[0] - base, 128), F32)
    high = small_ref[...].astype(BF)
    low = (small_ref[...] - high.astype(F32)).astype(BF)
    ones = jnp.ones((8, 128), BF)
    row = base
    for which in range(small_ref.shape[0] // D):
        part = slice(which * D, (which + 1) * D)
        line = dot_nt(ones, high[part]) + dot_nt(ones, low[part])
        flat_ref[row : row + 1, :] = line[0:1, 0:128]
        flat_ref[row + 1 : row + 2, 0 : D - 128] = line[0:1, 128:D]
        row += 2
    rows = out_refs[0].shape[0]
    for s, ref in enumerate(out_refs):
        owner = jnp.bitwise_xor(me, s)
        ref[...] = flat_ref[pl.ds(pl.multiple_of(owner * rows, 16), rows), :].astype(BF)


def put_side_by_side(out_ref, value):
    slots = value.shape[1] // STEP
    for k in range(STEP):
        out_ref[k] = value[:, k * slots : (k + 1) * slots]


def start_sums(start, ins, refs):
    for k, ref in enumerate(refs):
        ref[...] = jnp.zeros_like(ref) if start else ins[k][...]


def second_body(blocks, start, parts, unroll):
    def body(info_ref, x_ref, dy_ref, *rest):
        k_refs, rest = rest[:blocks], rest[blocks:]
        ins = ()
        if not start:
            ins, rest = rest[:2], rest[2:]
        (
            cols_ref, wqt_ref, wq_ref, wot_ref, wo_ref, upt_ref, up_ref, downt_ref, down_ref,
            pm_ref, pl_ref, tm_ref, tl_ref,
        ), rest = rest[:13], rest[13:]
        (out_ref, gmix_ref, gnq_ref, kg_ref), rest = rest[:4], rest[4:]
        if parts:
            packed_refs, (flat_ref, ga_ref, sm_ref, *rest) = rest[:parts], rest[parts:]
        else:
            (ga_ref, sm_ref), rest = rest[:2], rest[2:]
        (
            whole_ref, acc_ref, q_ref, gq_ref, ext_ref, phi_ref, phil_ref, s_ref, kt_ref, kl_ref, wide_ref,
            att_ref, rec_ref, act_ref, gup_ref, n1_ref, n2_ref,
        ) = rest
        j = pl.program_id(0)

        @pl.when(j == 0)
        def _():
            start_sums(start, ins, (ga_ref, sm_ref))
            acc_ref[...] = jnp.zeros_like(acc_ref)
            sum_kernels(k_refs, whole_ref)
            read_kernel(whole_ref, kt_ref, kl_ref)

        tokens, alive = tokens_and_marks(x_ref)
        row_alive = alive > 0
        normed, _, _ = norm_cols(tokens, column(cols_ref, G1), column(cols_ref, B1))
        n1_ref[...] = with_ones(normed)
        q_ref[...] = dot(wqt_ref[...], n1_ref[...]).astype(BF)
        shifts_of(q_ref, s_ref)
        left_features(q_ref, phil_ref, s_ref, pl_ref)
        wide_ref[...] = dot(kl_ref[...], phil_ref[...])
        for_heads(lambda h: main_features(h, q_ref, phi_ref, s_ref, pm_ref))

        def attend(h):
            combined = dot(kt_ref[ext_rows(h), :], phi_ref[main_rows(h), :]) + wide_ref[ext_rows(h), :]
            inverse = 1.0 / jnp.where(row_alive, combined[HEAD_SIZE : HEAD_SIZE + 1], 1.0)
            rec_ref[one_row(h), :] = inverse
            quotient = combined[:HEAD_SIZE] * inverse
            wide_ref[val_rows(h), :] = quotient
            att_ref[head_rows(h), :] = quotient.astype(BF)

        for_heads(attend)
        mixed = tokens + dot(wot_ref[...], att_ref[...]) + column(cols_ref, OB)
        second, second_normed, second_inverse = norm_cols(
            mixed, column(cols_ref, G2), column(cols_ref, B2)
        )
        n2_ref[...] = with_ones(second)
        upstream_wide = jnp.where(row_alive, side_by_side(dy_ref).astype(F32), 0.0)
        upstream = upstream_wide.astype(BF)
        for c in range(FF // FF_CHUNK):
            rows = slice(c * FF_CHUNK, (c + 1) * FF_CHUNK)
            up = dot(upt_ref[rows, :], n2_ref[...]) + cols_ref[rows, UB : UB + 1]
            grad_act = dot(downt_ref[rows, :], upstream)
            half = 0.5 * (1.0 + lax.erf(up * 0.7071067811865476))
            act_ref[rows, :] = (up * half).astype(BF)
            slope = half + up * jnp.exp(-0.5 * up * up) * 0.3989422804014327
            grad_up = (grad_act * slope).astype(BF)
            gup_ref[rows, :] = grad_up
        result = mixed + dot(down_ref[...], act_ref[...]) + column(cols_ref, DB)
        put_side_by_side(out_ref, jnp.where(row_alive, result, tokens).astype(BF))

        add_small(sm_ref, 3, upstream_wide)
        grad_second = dot(up_ref[...], gup_ref[...])
        add_blocks(ga_ref, DOWN_AT, dot_nt(upstream, act_ref[...]))
        add_small(sm_ref, 0, grad_second * second_normed)
        add_small(sm_ref, 1, grad_second)
        grad_mixed = upstream_wide + norm_cols_back(
            grad_second, second_normed, second_inverse, column(cols_ref, G2)
        )
        gmix_ref[0] = grad_mixed.astype(BF)
        grad_branch = grad_mixed.astype(BF)
        add_small(sm_ref, 2, grad_branch.astype(F32))
        pad_row = iota((16, alive.shape[1]), 0) == 0
        grad_att = dot(wo_ref[...], grad_branch)
        add_blocks(ga_ref, UP_AT, dot_nt(n2_ref[...], gup_ref[...]))
        add_blocks(ga_ref, WO_AT, dot_nt(grad_branch, att_ref[...]))
        for h in range(HEADS):
            grad_head = grad_att[h * HEAD_SIZE : (h + 1) * HEAD_SIZE]
            inverse = rec_ref[h : h + 1, :]
            ext_ref[val_rows(h), :] = (grad_head * inverse).astype(BF)
            grad_sum = -inverse * jnp.sum(grad_head * wide_ref[val_rows(h), :], axis=0, keepdims=True)
            ext_ref[h * EXT + HEAD_SIZE : (h + 1) * EXT, :] = jnp.where(pad_row, grad_sum, 0.0).astype(BF)
        add_left_kernel(acc_ref, ext_ref, phil_ref)
        left_grads(phil_ref, kl_ref, ext_ref, tl_ref, wide_ref)
        for_heads(lambda h: add_head_kernel(h, acc_ref, ext_ref, phi_ref))
        for_heads(lambda h: weigh(h, phi_ref, kt_ref, ext_ref), unroll)
        for_heads(lambda h: main_grads(h, gq_ref, q_ref, phi_ref, tm_ref, wide_ref), unroll)
        add_blocks(ga_ref, WQ_AT, dot_nt(n1_ref[...], gq_ref[...]))
        gnq_ref[0] = dot(wq_ref[...], gq_ref[...]).astype(BF)

        @pl.when(j == pl.num_programs(0) - 1)
        def _():
            kg_ref[...] = acc_ref[...].astype(BF)
            if parts:
                add_first_norm(sm_ref, 4, ga_ref, [wq_ref], cols_ref)
                pack_sums(packed_refs, ga_ref, sm_ref, flat_ref, info_ref[0], DX)

    return body


def third_body(blocks, start, parts):
    def body(info_ref, x_ref, gnq_ref, *rest):
        k_refs, rest = rest[:blocks], rest[blocks:]
        ins = ()
        if not start:
            ins, rest = rest[:1], rest[1:]
        (cols_ref, wkvt_ref, wkv_ref, pm_ref, pl_ref, tm_ref, tl_ref), rest = rest[:7], rest[7:]
        gn_ref, rest = rest[0], rest[1:]
        if parts:
            packed_refs, (flat_ref, ga_ref, sm_ref, *rest) = rest[:parts], rest[parts:]
        else:
            ga_ref, rest = rest[0], rest[1:]
        (
            whole_ref, k_ref, gkv_ref, ext_ref, phi_ref, phil_ref, s_ref, kt_ref, kl_ref, wide_ref, n1_ref,
        ) = rest

        @pl.when(pl.program_id(0) == 0)
        def _():
            start_sums(start, ins, (ga_ref,))
            sum_kernels(k_refs, whole_ref)
            read_kernel(whole_ref, kt_ref, kl_ref)

        tokens, alive = tokens_and_marks(x_ref)
        normed, _, _ = norm_cols(tokens, column(cols_ref, G1), column(cols_ref, B1))
        n1_ref[...] = with_ones(normed)
        keys_values(n1_ref[...], alive, wkvt_ref, k_ref, ext_ref)
        shifts_of(k_ref, s_ref)
        left_features(k_ref, phil_ref, s_ref, pl_ref)
        wide_ref[...] = dot(kl_ref[...], phil_ref[...])
        for_heads(lambda h: main_features(h, k_ref, phi_ref, s_ref, pm_ref))

        def value_grads(h):
            grad = dot(kt_ref[val_rows(h), :], phi_ref[main_rows(h), :]) + wide_ref[val_rows(h), :]
            gkv_ref[head_rows(HEADS + h), :] = (grad * alive).astype(BF)

        for_heads(value_grads)
        left_grads(phil_ref, kl_ref, ext_ref, tl_ref, wide_ref)
        for_heads(lambda h: weigh(h, phi_ref, kt_ref, ext_ref))
        for_heads(lambda h: main_grads(h, gkv_ref, k_ref, phi_ref, tm_ref, wide_ref))
        add_blocks(ga_ref, 0, dot_nt(n1_ref[...], gkv_ref[...]))
        gn_ref[0] = (gnq_ref[0].astype(F32) + dot(wkv_ref[...], gkv_ref[...])).astype(BF)

        if parts:

            @pl.when(pl.program_id(0) == pl.num_programs(0) - 1)
            def _():
                add_first_norm(sm_ref, 0, ga_ref, [wkv_ref], cols_ref)
                pack_sums(packed_refs, ga_ref, sm_ref, flat_ref, info_ref[0], D)

    return body


def last_body(info_ref, x_ref, dy_ref, gmix_ref, gn_ref, cols_ref, *rest):
    out_refs = rest[-GROUP:]
    tokens, alive = tokens_and_marks(x_ref)
    _, normed, inverse = norm_cols(tokens, column(cols_ref, G1), column(cols_ref, B1))
    grad_in = gmix_ref[0].astype(F32) + norm_cols_back(gn_ref[0].astype(F32), normed, inverse, column(cols_ref, G1))
    grad_in = jnp.where(alive > 0, grad_in, side_by_side(dy_ref).astype(F32))
    slots = grad_in.shape[1] // STEP
    odd = lax.rem(info_ref[1], 2) == 1
    first, second = grad_in[:, :slots], grad_in[:, slots:]
    first, second = jnp.where(odd, second, first).astype(BF), jnp.where(odd, first, second).astype(BF)
    for k in range(GROUP // STEP):

        @pl.when(pl.program_id(0) == k)
        def _():
            out_refs[STEP * k][0] = first
            out_refs[STEP * k + 1][0] = second


def place_body(info_ref, *refs):
    out_ref = refs[-1]
    for k, ref in enumerate(refs[:-1]):
        cell = k // GROUP * GROUP + jnp.bitwise_xor(info_ref[1], k % GROUP)
        out_ref[pl.ds(cell, 1)] = ref[...]


def unpack_body(count, block, pieces, sums, smalls, extras):
    def body(info_ref, *rest):
        in_refs, whole_ref = rest[:count], rest[-1]
        out_refs = list(rest[-1 - len(pieces) - len(sums) - len(smalls) : -1])
        rows = in_refs[0].shape[0]
        for s, ref in enumerate(in_refs):
            owner = jnp.bitwise_xor(info_ref[0], s)
            whole_ref[pl.ds(pl.multiple_of(owner * rows, 16), rows), :] = ref[...].astype(F32)
        for at, width in pieces:
            ref = out_refs.pop(0)
            for c in range(-(-width // 128)):
                take = min(128, width - c * 128)
                first = (at + c) * block
                ref[:, c * 128 : c * 128 + take] = whole_ref[first : first + D, 0:take]
        for at, width in sums:
            ref = out_refs.pop(0)
            ref[...] = jnp.zeros_like(ref)
            for c in range(-(-width // 128)):
                first = (at + c) * block + D
                ref[c : c + 1, :] = whole_ref[first : first + 1, :]
        for k, (row, width) in enumerate(smalls):
            ref = out_refs.pop(0)
            line = jnp.concatenate(
                [whole_ref[row : row + 1, :], whole_ref[row + 1 : row + 2, 0 : width - 128]], axis=1
            )
            ref[...] = line + rest[count + k][...] if k < extras else line

    return body


def whole(array):
    zeros = (0,) * len(array.shape)
    return pl.BlockSpec(array.shape, lambda i, info: zeros)


def call(body, info, ins, in_specs, outs, out_specs, scratch, grid=1, us=1, waits=(), limit=VMEM_LIMIT):
    if waits:
        first, _ = lax.optimization_barrier((ins[0], list(waits)))
        ins = [first] + list(ins[1:])
    return pl.pallas_call(
        body,
        grid_spec=pltpu.PrefetchScalarGridSpec(
            num_scalar_prefetch=1,
            grid=(grid,),
            in_specs=in_specs,
            out_specs=out_specs,
            scratch_shapes=[pltpu.VMEM(shape, kind) for shape, kind in scratch],
        ),
        out_shape=outs,
        compiler_params=pltpu.CompilerParams(
            dimension_semantics=("arbitrary",), vmem_limit_bytes=limit
        ),
        cost_estimate=pl.CostEstimate(
            flops=int(us * 1.15e9), bytes_accessed=int(us * 1e5), transcendentals=0
        ),
    )(info, *ins)


def swap(value, axis, groups=None):
    return lax.all_to_all(value, axis, 0, 0, axis_index_groups=groups, tiled=True)


def share_kernel(part, nt):
    others = nt // GROUP
    got = [part]
    for s in range(1, others):
        got.append(lax.ppermute(part, "tok", [(i, (i + s * GROUP) % nt) for i in range(nt)]))
    return got


class Reduction:
    def __init__(self, packed, info, rows, nc, nt):
        self.packed, self.info, self.rows, self.nc, self.nt = packed, info, rows, nc, nt
        self.quarter, self.share = rows // nc, rows // (nc * nt)

    def cross(self, values):
        return [values[0]] + [
            lax.ppermute(values[s], "cells", [(i, i ^ s) for i in range(self.nc)])
            for s in range(1, self.nc)
        ]

    def total(self, parts, waits):
        parts, _ = lax.optimization_barrier((parts, waits))
        total = parts[0].astype(F32)
        for part in parts[1:]:
            total = total + part.astype(F32)
        return total.astype(BF)

    def over_cells(self):
        self.one = self.cross(self.packed)

    def over_tok(self, waits):
        mine = self.total(self.one, waits)
        self.two = swap(mine.reshape(self.nt, self.share, 128), "tok")
        return mine

    def back_tok(self, waits):
        two, _ = lax.optimization_barrier((self.two, waits))
        mine = self.total([two[k] for k in range(self.nt)], [])
        mine = jnp.broadcast_to(mine[None], (self.nt,) + mine.shape)
        self.three = swap(mine, "tok")
        return mine

    def back_cells(self):
        self.four = self.cross([self.three.reshape(self.quarter, 128)] * self.nc)

    def results(self, block, pieces, sums, smalls, waits=(), extras=()):
        outs = [jax.ShapeDtypeStruct((D, width), F32) for _, width in pieces]
        outs += [jax.ShapeDtypeStruct((8, 128), F32) for _ in sums]
        outs += [jax.ShapeDtypeStruct((1, width), F32) for _, width in smalls]
        outs = call(
            unpack_body(self.nc, block, pieces, sums, smalls, len(extras)), self.info,
            self.four + list(extras), [whole(v) for v in self.four + list(extras)], outs, [whole(v) for v in outs], [((self.rows, 128), F32)],
            us=0.02, waits=waits, limit=SMALL_LIMIT,
        )
        return outs[: len(pieces)], outs[len(pieces) :]


def padded_rows(need, nc, nt):
    unit = nc * nt * 16
    return -(-need // unit) * unit


def shards(
    tokens, cotangent, gene_count, expressed, projection, first_gain, first_bias, query_weight,
    key_weight, value_weight, out_weight, out_bias, second_gain, second_bias, up_weight, up_bias,
    down_weight, down_bias,
):
    cells, _, slots = tokens.shape
    turns = cells // GROUP
    steps, lanes = GROUP // STEP, STEP * slots
    nt, nc = lax.axis_size("tok"), lax.axis_size("cells")
    position = lax.axis_index("tok")
    groups = [[g * GROUP + i for i in range(GROUP)] for g in range(nt // GROUP)]
    info = jnp.stack([lax.axis_index("cells"), position % GROUP]).astype(jnp.int32)

    slot_index = position * slots + lax.broadcasted_iota(jnp.int32, (cells, slots), 1)
    alive = ((slot_index < gene_count[:, None]) & (expressed > 0)).astype(BF)
    marks = jnp.pad(alive[:, None, :], ((0, 0), (0, DX - D - 1), (0, 0)))

    def turn_of(array, c):
        return array[c * GROUP : (c + 1) * GROUP]

    def to_cells(c):
        return swap(jnp.concatenate([turn_of(tokens, c), turn_of(marks, c)], axis=1), "tok", groups)

    x = [to_cells(0)]

    vectors = [first_gain, first_bias, second_gain, second_bias, out_bias, down_bias, up_bias]
    vec = jnp.stack([jnp.pad(v, (0, FF - v.shape[0])) for v in vectors + [jnp.zeros((FF,), F32)]])
    outs = [jax.ShapeDtypeStruct((FF, 8), F32)] + [
        jax.ShapeDtypeStruct(shape, BF)
        for shape in (
            (INNER, DX), (D, 2 * INNER), (2 * INNER, DX), (INNER, D), (FF, DX), (FF, D),
            (MAIN, HEAD_SIZE), (LEFT, INNER), (EXT, MAIN), (HEADS * EXT, LEFT),
        )
    ]
    wot = out_weight.T
    ins = [
        vec, projection.T, query_weight, key_weight, value_weight, wot, up_weight, down_weight,
    ]
    cols, wqt, wkv, wkvt, wo, upt, downt, pm, left_proj, tm, tl = call(
        prep_body, info, ins, [whole(v) for v in ins], outs, [whole(v) for v in outs], [], us=4,
    )

    tokens, marks, cols = lax.optimization_barrier((tokens, marks, cols))
    x += [to_cells(c) for c in range(1, turns)]
    x_spec = pl.BlockSpec((STEP, DX, slots), lambda j, info: (j, 0, 0))

    def step_spec(rows):
        return pl.BlockSpec((1, rows, lanes), lambda j, info: (j, 0, 0))

    k_out = jax.ShapeDtypeStruct((KROWS, MAIN), BF)
    k_acc = ((KROWS, MAIN), F32)
    key_scratch = [
        ((INNER, lanes), BF), ((HEADS * EXT, lanes), BF), ((HEADS * MAIN, lanes), BF),
        ((LEFT, lanes), BF), ((16, lanes), F32),
    ]
    kernels, dy = [], []
    for c in range(turns):
        ins = [x[c], cols, wkvt, pm, left_proj]
        part = call(
            first_body, info, ins, [x_spec] + [whole(v) for v in ins[1:]],
            k_out, whole(k_out), [k_acc] + key_scratch, grid=steps, us=12,
        )
        mine, part = lax.optimization_barrier((turn_of(cotangent, c), part))
        kernels.append(share_kernel(part, nt))
        dy.append(swap(mine, "tok", groups))

    token_out = jax.ShapeDtypeStruct((GROUP, D, slots), BF)
    token_spec = pl.BlockSpec((STEP, D, slots), lambda j, info: (j, 0, 0))
    wide_out = jax.ShapeDtypeStruct((steps, D, lanes), BF)
    common = [
        ((HEADS * EXT, lanes), BF), ((HEADS * MAIN, lanes), BF), ((LEFT, lanes), BF),
        ((16, lanes), F32), ((HEADS * EXT, MAIN), BF), ((HEADS * EXT, LEFT), BF),
        ((HEADS * EXT, lanes), F32),
    ]
    weights = [
        cols, wqt, query_weight, wot, wo, upt, up_weight, downt, down_weight,
        pm, left_proj, tm, tl,
    ]
    rows2 = padded_rows(GRAD2 + 2 * SMALL2, nc, nt)
    sums = [((GRAD2, 128), F32), ((SMALL2 * D, 128), F32)]
    mixed_grads, query_grads, kernel_grads = [], [], []
    results, sums2 = [], []
    for c in range(turns):
        start, last = c == 0, c == turns - 1
        fixed = kernels[c] + sums2 + weights
        if last:
            sum_outs = [jax.ShapeDtypeStruct((rows2 // nc, 128), BF)] * nc
            sum_scratch = [((rows2, 128), F32)] + sums
        else:
            sum_outs = [jax.ShapeDtypeStruct(shape, kind) for shape, kind in sums]
            sum_scratch = []
        out, gmix, gnq, kg, *sums2 = call(
            second_body(len(kernels[c]), start, nc if last else 0, HEADS if start else UNROLL), info, [x[c], dy[c]] + fixed,
            [x_spec, token_spec] + [whole(v) for v in fixed],
            [token_out, wide_out, wide_out, k_out] + sum_outs,
            [token_spec, step_spec(D), step_spec(D)] + [whole(v) for v in [k_out] + sum_outs],
            sum_scratch + [((KROWS, MAIN), BF), k_acc, ((INNER, lanes), BF), ((INNER, lanes), BF)]
            + common
            + [
                ((INNER, lanes), BF), ((16, lanes), F32), ((FF, lanes), BF), ((FF, lanes), BF),
                ((DX, lanes), BF), ((DX, lanes), BF),
            ],
            grid=steps, us=40,
        )
        results.append(swap(out, "tok", groups))
        mixed_grads.append(gmix)
        query_grads.append(gnq)
        kernel_grads.append(share_kernel(kg, nt))
    reduce2 = Reduction(sums2, info, rows2, nc, nt)
    reduce2.over_cells()

    rows3 = padded_rows(2 * Q_BLOCKS * D + 2 * SMALL3, nc, nt)
    weights = [cols, wkvt, wkv, pm, left_proj, tm, tl]
    normed_grads, sums3 = [], []
    waits = [sums2[0], results[0]]
    for c in range(turns):
        start, last = c == 0, c == turns - 1
        fixed = kernel_grads[c] + sums3 + weights
        if last:
            sum_outs = [jax.ShapeDtypeStruct((rows3 // nc, 128), BF)] * nc
            sum_scratch = [((rows3, 128), F32), ((GRAD3, 128), F32), ((SMALL3 * D, 128), F32)]
        else:
            sum_outs = [jax.ShapeDtypeStruct((GRAD3, 128), F32)]
            sum_scratch = []
        got, *sums3 = call(
            third_body(len(kernel_grads[c]), start, nc if last else 0), info,
            [x[c], query_grads[c]] + fixed, [x_spec, step_spec(D)] + [whole(v) for v in fixed],
            [wide_out] + sum_outs, [step_spec(D)] + [whole(v) for v in sum_outs],
            sum_scratch
            + [((KROWS, MAIN), BF), ((INNER, lanes), BF), ((2 * INNER, lanes), BF)] + common
            + [((DX, lanes), BF)],
            grid=steps, us=22, waits=waits,
        )
        normed_grads.append(got)
        if start:
            waits = [reduce2.over_tok([got, results[-1]] + kernel_grads[-1][1:])]
    reduce3 = Reduction(sums3, info, rows3, nc, nt)
    reduce3.over_cells()
    waits = [sums3[0], results[-1], reduce2.back_tok([sums3[0]])]
    one_out = jax.ShapeDtypeStruct((1, D, slots), BF)
    grads = []
    for c in range(turns):
        ins = [x[c], dy[c], mixed_grads[c], normed_grads[c], cols]

        def pair(rows, blocks=STEP, columns=slots):
            return pl.BlockSpec(
                (blocks, rows, columns), lambda j, info: (jnp.bitwise_xor(info[1] // STEP, j), 0, 0)
            )

        specs = [pair(DX), pair(D), pair(D, 1, lanes), pair(D, 1, lanes), whole(cols)]
        out = call(
            last_body, info, ins, specs, [one_out] * GROUP,
            [whole(one_out)] * GROUP, [], grid=steps, us=6, waits=waits,
        )
        if c == turns - 1:
            reduce2.back_cells()
            mine = reduce3.back_tok([out[0]] + reduce2.four[1:3] + grads[1:])
            out, _ = lax.optimization_barrier((out, mine))
        grads += [out[0]] + [
            lax.ppermute(out[s], "tok", [(i, i - i % GROUP + (i % GROUP ^ s)) for i in range(nt)])
            for s in range(1, GROUP)
        ]
        if c == 0:
            waits = [reduce3.over_tok([out[0]]), reduce2.three]
    (dwq, dwot, dup, ddown), (upb, gain2, bias2, outb, downb, gain1q, bias1q) = reduce2.results(
        DX, [(WQ_AT, INNER), (WO_AT, INNER), (UP_AT, FF), (DOWN_AT, FF)], [(UP_AT, FF)],
        [(GRAD2 + 2 * k, D) for k in range(SMALL2)], waits=[mine],
    )
    reduce3.three, _ = lax.optimization_barrier((reduce3.three, gain1q))
    reduce3.back_cells()

    result = jnp.concatenate(results, axis=0)
    grad_in = call(
        place_body, info, grads, [whole(v) for v in grads], jax.ShapeDtypeStruct((cells, D, slots), BF),
        pl.BlockSpec((cells, D, slots), lambda i, info: (0, 0, 0)), [], us=0.02,
        waits=[reduce3.three], limit=SMALL_LIMIT,
    )
    (dwk, dwv), (gain1, bias1) = reduce3.results(
        D, [(0, INNER), (Q_BLOCKS, INNER)], [], [(2 * Q_BLOCKS * D + 2 * k, D) for k in range(SMALL3)],
        extras=[gain1q, bias1q], waits=[grad_in],
    )
    return (
        result, grad_in, gain1[0], bias1[0], dwq, dwk, dwv, dwot.T, outb[0],
        gain2[0], bias2[0], dup, upb.reshape(8 * 128)[:FF], ddown, downb[0],
    )


def solution(mesh):
    rows = P("cells", None, "tok")
    placed = (rows, rows, P("cells"), P("cells", "tok")) + (P(),) * 14
    return jax.shard_map(
        shards,
        mesh=mesh,
        in_specs=placed,
        out_specs=(rows, rows) + (P(),) * 13,
        check_vma=False,
    )
```

```python
import math

import jax
import jax.numpy as jnp
from jax import lax
from jax.experimental import pallas as pl
from jax.experimental.pallas import tpu as pltpu
from jax.sharding import PartitionSpec as P

HEADS = 10
HEAD_SIZE = 64
FEATURES = 266
D = 200
INNER = HEADS * HEAD_SIZE
DX = 208
FF = 800
EPSILON = 1e-05

MAIN = 256
REST = FEATURES - MAIN
LEFT = 128
EXT = 80
SUM_ROW = INNER
LEFT_ROW = INNER + 16
KROWS = LEFT_ROW + 48

C0 = HEAD_SIZE ** (-0.25)
LOG2E = 1.0 / math.log(2.0)
RAW_SCALE = C0 * LOG2E
SQ_SCALE = 0.5 * C0 * C0 * LOG2E
SHIFT = -0.5 * math.log2(FEATURES)
FF_CHUNK = 160
Q_BLOCKS = INNER // 128
F_BLOCKS = -(-FF // 128)
WQ_AT, WO_AT, UP_AT, DOWN_AT = 0, Q_BLOCKS, 2 * Q_BLOCKS, 2 * Q_BLOCKS + F_BLOCKS
GRAD2 = (2 * Q_BLOCKS + 2 * F_BLOCKS) * DX
GRAD3 = 2 * Q_BLOCKS * DX
SMALL2 = 6
SMALL3 = 2

BF = jnp.bfloat16
F32 = jnp.float32
VMEM_LIMIT = 56 * 1024 * 1024
GROUP = 4
STEP = 2
UNROLL = 5


def dot(left, right):
    return jnp.dot(left, right, preferred_element_type=F32)


def dot_nt(left, right):
    return lax.dot_general(left, right, (((1,), (1,)), ((), ())), preferred_element_type=F32)


def dot_tn(left, right):
    return lax.dot_general(left, right, (((0,), (0,)), ((), ())), preferred_element_type=F32)


def iota(shape, axis):
    return lax.broadcasted_iota(jnp.int32, shape, axis)


def norm_cols(values, gain, bias):
    average = jnp.mean(values, axis=0, keepdims=True)
    centred = values - average
    inverse = lax.rsqrt(jnp.mean(centred * centred, axis=0, keepdims=True) + EPSILON)
    normed = centred * inverse
    return normed * gain + bias, normed, inverse


def norm_cols_back(grad_out, normed, inverse, gain):
    scaled = grad_out * gain
    return inverse * (
        scaled
        - jnp.mean(scaled, axis=0, keepdims=True)
        - normed * jnp.mean(scaled * normed, axis=0, keepdims=True)
    )


def lane_sums(values):
    total = values[:, :128]
    for start in range(128, values.shape[1], 128):
        total = total + values[:, start : start + 128]
    return total


def ext_rows(h):
    return pl.ds(pl.multiple_of(h * EXT, 16), EXT)


def val_rows(h):
    return pl.ds(pl.multiple_of(h * EXT, 16), HEAD_SIZE)


def main_rows(h):
    return pl.ds(pl.multiple_of(h * MAIN, MAIN), MAIN)


def head_rows(h):
    return pl.ds(pl.multiple_of(h * HEAD_SIZE, HEAD_SIZE), HEAD_SIZE)


def one_row(h):
    return pl.ds(h, 1)


def for_heads(step, unroll=HEADS):
    def turn(i, _):
        for k in range(unroll):
            step(i * unroll + k)
        return 0

    if unroll == HEADS:
        turn(0, 0)
    else:
        lax.fori_loop(0, HEADS // unroll, turn, 0)


G1, B1, G2, B2, OB, DB, UB = range(7)


def column(cols_ref, which, rows=D):
    return cols_ref[0:rows, which : which + 1]


def prep_body(
    info_ref, vec_ref, projt_ref, wq_ref, wk_ref, wv_ref, wot_ref, up_ref, down_ref,
    cols_ref, wqt_ref, wkv_ref, wkvt_ref, wo_ref, upt_ref, downt_ref,
    pm_ref, pl_ref, tm_ref, tl_ref,
):
    cols_ref[...] = vec_ref[...].T
    def padded(matrix):
        return jnp.concatenate([matrix.T, jnp.zeros((matrix.shape[1], DX - D), BF)], axis=1)

    wqt_ref[...] = padded(wq_ref[...])
    wkv_ref[:, :INNER] = wk_ref[...]
    wkv_ref[:, INNER:] = wv_ref[...]
    wkvt_ref[:INNER] = padded(wk_ref[...])
    wkvt_ref[INNER:] = padded(wv_ref[...])
    wo_ref[...] = wot_ref[...].T
    upt_ref[...] = padded(up_ref[...])
    downt_ref[...] = down_ref[...].T
    proj = projt_ref[...].T

    def one_hot(shape, mask):
        return jnp.where(mask, 1.0, 0.0).astype(BF)

    pm_ref[...] = proj[:MAIN]
    s = (16, FEATURES)
    rest = dot(one_hot(s, (iota(s, 0) + MAIN == iota(s, 1)) & (iota(s, 0) < REST)), proj).astype(BF)
    s = (HEAD_SIZE, INNER)
    wide = dot(rest, one_hot(s, iota(s, 0) == iota(s, 1) % HEAD_SIZE)).astype(BF)
    s = (LEFT, 16)
    tall = dot(one_hot(s, iota(s, 0) % REST == iota(s, 1)), wide)
    s = (LEFT, INNER)
    pl_ref[...] = jnp.where(iota(s, 0) // REST == iota(s, 1) // HEAD_SIZE, tall, 0.0).astype(BF)
    s = (EXT, HEAD_SIZE)
    pick = one_hot(s, iota(s, 0) == iota(s, 1))
    s = (EXT, MAIN)
    tm_ref[...] = jnp.where(iota(s, 0) == HEAD_SIZE, 1.0, dot_nt(pick, proj[:MAIN])).astype(BF)
    s = (EXT, 16)
    rest_ext = jnp.where(iota(s, 0) == HEAD_SIZE, 1.0, dot_nt(pick, rest)).astype(BF)
    s = (16, LEFT)
    spread = dot(rest_ext, one_hot(s, iota(s, 0) == iota(s, 1) % REST))
    s = (EXT, LEFT)
    for h in range(HEADS):
        tl_ref[ext_rows(h), :] = jnp.where(iota(s, 1) // REST == h, spread, 0.0).astype(BF)


def shifts_of(u_ref, s_ref):
    for h in range(HEADS):
        wide = u_ref[head_rows(h), :].astype(F32)
        s_ref[h : h + 1, :] = SHIFT - SQ_SCALE * jnp.sum(wide * wide, axis=0, keepdims=True)


def left_features(u_ref, phil_ref, s_ref, pl_ref):
    shape = (LEFT, u_ref.shape[1])
    owner = iota(shape, 0) // REST
    shifts = jnp.zeros(shape, F32)
    for h in range(HEADS):
        shifts = jnp.where(owner == h, s_ref[h : h + 1, :], shifts)
    phil_ref[...] = jnp.exp2(dot(pl_ref[...], u_ref[...]) * RAW_SCALE + shifts).astype(BF)


def main_features(h, u_ref, phi_ref, s_ref, pm_ref):
    raw = dot(pm_ref[...], u_ref[head_rows(h), :])
    phi_ref[main_rows(h), :] = jnp.exp2(raw * RAW_SCALE + s_ref[one_row(h), :]).astype(BF)


def add_head_kernel(h, acc_ref, ext_ref, phi_ref):
    total = dot_nt(ext_ref[ext_rows(h), :], phi_ref[main_rows(h), :])
    acc_ref[head_rows(h), :] += total[:HEAD_SIZE]
    acc_ref[one_row(SUM_ROW + h), :] += total[HEAD_SIZE : HEAD_SIZE + 1]


def add_left_kernel(acc_ref, ext_ref, phil_ref):
    every = dot_nt(ext_ref[...], phil_ref[...])
    owner = iota((EXT, LEFT), 1) // REST
    left = jnp.zeros((EXT, LEFT), F32)
    for h in range(HEADS):
        left = jnp.where(owner == h, every[h * EXT : (h + 1) * EXT], left)
    acc_ref[LEFT_ROW:KROWS, 0:LEFT] += left[:48]
    acc_ref[LEFT_ROW : LEFT_ROW + 32, LEFT:MAIN] += left[48:EXT]


def sum_kernels(in_refs, whole_ref):
    total = in_refs[0][...].astype(F32)
    for ref in in_refs[1:]:
        total = total + ref[...].astype(F32)
    whole_ref[...] = total.astype(BF)


def read_kernel(whole_ref, kt_ref, kl_ref):
    sums = whole_ref[SUM_ROW : SUM_ROW + 16, :].astype(F32)
    first = iota((16, MAIN), 0) == 0
    left = jnp.concatenate(
        [whole_ref[LEFT_ROW:KROWS, 0:LEFT], whole_ref[LEFT_ROW : LEFT_ROW + 32, LEFT:MAIN]], axis=0
    ).astype(F32)
    owner = iota((EXT, LEFT), 1) // REST
    for h in range(HEADS):
        kt_ref[val_rows(h), :] = whole_ref[head_rows(h), :]
        kt_ref[h * EXT + HEAD_SIZE : (h + 1) * EXT, :] = jnp.where(
            first, sums[h : h + 1, :], 0.0
        ).astype(BF)
        kl_ref[ext_rows(h), :] = jnp.where(owner == h, left, 0.0).astype(BF)


def left_grads(phil_ref, kl_ref, ext_ref, tl_ref, wide_ref):
    phil_ref[...] = (dot_tn(kl_ref[...], ext_ref[...]) * phil_ref[...].astype(F32)).astype(BF)
    wide_ref[...] = dot(tl_ref[...], phil_ref[...])


def weigh(h, phi_ref, kt_ref, ext_ref):
    grad = dot_tn(kt_ref[ext_rows(h), :], ext_ref[ext_rows(h), :])
    phi_ref[main_rows(h), :] = (grad * phi_ref[main_rows(h), :].astype(F32)).astype(BF)


def main_grads(h, grad_ref, u_ref, phi_ref, tm_ref, wide_ref):
    through = dot(tm_ref[...], phi_ref[main_rows(h), :]) + wide_ref[ext_rows(h), :]
    grad_ref[head_rows(h), :] = (
        C0 * through[:HEAD_SIZE]
        - (C0 * C0) * u_ref[head_rows(h), :].astype(F32) * through[HEAD_SIZE : HEAD_SIZE + 1]
    ).astype(BF)


def with_ones(values):
    rows = iota((DX - D, values.shape[1]), 0)
    return jnp.concatenate([values, jnp.where(rows == 0, 1.0, 0.0)], axis=0).astype(BF)


def side_by_side(ref):
    blocks = [ref[(k,) + (0,) * (len(ref.shape) - 3)] for k in range(STEP)]
    return jnp.concatenate(blocks, axis=1)


def tokens_and_marks(x_ref):
    both = side_by_side(x_ref).astype(F32)
    return both[:D], both[D : D + 1]


def keys_values(normed_low, alive, wkvt_ref, k_ref, ext_ref):
    k_ref[...] = dot(wkvt_ref[:INNER, :], normed_low).astype(BF)
    values = dot(wkvt_ref[INNER:, :], normed_low)
    mark = jnp.where(iota((16, values.shape[1]), 0) == 0, alive, 0.0).astype(BF)
    for h in range(HEADS):
        ext_ref[val_rows(h), :] = (values[h * HEAD_SIZE : (h + 1) * HEAD_SIZE] * alive).astype(BF)
        ext_ref[h * EXT + HEAD_SIZE : (h + 1) * EXT, :] = mark


def key_sums(x, alive, cols_ref, wkvt_ref, pm_ref, pl_ref, acc_ref, k_ref, ext_ref, phi_ref, phil_ref, s_ref):
    normed, _, _ = norm_cols(x, column(cols_ref, G1), column(cols_ref, B1))
    keys_values(with_ones(normed), alive, wkvt_ref, k_ref, ext_ref)
    shifts_of(k_ref, s_ref)
    left_features(k_ref, phil_ref, s_ref, pl_ref)
    for_heads(lambda h: main_features(h, k_ref, phi_ref, s_ref, pm_ref))
    for_heads(lambda h: add_head_kernel(h, acc_ref, ext_ref, phi_ref))
    add_left_kernel(acc_ref, ext_ref, phil_ref)


def first_body(info_ref, x_ref, cols_ref, wkvt_ref, pm_ref, pl_ref, out_ref, acc_ref, *scratch):
    @pl.when(pl.program_id(0) == 0)
    def _():
        acc_ref[...] = jnp.zeros_like(acc_ref)

    tokens, alive = tokens_and_marks(x_ref)
    key_sums(tokens, alive, cols_ref, wkvt_ref, pm_ref, pl_ref, acc_ref, *scratch)

    @pl.when(pl.program_id(0) == pl.num_programs(0) - 1)
    def _():
        out_ref[...] = acc_ref[...].astype(BF)


def add_blocks(acc_ref, at, values):
    rows, width = values.shape
    for c in range(-(-width // 128)):
        take = min(128, width - c * 128)
        first = (at + c) * DX
        acc_ref[first : first + rows, 0:take] += values[:, c * 128 : c * 128 + take]


def add_small(small_ref, which, values):
    small_ref[which * D : (which + 1) * D, :] += lane_sums(values)


def add_first_norm(small_ref, which, acc_ref, weight_refs, cols_ref):
    with_normed = jnp.zeros((D, 128), F32)
    alone = jnp.zeros((D, 128), F32)
    block = 0
    for ref in weight_refs:
        for c in range(ref.shape[1] // 128):
            weight = ref[:, c * 128 : (c + 1) * 128].astype(F32)
            first = block * DX
            with_normed += weight * acc_ref[first : first + D, :]
            alone += weight * acc_ref[first + D : first + D + 1, :]
            block += 1
    gain = (with_normed - column(cols_ref, B1) * alone) / column(cols_ref, G1)
    small_ref[which * D : (which + 1) * D, :] = gain
    small_ref[(which + 1) * D : (which + 2) * D, :] = alone


def pack_sums(out_refs, acc_ref, small_ref, flat_ref, me, rows):
    blocks = acc_ref.shape[0] // DX
    base = blocks * rows
    for k in range(blocks):
        flat_ref[k * rows : (k + 1) * rows, :] = acc_ref[k * DX : k * DX + rows, :]
    flat_ref[base:, :] = jnp.zeros((flat_ref.shape[0] - base, 128), F32)
    high = small_ref[...].astype(BF)
    low = (small_ref[...] - high.astype(F32)).astype(BF)
    ones = jnp.ones((8, 128), BF)
    row = base
    for which in range(small_ref.shape[0] // D):
        part = slice(which * D, (which + 1) * D)
        line = dot_nt(ones, high[part]) + dot_nt(ones, low[part])
        flat_ref[row : row + 1, :] = line[0:1, 0:128]
        flat_ref[row + 1 : row + 2, 0 : D - 128] = line[0:1, 128:D]
        row += 2
    rows = out_refs[0].shape[0]
    for s, ref in enumerate(out_refs):
        owner = jnp.bitwise_xor(me, s)
        ref[...] = flat_ref[pl.ds(pl.multiple_of(owner * rows, 16), rows), :].astype(BF)


def put_side_by_side(out_ref, value):
    slots = value.shape[1] // STEP
    for k in range(STEP):
        out_ref[k] = value[:, k * slots : (k + 1) * slots]


def start_sums(start, ins, refs):
    for k, ref in enumerate(refs):
        ref[...] = jnp.zeros_like(ref) if start else ins[k][...]


def second_body(blocks, start, parts, unroll):
    def body(info_ref, x_ref, dy_ref, *rest):
        k_refs, rest = rest[:blocks], rest[blocks:]
        ins = ()
        if not start:
            ins, rest = rest[:2], rest[2:]
        (
            cols_ref, wqt_ref, wq_ref, wot_ref, wo_ref, upt_ref, up_ref, downt_ref, down_ref,
            pm_ref, pl_ref, tm_ref, tl_ref,
        ), rest = rest[:13], rest[13:]
        (out_ref, gmix_ref, gnq_ref, kg_ref), rest = rest[:4], rest[4:]
        if parts:
            packed_refs, (flat_ref, ga_ref, sm_ref, *rest) = rest[:parts], rest[parts:]
        else:
            (ga_ref, sm_ref), rest = rest[:2], rest[2:]
        (
            whole_ref, acc_ref, q_ref, gq_ref, ext_ref, phi_ref, phil_ref, s_ref, kt_ref, kl_ref, wide_ref,
            att_ref, rec_ref, act_ref, gup_ref, n1_ref, n2_ref,
        ) = rest
        j = pl.program_id(0)

        @pl.when(j == 0)
        def _():
            start_sums(start, ins, (ga_ref, sm_ref))
            acc_ref[...] = jnp.zeros_like(acc_ref)
            sum_kernels(k_refs, whole_ref)
            read_kernel(whole_ref, kt_ref, kl_ref)

        tokens, alive = tokens_and_marks(x_ref)
        row_alive = alive > 0
        normed, _, _ = norm_cols(tokens, column(cols_ref, G1), column(cols_ref, B1))
        n1_ref[...] = with_ones(normed)
        q_ref[...] = dot(wqt_ref[...], n1_ref[...]).astype(BF)
        shifts_of(q_ref, s_ref)
        left_features(q_ref, phil_ref, s_ref, pl_ref)
        wide_ref[...] = dot(kl_ref[...], phil_ref[...])
        for_heads(lambda h: main_features(h, q_ref, phi_ref, s_ref, pm_ref))

        def attend(h):
            combined = dot(kt_ref[ext_rows(h), :], phi_ref[main_rows(h), :]) + wide_ref[ext_rows(h), :]
            inverse = 1.0 / jnp.where(row_alive, combined[HEAD_SIZE : HEAD_SIZE + 1], 1.0)
            rec_ref[one_row(h), :] = inverse
            quotient = combined[:HEAD_SIZE] * inverse
            wide_ref[val_rows(h), :] = quotient
            att_ref[head_rows(h), :] = quotient.astype(BF)

        for_heads(attend)
        mixed = tokens + dot(wot_ref[...], att_ref[...]) + column(cols_ref, OB)
        second, second_normed, second_inverse = norm_cols(
            mixed, column(cols_ref, G2), column(cols_ref, B2)
        )
        n2_ref[...] = with_ones(second)
        upstream_wide = jnp.where(row_alive, side_by_side(dy_ref).astype(F32), 0.0)
        upstream = upstream_wide.astype(BF)
        for c in range(FF // FF_CHUNK):
            rows = slice(c * FF_CHUNK, (c + 1) * FF_CHUNK)
            up = dot(upt_ref[rows, :], n2_ref[...]) + cols_ref[rows, UB : UB + 1]
            grad_act = dot(downt_ref[rows, :], upstream)
            half = 0.5 * (1.0 + lax.erf(up * 0.7071067811865476))
            act_ref[rows, :] = (up * half).astype(BF)
            slope = half + up * jnp.exp(-0.5 * up * up) * 0.3989422804014327
            grad_up = (grad_act * slope).astype(BF)
            gup_ref[rows, :] = grad_up
        result = mixed + dot(down_ref[...], act_ref[...]) + column(cols_ref, DB)
        put_side_by_side(out_ref, jnp.where(row_alive, result, tokens).astype(BF))

        add_small(sm_ref, 3, upstream_wide)
        grad_second = dot(up_ref[...], gup_ref[...])
        add_blocks(ga_ref, DOWN_AT, dot_nt(upstream, act_ref[...]))
        add_small(sm_ref, 0, grad_second * second_normed)
        add_small(sm_ref, 1, grad_second)
        grad_mixed = upstream_wide + norm_cols_back(
            grad_second, second_normed, second_inverse, column(cols_ref, G2)
        )
        gmix_ref[0] = grad_mixed.astype(BF)
        grad_branch = grad_mixed.astype(BF)
        add_small(sm_ref, 2, grad_branch.astype(F32))
        pad_row = iota((16, alive.shape[1]), 0) == 0
        grad_att = dot(wo_ref[...], grad_branch)
        add_blocks(ga_ref, UP_AT, dot_nt(n2_ref[...], gup_ref[...]))
        add_blocks(ga_ref, WO_AT, dot_nt(grad_branch, att_ref[...]))
        for h in range(HEADS):
            grad_head = grad_att[h * HEAD_SIZE : (h + 1) * HEAD_SIZE]
            inverse = rec_ref[h : h + 1, :]
            ext_ref[val_rows(h), :] = (grad_head * inverse).astype(BF)
            grad_sum = -inverse * jnp.sum(grad_head * wide_ref[val_rows(h), :], axis=0, keepdims=True)
            ext_ref[h * EXT + HEAD_SIZE : (h + 1) * EXT, :] = jnp.where(pad_row, grad_sum, 0.0).astype(BF)
        add_left_kernel(acc_ref, ext_ref, phil_ref)
        left_grads(phil_ref, kl_ref, ext_ref, tl_ref, wide_ref)
        for_heads(lambda h: add_head_kernel(h, acc_ref, ext_ref, phi_ref))
        for_heads(lambda h: weigh(h, phi_ref, kt_ref, ext_ref))
        for_heads(lambda h: main_grads(h, gq_ref, q_ref, phi_ref, tm_ref, wide_ref), unroll)
        add_blocks(ga_ref, WQ_AT, dot_nt(n1_ref[...], gq_ref[...]))
        gnq_ref[0] = dot(wq_ref[...], gq_ref[...]).astype(BF)

        @pl.when(j == pl.num_programs(0) - 1)
        def _():
            kg_ref[...] = acc_ref[...].astype(BF)
            if parts:
                add_first_norm(sm_ref, 4, ga_ref, [wq_ref], cols_ref)
                pack_sums(packed_refs, ga_ref, sm_ref, flat_ref, info_ref[0], DX)

    return body


def third_body(blocks, start, parts):
    def body(info_ref, x_ref, gnq_ref, *rest):
        k_refs, rest = rest[:blocks], rest[blocks:]
        ins = ()
        if not start:
            ins, rest = rest[:1], rest[1:]
        (cols_ref, wkvt_ref, wkv_ref, pm_ref, pl_ref, tm_ref, tl_ref), rest = rest[:7], rest[7:]
        gn_ref, rest = rest[0], rest[1:]
        if parts:
            packed_refs, (flat_ref, ga_ref, sm_ref, *rest) = rest[:parts], rest[parts:]
        else:
            ga_ref, rest = rest[0], rest[1:]
        (
            whole_ref, k_ref, gkv_ref, ext_ref, phi_ref, phil_ref, s_ref, kt_ref, kl_ref, wide_ref, n1_ref,
        ) = rest

        @pl.when(pl.program_id(0) == 0)
        def _():
            start_sums(start, ins, (ga_ref,))
            sum_kernels(k_refs, whole_ref)
            read_kernel(whole_ref, kt_ref, kl_ref)

        tokens, alive = tokens_and_marks(x_ref)
        normed, _, _ = norm_cols(tokens, column(cols_ref, G1), column(cols_ref, B1))
        n1_ref[...] = with_ones(normed)
        keys_values(n1_ref[...], alive, wkvt_ref, k_ref, ext_ref)
        shifts_of(k_ref, s_ref)
        left_features(k_ref, phil_ref, s_ref, pl_ref)
        wide_ref[...] = dot(kl_ref[...], phil_ref[...])
        for_heads(lambda h: main_features(h, k_ref, phi_ref, s_ref, pm_ref))

        def value_grads(h):
            grad = dot(kt_ref[val_rows(h), :], phi_ref[main_rows(h), :]) + wide_ref[val_rows(h), :]
            gkv_ref[head_rows(HEADS + h), :] = (grad * alive).astype(BF)

        for_heads(value_grads)
        left_grads(phil_ref, kl_ref, ext_ref, tl_ref, wide_ref)
        for_heads(lambda h: weigh(h, phi_ref, kt_ref, ext_ref))
        for_heads(lambda h: main_grads(h, gkv_ref, k_ref, phi_ref, tm_ref, wide_ref))
        add_blocks(ga_ref, 0, dot_nt(n1_ref[...], gkv_ref[...]))
        gn_ref[0] = (gnq_ref[0].astype(F32) + dot(wkv_ref[...], gkv_ref[...])).astype(BF)

        if parts:

            @pl.when(pl.program_id(0) == pl.num_programs(0) - 1)
            def _():
                add_first_norm(sm_ref, 0, ga_ref, [wkv_ref], cols_ref)
                pack_sums(packed_refs, ga_ref, sm_ref, flat_ref, info_ref[0], D)

    return body


def last_body(info_ref, x_ref, dy_ref, gmix_ref, gn_ref, cols_ref, *rest):
    out_refs = rest[-GROUP:]
    tokens, alive = tokens_and_marks(x_ref)
    _, normed, inverse = norm_cols(tokens, column(cols_ref, G1), column(cols_ref, B1))
    grad_in = gmix_ref[0].astype(F32) + norm_cols_back(gn_ref[0].astype(F32), normed, inverse, column(cols_ref, G1))
    grad_in = jnp.where(alive > 0, grad_in, side_by_side(dy_ref).astype(F32))
    slots = grad_in.shape[1] // STEP
    odd = lax.rem(info_ref[1], 2) == 1
    first, second = grad_in[:, :slots], grad_in[:, slots:]
    first, second = jnp.where(odd, second, first).astype(BF), jnp.where(odd, first, second).astype(BF)
    for k in range(GROUP // STEP):

        @pl.when(pl.program_id(0) == k)
        def _():
            out_refs[STEP * k][0] = first
            out_refs[STEP * k + 1][0] = second


def place_body(info_ref, *refs):
    out_ref = refs[-1]
    for k, ref in enumerate(refs[:-1]):
        cell = k // GROUP * GROUP + jnp.bitwise_xor(info_ref[1], k % GROUP)
        out_ref[pl.ds(cell, 1)] = ref[...]


def unpack_body(count, block, pieces, sums, smalls, extras):
    def body(info_ref, *rest):
        in_refs, whole_ref = rest[:count], rest[-1]
        out_refs = list(rest[-1 - len(pieces) - len(sums) - len(smalls) : -1])
        rows = in_refs[0].shape[0]
        for s, ref in enumerate(in_refs):
            owner = jnp.bitwise_xor(info_ref[0], s)
            whole_ref[pl.ds(pl.multiple_of(owner * rows, 16), rows), :] = ref[...].astype(F32)
        for at, width in pieces:
            ref = out_refs.pop(0)
            for c in range(-(-width // 128)):
                take = min(128, width - c * 128)
                first = (at + c) * block
                ref[:, c * 128 : c * 128 + take] = whole_ref[first : first + D, 0:take]
        for at, width in sums:
            ref = out_refs.pop(0)
            ref[...] = jnp.zeros_like(ref)
            for c in range(-(-width // 128)):
                first = (at + c) * block + D
                ref[c : c + 1, :] = whole_ref[first : first + 1, :]
        for k, (row, width) in enumerate(smalls):
            ref = out_refs.pop(0)
            line = jnp.concatenate(
                [whole_ref[row : row + 1, :], whole_ref[row + 1 : row + 2, 0 : width - 128]], axis=1
            )
            ref[...] = line + rest[count + k][...] if k < extras else line

    return body


def whole(array):
    zeros = (0,) * len(array.shape)
    return pl.BlockSpec(array.shape, lambda i, info: zeros)


def call(body, info, ins, in_specs, outs, out_specs, scratch, grid=1, us=1, waits=()):
    if waits:
        first, _ = lax.optimization_barrier((ins[0], list(waits)))
        ins = [first] + list(ins[1:])
    return pl.pallas_call(
        body,
        grid_spec=pltpu.PrefetchScalarGridSpec(
            num_scalar_prefetch=1,
            grid=(grid,),
            in_specs=in_specs,
            out_specs=out_specs,
            scratch_shapes=[pltpu.VMEM(shape, kind) for shape, kind in scratch],
        ),
        out_shape=outs,
        compiler_params=pltpu.CompilerParams(
            dimension_semantics=("arbitrary",), vmem_limit_bytes=VMEM_LIMIT
        ),
        cost_estimate=pl.CostEstimate(
            flops=int(us * 1.15e9), bytes_accessed=int(us * 1e5), transcendentals=0
        ),
    )(info, *ins)


def swap(value, axis, groups=None):
    return lax.all_to_all(value, axis, 0, 0, axis_index_groups=groups, tiled=True)


def share_kernel(part, nt):
    others = nt // GROUP
    got = [part]
    for s in range(1, others):
        got.append(lax.ppermute(part, "tok", [(i, (i + s * GROUP) % nt) for i in range(nt)]))
    return got


class Reduction:
    def __init__(self, packed, info, rows, nc, nt):
        self.packed, self.info, self.rows, self.nc, self.nt = packed, info, rows, nc, nt
        self.quarter, self.share = rows // nc, rows // (nc * nt)

    def cross(self, values):
        return [values[0]] + [
            lax.ppermute(values[s], "cells", [(i, i ^ s) for i in range(self.nc)])
            for s in range(1, self.nc)
        ]

    def total(self, parts, waits):
        parts, _ = lax.optimization_barrier((parts, waits))
        total = parts[0].astype(F32)
        for part in parts[1:]:
            total = total + part.astype(F32)
        return total.astype(BF)

    def over_cells(self):
        self.one = self.cross(self.packed)

    def over_tok(self, waits):
        mine = self.total(self.one, waits)
        self.two = swap(mine.reshape(self.nt, self.share, 128), "tok")
        return mine

    def back_tok(self, waits):
        two, _ = lax.optimization_barrier((self.two, waits))
        mine = self.total([two[k] for k in range(self.nt)], [])
        mine = jnp.broadcast_to(mine[None], (self.nt,) + mine.shape)
        self.three = swap(mine, "tok")
        return mine

    def back_cells(self):
        self.four = self.cross([self.three.reshape(self.quarter, 128)] * self.nc)

    def results(self, block, pieces, sums, smalls, waits=(), extras=()):
        outs = [jax.ShapeDtypeStruct((D, width), F32) for _, width in pieces]
        outs += [jax.ShapeDtypeStruct((8, 128), F32) for _ in sums]
        outs += [jax.ShapeDtypeStruct((1, width), F32) for _, width in smalls]
        outs = call(
            unpack_body(self.nc, block, pieces, sums, smalls, len(extras)), self.info,
            self.four + list(extras), [whole(v) for v in self.four + list(extras)], outs, [whole(v) for v in outs], [((self.rows, 128), F32)],
            us=0.02, waits=waits,
        )
        return outs[: len(pieces)], outs[len(pieces) :]


def padded_rows(need, nc, nt):
    unit = nc * nt * 16
    return -(-need // unit) * unit


def shards(
    tokens, cotangent, gene_count, expressed, projection, first_gain, first_bias, query_weight,
    key_weight, value_weight, out_weight, out_bias, second_gain, second_bias, up_weight, up_bias,
    down_weight, down_bias,
):
    cells, _, slots = tokens.shape
    turns = cells // GROUP
    steps, lanes = GROUP // STEP, STEP * slots
    nt, nc = lax.axis_size("tok"), lax.axis_size("cells")
    position = lax.axis_index("tok")
    groups = [[g * GROUP + i for i in range(GROUP)] for g in range(nt // GROUP)]
    info = jnp.stack([lax.axis_index("cells"), position % GROUP]).astype(jnp.int32)

    slot_index = position * slots + lax.broadcasted_iota(jnp.int32, (cells, slots), 1)
    alive = ((slot_index < gene_count[:, None]) & (expressed > 0)).astype(BF)
    marks = jnp.pad(alive[:, None, :], ((0, 0), (0, DX - D - 1), (0, 0)))

    def turn_of(array, c):
        return array[c * GROUP : (c + 1) * GROUP]

    def to_cells(c):
        return swap(jnp.concatenate([turn_of(tokens, c), turn_of(marks, c)], axis=1), "tok", groups)

    x = [to_cells(0)]

    vectors = [first_gain, first_bias, second_gain, second_bias, out_bias, down_bias, up_bias]
    vec = jnp.stack([jnp.pad(v, (0, FF - v.shape[0])) for v in vectors + [jnp.zeros((FF,), F32)]])
    outs = [jax.ShapeDtypeStruct((FF, 8), F32)] + [
        jax.ShapeDtypeStruct(shape, BF)
        for shape in (
            (INNER, DX), (D, 2 * INNER), (2 * INNER, DX), (INNER, D), (FF, DX), (FF, D),
            (MAIN, HEAD_SIZE), (LEFT, INNER), (EXT, MAIN), (HEADS * EXT, LEFT),
        )
    ]
    wot = out_weight.T
    ins = [
        vec, projection.T, query_weight, key_weight, value_weight, wot, up_weight, down_weight,
    ]
    cols, wqt, wkv, wkvt, wo, upt, downt, pm, left_proj, tm, tl = call(
        prep_body, info, ins, [whole(v) for v in ins], outs, [whole(v) for v in outs], [], us=4,
    )

    tokens, marks, cols = lax.optimization_barrier((tokens, marks, cols))
    x += [to_cells(c) for c in range(1, turns)]
    x_spec = pl.BlockSpec((STEP, DX, slots), lambda j, info: (j, 0, 0))

    def step_spec(rows):
        return pl.BlockSpec((1, rows, lanes), lambda j, info: (j, 0, 0))

    k_out = jax.ShapeDtypeStruct((KROWS, MAIN), BF)
    k_acc = ((KROWS, MAIN), F32)
    key_scratch = [
        ((INNER, lanes), BF), ((HEADS * EXT, lanes), BF), ((HEADS * MAIN, lanes), BF),
        ((LEFT, lanes), BF), ((16, lanes), F32),
    ]
    kernels, dy = [], []
    for c in range(turns):
        ins = [x[c], cols, wkvt, pm, left_proj]
        part = call(
            first_body, info, ins, [x_spec] + [whole(v) for v in ins[1:]],
            k_out, whole(k_out), [k_acc] + key_scratch, grid=steps, us=12,
        )
        mine, part = lax.optimization_barrier((turn_of(cotangent, c), part))
        kernels.append(share_kernel(part, nt))
        dy.append(swap(mine, "tok", groups))

    token_out = jax.ShapeDtypeStruct((GROUP, D, slots), BF)
    token_spec = pl.BlockSpec((STEP, D, slots), lambda j, info: (j, 0, 0))
    wide_out = jax.ShapeDtypeStruct((steps, D, lanes), BF)
    common = [
        ((HEADS * EXT, lanes), BF), ((HEADS * MAIN, lanes), BF), ((LEFT, lanes), BF),
        ((16, lanes), F32), ((HEADS * EXT, MAIN), BF), ((HEADS * EXT, LEFT), BF),
        ((HEADS * EXT, lanes), F32),
    ]
    weights = [
        cols, wqt, query_weight, wot, wo, upt, up_weight, downt, down_weight,
        pm, left_proj, tm, tl,
    ]
    rows2 = padded_rows(GRAD2 + 2 * SMALL2, nc, nt)
    sums = [((GRAD2, 128), F32), ((SMALL2 * D, 128), F32)]
    mixed_grads, query_grads, kernel_grads = [], [], []
    results, sums2 = [], []
    for c in range(turns):
        start, last = c == 0, c == turns - 1
        fixed = kernels[c] + sums2 + weights
        if last:
            sum_outs = [jax.ShapeDtypeStruct((rows2 // nc, 128), BF)] * nc
            sum_scratch = [((rows2, 128), F32)] + sums
        else:
            sum_outs = [jax.ShapeDtypeStruct(shape, kind) for shape, kind in sums]
            sum_scratch = []
        out, gmix, gnq, kg, *sums2 = call(
            second_body(len(kernels[c]), start, nc if last else 0, HEADS if start else UNROLL), info, [x[c], dy[c]] + fixed,
            [x_spec, token_spec] + [whole(v) for v in fixed],
            [token_out, wide_out, wide_out, k_out] + sum_outs,
            [token_spec, step_spec(D), step_spec(D)] + [whole(v) for v in [k_out] + sum_outs],
            sum_scratch + [((KROWS, MAIN), BF), k_acc, ((INNER, lanes), BF), ((INNER, lanes), BF)]
            + common
            + [
                ((INNER, lanes), BF), ((16, lanes), F32), ((FF, lanes), BF), ((FF, lanes), BF),
                ((DX, lanes), BF), ((DX, lanes), BF),
            ],
            grid=steps, us=40,
        )
        results.append(swap(out, "tok", groups))
        mixed_grads.append(gmix)
        query_grads.append(gnq)
        kernel_grads.append(share_kernel(kg, nt))
    reduce2 = Reduction(sums2, info, rows2, nc, nt)
    reduce2.over_cells()

    rows3 = padded_rows(2 * Q_BLOCKS * D + 2 * SMALL3, nc, nt)
    weights = [cols, wkvt, wkv, pm, left_proj, tm, tl]
    normed_grads, sums3 = [], []
    waits = [sums2[0], results[0]]
    for c in range(turns):
        start, last = c == 0, c == turns - 1
        fixed = kernel_grads[c] + sums3 + weights
        if last:
            sum_outs = [jax.ShapeDtypeStruct((rows3 // nc, 128), BF)] * nc
            sum_scratch = [((rows3, 128), F32), ((GRAD3, 128), F32), ((SMALL3 * D, 128), F32)]
        else:
            sum_outs = [jax.ShapeDtypeStruct((GRAD3, 128), F32)]
            sum_scratch = []
        got, *sums3 = call(
            third_body(len(kernel_grads[c]), start, nc if last else 0), info,
            [x[c], query_grads[c]] + fixed, [x_spec, step_spec(D)] + [whole(v) for v in fixed],
            [wide_out] + sum_outs, [step_spec(D)] + [whole(v) for v in sum_outs],
            sum_scratch
            + [((KROWS, MAIN), BF), ((INNER, lanes), BF), ((2 * INNER, lanes), BF)] + common
            + [((DX, lanes), BF)],
            grid=steps, us=22, waits=waits,
        )
        normed_grads.append(got)
        if start:
            waits = [reduce2.over_tok([got, results[-1]] + kernel_grads[-1][1:])]
    reduce3 = Reduction(sums3, info, rows3, nc, nt)
    reduce3.over_cells()
    waits = [sums3[0], results[-1], reduce2.back_tok([sums3[0]])]
    one_out = jax.ShapeDtypeStruct((1, D, slots), BF)
    grads = []
    for c in range(turns):
        ins = [x[c], dy[c], mixed_grads[c], normed_grads[c], cols]

        def pair(rows, blocks=STEP, columns=slots):
            return pl.BlockSpec(
                (blocks, rows, columns), lambda j, info: (jnp.bitwise_xor(info[1] // STEP, j), 0, 0)
            )

        specs = [pair(DX), pair(D), pair(D, 1, lanes), pair(D, 1, lanes), whole(cols)]
        out = call(
            last_body, info, ins, specs, [one_out] * GROUP,
            [whole(one_out)] * GROUP, [], grid=steps, us=6, waits=waits,
        )
        if c == turns - 1:
            reduce2.back_cells()
            mine = reduce3.back_tok([out[0]] + reduce2.four[1:3] + grads[1:])
            out, _ = lax.optimization_barrier((out, mine))
        grads += [out[0]] + [
            lax.ppermute(out[s], "tok", [(i, i - i % GROUP + (i % GROUP ^ s)) for i in range(nt)])
            for s in range(1, GROUP)
        ]
        if c == 0:
            waits = [reduce3.over_tok([out[0]]), reduce2.three]
    (dwq, dwot, dup, ddown), (upb, gain2, bias2, outb, downb, gain1q, bias1q) = reduce2.results(
        DX, [(WQ_AT, INNER), (WO_AT, INNER), (UP_AT, FF), (DOWN_AT, FF)], [(UP_AT, FF)],
        [(GRAD2 + 2 * k, D) for k in range(SMALL2)], waits=[mine],
    )
    reduce3.three, _ = lax.optimization_barrier((reduce3.three, gain1q))
    reduce3.back_cells()

    result = jnp.concatenate(results, axis=0)
    grad_in = call(
        place_body, info, grads, [whole(v) for v in grads], jax.ShapeDtypeStruct((cells, D, slots), BF),
        pl.BlockSpec((cells, D, slots), lambda i, info: (0, 0, 0)), [], us=0.02,
        waits=[reduce3.three],
    )
    (dwk, dwv), (gain1, bias1) = reduce3.results(
        D, [(0, INNER), (Q_BLOCKS, INNER)], [], [(2 * Q_BLOCKS * D + 2 * k, D) for k in range(SMALL3)],
        extras=[gain1q, bias1q], waits=[grad_in],
    )
    return (
        result, grad_in, gain1[0], bias1[0], dwq, dwk, dwv, dwot.T, outb[0],
        gain2[0], bias2[0], dup, upb.reshape(8 * 128)[:FF], ddown, downb[0],
    )


def solution(mesh):
    rows = P("cells", None, "tok")
    placed = (rows, rows, P("cells"), P("cells", "tok")) + (P(),) * 14
    return jax.shard_map(
        shards,
        mesh=mesh,
        in_specs=placed,
        out_specs=(rows, rows) + (P(),) * 13,
        check_vma=False,
    )
```
